128 devices in a mesh: seq: 8 (over z, core), head: 16 (over x, y).
Axes of the slice: x: 4, y: 4, z: 4, core: 2. Of those that a mesh axis runs over, the one named last changes fastest.
Arguments:
- tokens: bfloat16 [16384, 2048], P(('seq', 'head')), may hold values from -6 to 6
- doc_starts: int32 [8, 3], P('seq'), may hold values from 0 to 127, as said below
- norm_gain: float32 [2048], replicated, may hold values from 0.5 to 1.5
- w_in: bfloat16 [2048, 4, 2048], P(None, None, 'head'), may hold values from -0.125 to 0.125
- w_rate: bfloat16 [2048, 32], P(None, 'head'), may hold values from -0.125 to 0.125
- rate_bias: float32 [32], P('head'), may hold values from -2 to 2
- ttt_w: float32 [32, 64, 64], P('head'), may hold values from -0.75 to 0.75
- ttt_b: float32 [32, 64], P('head'), may hold values from -2 to 2
- ttt_gain: float32 [32, 64], P('head'), may hold values from 0.25 to 1.75
- ttt_shift: float32 [32, 64], P('head'), may hold values from -2 to 2
- post_gain: float32 [2048], P('head'), may hold values from 0.25 to 1.75
- post_bias: float32 [2048], P('head'), may hold values from -2 to 2
- w_out: bfloat16 [2048, 2048], P('head'), may hold values from -0.25 to 0.25
- ffn_gain: float32 [2048], replicated, may hold values from 0.5 to 1.5
- w_gate_up: bfloat16 [2048, 2, 5504], P(None, None, 'head'), may hold values from -0.125 to 0.125
- w_down: bfloat16 [5504, 2048], P('head'), may hold values from -0.15625 to 0.15625
- cotangent: bfloat16 [16384, 2048], P(('seq', 'head')), may hold values from -6 to 6
Outputs:
- output: bfloat16 [16384, 2048], P(('seq', 'head'))
- grad_tokens: float32 [16384, 2048], P(('seq', 'head'))
- grad_norm_gain: float32 [2048], replicated
- grad_w_in: float32 [2048, 4, 2048], P(None, None, 'head')
- grad_w_rate: float32 [2048, 32], P(None, 'head')
- grad_rate_bias: float32 [32], P('head')
- grad_ttt_w: float32 [32, 64, 64], P('head')
- grad_ttt_b: float32 [32, 64], P('head')
- grad_ttt_gain: float32 [32, 64], P('head')
- grad_ttt_shift: float32 [32, 64], P('head')
- grad_post_gain: float32 [2048], P('head')
- grad_post_bias: float32 [2048], P('head')
- grad_w_out: float32 [2048, 2048], P('head')
- grad_ffn_gain: float32 [2048], replicated
- grad_w_gate_up: float32 [2048, 2, 5504], P(None, None, 'head')
- grad_w_down: float32 [5504, 2048], P('head')
The draws below stay inside these ranges and needn't reach their ends.
Inputs may be any that keep to these rules, and one draw needn't show every extreme that they name: `doc_starts`: in each row the three starts increase; the first is 0, the second lies in 1 to 7 and the third in 121 to 127; in some row the third is 127.
All inputs are finite; a program needn't handle non-finite values.
Results may differ from the reference program's by a relative error of at most 0.025.
Values may be sent and summed in bfloat16 or wider, within the bound.
A program may use at most 192 MiB of HBM per device.

```python
from functools import partial
import jax
import jax.numpy as jnp
from jax import lax

D = 2048
NH = 32
HD = 64
FF = 5504
MB = 16
TOK_DEV = 128
L = 2048
BLOCKS = 128
ROWS = 8
TOKENS = 16384


def draw_doc_starts(key, part):
    key = jax.random.fold_in(key, 11)
    second_key, third_key, pick_key = jax.random.split(key, 3)
    per_device = TOK_DEV // MB
    second_start = jax.random.randint(second_key, (ROWS, 1), 1, per_device)
    third_start = jax.random.randint(third_key, (ROWS, 1), BLOCKS - per_device + 1, BLOCKS)
    chosen_row = jax.random.randint(pick_key, (), 0, ROWS)
    row_marks = jnp.arange(ROWS, dtype=jnp.int32)[:, None]
    third_start = jnp.where(row_marks == chosen_row, BLOCKS - 1, third_start)
    first_start = jnp.zeros((ROWS, 1), jnp.int32)
    return jnp.concatenate([first_start, second_start, third_start], axis=1).astype(jnp.int32)


def level_of(key, extent, cuts, smallest, largest):
    gain = 1.0
    for axis_at, shards_of in cuts:
        steps = jax.random.uniform(jax.random.fold_in(jax.random.fold_in(key, 6), axis_at), (shards_of,), jnp.float32, smallest / len(cuts), largest / len(cuts))
        gain = gain * jnp.repeat(jnp.exp(steps), extent[axis_at] // shards_of).reshape((-1,) + (1,) * (len(extent) - 1 - axis_at))
    return gain


def normal_values(own_key, shape, deviation, most, pieces=(), kind=jnp.bfloat16):
    drawn = deviation * jax.random.normal(own_key, shape, jnp.float32)
    if pieces:
        drawn = drawn * level_of(own_key, shape, pieces, -0.22, 0.18)
    return jnp.clip(drawn, -most, most).astype(kind)


def setup_inputs(seed: int = 0) -> dict:
    splits = jax.random.split(jax.random.key(seed), 18)
    tokens = normal_values(splits[0], (TOKENS, D), 1.0, 6.0, ((0, 128),))
    doc_starts = draw_doc_starts(jax.random.fold_in(splits[17], 71), 0)
    norm_gain = jnp.clip(1.0 + 0.1 * jax.random.normal(splits[2], (D,), jnp.float32), 0.5, 1.5)
    w_in = normal_values(splits[3], (D, 4, D), D ** -0.5, 0.125, ((2, 16),))
    w_rate = normal_values(splits[4], (D, NH), D ** -0.5, 0.125, ((1, 16),))
    rate_bias = jnp.clip(jax.random.uniform(splits[5], (NH,), jnp.float32, -2.0, 2.0) * level_of(splits[5], (NH,), ((0, 16),), -0.4, 0.0), -2.0, 2.0)
    ttt_w = normal_values(splits[6], (NH, HD, HD), HD ** -0.5, 0.75, ((0, 16),), jnp.float32)
    ttt_b = normal_values(splits[7], (NH, HD), 0.3, 2.0, ((0, 16),), jnp.float32)
    ttt_gain = jnp.clip(1.0 + 0.15 * jax.random.normal(splits[8], (NH, HD), jnp.float32), 0.25, 1.75)
    ttt_shift = normal_values(splits[9], (NH, HD), 0.3, 2.0, ((0, 16),), jnp.float32)
    post_gain = jnp.clip(1.0 + 0.15 * jax.random.normal(splits[10], (D,), jnp.float32), 0.25, 1.75)
    post_bias = normal_values(splits[11], (D,), 0.3, 2.0, ((0, 16),), jnp.float32)
    w_out = normal_values(splits[12], (D, D), (D // 4) ** -0.5, 0.25, ((0, 16),))
    ffn_gain = jnp.clip(1.0 + 0.1 * jax.random.normal(splits[13], (D,), jnp.float32), 0.5, 1.5)
    w_gate_up = normal_values(splits[14], (D, 2, FF), D ** -0.5, 0.125, ((2, 16),))
    w_down = normal_values(splits[15], (FF, D), (FF // 4) ** -0.5, 0.15625, ((0, 16),))
    cotangent = normal_values(splits[16], (TOKENS, D), 1.0, 6.0, ((0, 128),))
    return {"tokens": tokens, "doc_starts": doc_starts, "norm_gain": norm_gain, "w_in": w_in, "w_rate": w_rate, "rate_bias": rate_bias, "ttt_w": ttt_w, "ttt_b": ttt_b, "ttt_gain": ttt_gain, "ttt_shift": ttt_shift, "post_gain": post_gain, "post_bias": post_bias, "w_out": w_out, "ffn_gain": ffn_gain, "w_gate_up": w_gate_up, "w_down": w_down, "cotangent": cotangent}


EPS = 1e-06
HIGH_ACCURACY = lax.Precision.HIGHEST

@jax.custom_vjp
def low(v):
    return lax.optimization_barrier(v.astype(jnp.bfloat16)).astype(jnp.float32)

@jax.custom_vjp
def low_back(v):
    return v

def low_keep(v):
    return (low(v), None)

def low_pass(kept, grad):
    return (grad,)

def back_keep(v):
    return (v, None)

def back_low(kept, grad):
    return (low(grad),)
low.defvjp(low_keep, low_pass)
low_back.defvjp(back_keep, back_low)

def layer_norm(values, gain_in, offset):
    center = values - lax.optimization_barrier(jnp.mean(values, axis=-1, keepdims=True))
    inverse = lax.rsqrt(lax.optimization_barrier(jnp.mean(center * center, axis=-1, keepdims=True)) + EPS)
    normal = center * inverse
    return (normal * gain_in + offset, normal, inverse)

def inner_run(queries, key_rows, value_rows, rate_heads, flag_heads, start_w, start_b, gain_in, shift_in):
    block_len = queries.shape[2]
    places = jnp.arange(block_len, dtype=jnp.int32)
    lower_mask = (places[:, None] >= places[None, :]).astype(jnp.float32)
    step_scale = lower_mask / (places[:, None].astype(jnp.float32) + 1.0)
    gain_rows = gain_in[:, None, :]
    shift_rows = shift_in[:, None, :]

    def advance(state_now, inputs):
        inner_weight, inner_bias = state_now
        query_input, key_input, value_in, rate_in, flag_in = inputs
        inner_weight = inner_weight + flag_in[:, None, None] * (start_w - inner_weight)
        inner_bias = inner_bias + flag_in[:, None] * (start_b - inner_bias)
        hidden_state = jnp.einsum('wlt,wtf->wlf', key_input, inner_weight, precision=HIGH_ACCURACY) + inner_bias[:, None, :]
        fitted, normal, inverse = layer_norm(hidden_state, gain_rows, shift_rows)
        scaled = (fitted - (value_in - key_input)) * gain_rows
        hidden_gradient = inverse * (scaled - lax.optimization_barrier(jnp.mean(scaled, axis=-1, keepdims=True)) - normal * lax.optimization_barrier(jnp.mean(scaled * normal, axis=-1, keepdims=True)))
        step_learning_rate = step_scale[None, :, :] * rate_in[:, None, :]
        score_matrix = jnp.einsum('hid,hjd->hij', query_input, key_input, precision=HIGH_ACCURACY)
        bias_per_row = inner_bias[:, None, :] - jnp.einsum('mfc,mck->mfk', step_learning_rate, hidden_gradient, precision=HIGH_ACCURACY)
        block_output = jnp.einsum('wlt,wtf->wlf', query_input, inner_weight, precision=HIGH_ACCURACY) - jnp.einsum('mfc,mck->mfk', step_learning_rate * score_matrix, hidden_gradient, precision=HIGH_ACCURACY) + bias_per_row
        final_rate = rate_in / block_len
        inner_weight = inner_weight - jnp.einsum('hjd,hje->hde', final_rate[:, :, None] * key_input, hidden_gradient, precision=HIGH_ACCURACY)
        inner_bias = inner_bias - lax.optimization_barrier(jnp.sum(final_rate[:, :, None] * hidden_gradient, axis=1))
        output_rows, _, _ = layer_norm(block_output, gain_rows, shift_rows)
        return ((inner_weight, inner_bias), query_input + output_rows)
    inputs = (queries.transpose(1, 0, 2, 3), key_rows.transpose(1, 0, 2, 3), value_rows.transpose(1, 0, 2, 3), rate_heads.transpose(1, 0, 2), flag_heads.transpose(1, 0))
    _, stacked = lax.scan(jax.checkpoint(advance), (start_w, start_b), inputs)
    return stacked.transpose(1, 0, 2, 3)

def forward(flags, resid, norm_gain, w_in, w_rate, rate_bias, ttt_w, ttt_b, ttt_gain, ttt_shift, post_gain, post_bias, w_out, ffn_gain, w_gate_up, w_down):
    total = resid.shape[0]
    row_count = total // L
    norm_one = low(resid * lax.rsqrt(lax.optimization_barrier(jnp.mean(resid * resid, axis=-1, keepdims=True)) + EPS) * norm_gain)
    projected = low_back(low(jnp.dot(norm_one, w_in.reshape(D, 4 * D), precision=HIGH_ACCURACY)))
    logits = low_back(jnp.dot(norm_one, w_rate, precision=HIGH_ACCURACY) + rate_bias)
    rates = jax.nn.sigmoid(logits) / HD
    split_proj = projected.reshape(row_count, BLOCKS, MB, 4, NH, HD)

    def heads_of(index):
        return split_proj[:, :, :, index].transpose(0, 3, 1, 2, 4).reshape(row_count * NH, BLOCKS, MB, HD)
    rate_heads = rates.reshape(row_count, BLOCKS, MB, NH).transpose(0, 3, 1, 2).reshape(row_count * NH, BLOCKS, MB)
    flag_heads = jnp.broadcast_to(flags[:, None, :], (row_count, NH, BLOCKS)).reshape(row_count * NH, BLOCKS)
    start_w = jnp.broadcast_to(ttt_w[None], (row_count, NH, HD, HD)).reshape(row_count * NH, HD, HD)
    start_b = jnp.broadcast_to(ttt_b[None], (row_count, NH, HD)).reshape(row_count * NH, HD)
    gain_heads = jnp.broadcast_to(ttt_gain[None], (row_count, NH, HD)).reshape(row_count * NH, HD)
    shift_heads = jnp.broadcast_to(ttt_shift[None], (row_count, NH, HD)).reshape(row_count * NH, HD)
    inner = inner_run(heads_of(0), heads_of(1), heads_of(2), rate_heads, flag_heads, start_w, start_b, gain_heads, shift_heads)
    inner = inner.reshape(row_count, NH, BLOCKS, MB, HD).transpose(0, 2, 3, 1, 4).reshape(total, D)
    gate_in = projected[:, 3 * D:]
    post, _, _ = layer_norm(inner, post_gain, post_bias)
    mixed_in = low(post * jax.nn.gelu(gate_in, approximate=True))
    hidden_res = resid + low_back(jnp.dot(mixed_in, w_out, precision=HIGH_ACCURACY))
    norm_two = low(hidden_res * lax.rsqrt(lax.optimization_barrier(jnp.mean(hidden_res * hidden_res, axis=-1, keepdims=True)) + EPS) * ffn_gain)
    gate_up = low_back(low(jnp.dot(norm_two, w_gate_up.reshape(D, 2 * FF), precision=HIGH_ACCURACY)))
    hidden_state = low(jax.nn.silu(gate_up[:, :FF]) * gate_up[:, FF:])
    return hidden_res + low_back(jnp.dot(hidden_state, w_down, precision=HIGH_ACCURACY))

def reference(tokens, doc_starts, norm_gain, w_in, w_rate, rate_bias, ttt_w, ttt_b, ttt_gain, ttt_shift, post_gain, post_bias, w_out, ffn_gain, w_gate_up, w_down, cotangent):
    block_marks = jnp.arange(BLOCKS, dtype=jnp.int32)
    flags = jnp.any(doc_starts[:, :, None] == block_marks[None, None, :], axis=1).astype(jnp.float32)
    params = [item.astype(jnp.float32) for item in (tokens, norm_gain, w_in, w_rate, rate_bias, ttt_w, ttt_b, ttt_gain, ttt_shift, post_gain, post_bias, w_out, ffn_gain, w_gate_up, w_down)]
    block_output, pullback = jax.vjp(partial(forward, flags), *params)
    grads = pullback(cotangent.astype(jnp.float32))
    return (block_output.astype(jnp.bfloat16), grads[0], grads[1], grads[2], grads[3], grads[4], grads[5], grads[6], grads[7], grads[8], grads[9], grads[10], grads[11], grads[12], grads[13], grads[14])
```

```python
from functools import partial

import jax
import jax.numpy as jnp
from jax import lax
from jax.experimental import pallas as pl
from jax.experimental.pallas import tpu as pltpu
from jax.sharding import PartitionSpec as P

MB = 16
EPS = 1e-06
HD = 64
STEPS = 4
CHUNK = STEPS * MB
LANES = 2 * CHUNK
BF16 = jnp.bfloat16
F32 = jnp.float32


def dot_nn(a, b):
    return lax.dot_general(a, b, (((1,), (0,)), ((), ())), preferred_element_type=F32)


def dot_nt(a, b):
    return lax.dot_general(a, b, (((1,), (1,)), ((), ())), preferred_element_type=F32)


def dot_tn(a, b):
    return lax.dot_general(a, b, (((0,), (0,)), ((), ())), preferred_element_type=F32)


def sum_rows(x):
    return jnp.sum(x, axis=0, keepdims=True)


def square_iota(dim):
    return lax.broadcasted_iota(jnp.int32, (LANES, LANES), dim)


def step_of(index):
    return (index >> 4) & (STEPS - 1)


class Places:
    def __init__(self, starts_ref):
        self.second = starts_ref[0, 1]
        self.third = starts_ref[0, 2]

    def document(self, step):
        return (step >= self.second).astype(jnp.int32) + (step >= self.third).astype(jnp.int32)

    def lane_documents(self, chunk):
        return self.document(chunk * STEPS + step_of(lax.broadcasted_iota(jnp.int32, (1, LANES), 1)))

    def row_documents(self, chunk):
        return self.document(chunk * STEPS + step_of(lax.broadcasted_iota(jnp.int32, (LANES, 1), 0)))

    def entry(self, chunk):
        return self.document(chunk * STEPS - 1)

    def last(self, chunk):
        return self.document(chunk * STEPS + STEPS - 1)

    def keeps(self, chunk):
        return (self.entry(chunk) == self.last(chunk)).astype(F32)


def split_heads(rows):
    first = lax.broadcasted_iota(jnp.int32, rows.shape, 1) < HD
    zero = jnp.zeros_like(rows)
    return jnp.concatenate([jnp.where(first, rows, zero), jnp.where(first, zero, rows)], axis=0)


def join_heads(square):
    first = lax.broadcasted_iota(jnp.int32, (CHUNK, LANES), 1) < HD
    return jnp.where(first, square[:CHUNK], square[CHUNK:])


def to_columns(rows):
    turned = split_heads(rows).T
    return turned[:HD] + turned[HD:]


def to_rows(columns):
    return join_heads(split_heads(columns).T)


def selector():
    row = lax.broadcasted_iota(jnp.int32, (HD, LANES), 0)
    col = lax.broadcasted_iota(jnp.int32, (HD, LANES), 1)
    return (row == (col & (HD - 1))).astype(F32).astype(BF16)


RING = 4


def slot(chunk):
    return lax.rem(chunk, RING)


def wrap(chunk, chunks):
    return lax.rem(chunk + chunks, chunks)


def chunk_rows(chunk):
    return pl.ds(pl.multiple_of(chunk * CHUNK, CHUNK), CHUNK)


def same_head():
    return (square_iota(0) >> 6) == (square_iota(1) >> 6)


def masked(values, keep):
    return jnp.where(keep, values, jnp.zeros_like(values))


def inner_masks(head_ref, earlier_ref, output_ref):
    row, col = square_iota(0), square_iota(1)
    same = same_head()
    step_row, step_col = step_of(row), step_of(col)
    earlier = jnp.where(same & (step_row < step_col), 1.0, 0.0)
    place = (col & (MB - 1)).astype(F32)
    within = jnp.where(
        same & (step_row == step_col) & ((row & (MB - 1)) <= (col & (MB - 1))),
        MB / (place + 1.0),
        0.0,
    )
    head_ref[...] = jnp.where(same, 1.0, 0.0)
    earlier_ref[...] = earlier
    output_ref[...] = earlier + within


def centred_columns(values):
    return values - sum_rows(values) / HD


def spread(pairs):
    return jnp.concatenate(
        [jnp.broadcast_to(pairs[h : h + 1], (HD, HD)) for h in range(2)], axis=0
    ).T


def forward_kernel(
    starts_ref,
    proj_ref,
    rate_ref,
    ttt_w_ref,
    ttt_b_ref,
    ttt_gain_ref,
    ttt_shift_ref,
    cot_ref,
    inner_ref,
    z_ref,
    g_ref,
    out_ref,
    target_ref,
    state_ref,
    mi_ref,
    mx_ref,
    mo_ref,
    w_ref,
    gain_ref,
    base_ref,
    offset_ref,
    cot_rows_ref,
    head_ref,
    earlier_ref,
    output_ref,
    c_ref,
    shift_ref,
    *gather_sems,
):
    chunks = rate_ref.shape[0]
    gather = Gather(cot_ref, cot_rows_ref, *gather_sems)
    gather.start()
    places = Places(starts_ref)
    inner_masks(head_ref, earlier_ref, output_ref)
    w_ref[...] = centred_columns(jnp.concatenate([ttt_w_ref[0], ttt_w_ref[1]], axis=0).T)
    c_ref[...] = centred_columns(spread(ttt_b_ref[...]))
    gain_ref[...] = spread(ttt_gain_ref[...])
    shift_ref[...] = spread(ttt_shift_ref[...])

    def columns(chunk, index):
        return proj_ref[chunk_rows(chunk), index * LANES : (index + 1) * LANES]

    def prepare(chunk):
        source = wrap(chunk, chunks)
        before = wrap(source - 1, chunks)
        keys = split_heads(columns(source, 1))
        values = split_heads(columns(source, 2))
        docs_row, docs_lane = places.row_documents(source), places.lane_documents(source)
        gram = dot_nt(keys, keys) + 1.0
        mi_ref[chunk] = masked(gram * earlier_ref[...], docs_row == docs_lane).astype(BF16)
        cross = dot_nt(split_heads(columns(before, 1)), keys) + 1.0
        mx_ref[chunk] = masked(
            cross * head_ref[...], places.row_documents(before) == docs_lane
        ).astype(BF16)
        pick = selector()
        target = dot_nt(pick, keys) - dot_nt(pick, values) + shift_ref[...]
        target_ref[chunk] = target
        offset_ref[slot(chunk)] = jnp.broadcast_to(
            sum_rows(target * gain_ref[...]) / HD, offset_ref.shape[1:]
        )

    def read_state(rows, source, weight, bias, entry):
        docs_row = places.row_documents(source)
        live_lane = places.lane_documents(source) == entry
        both = jnp.concatenate(
            [masked(rows, docs_row == entry), masked(rows, docs_row != entry)], axis=1
        )
        weights = jnp.concatenate([weight, w_ref[...]], axis=1).astype(BF16)
        return dot_nt(weights, both) + jnp.where(live_lane, bias, c_ref[...])

    def base(chunk, weight, bias, entry):
        source = wrap(chunk, chunks)
        base_ref[slot(chunk)] = read_state(split_heads(columns(source, 1)), source, weight, bias, entry)

    def chain(chunk, rated_before):
        gain = gain_ref[...]
        gain2 = gain * gain
        tied = target_ref[chunk] * gain
        tied_mean = offset_ref[slot(chunk)][0:1]
        rate = rate_ref[chunk]
        matrix = mi_ref[chunk]

        def gradient(z):
            zg = z * gain2
            s1, s2, s3, s4 = sum_rows(z * z), sum_rows(zg), sum_rows(z * zg), sum_rows(z * tied)
            rs = lax.rsqrt(s1 / HD + EPS)
            mean_g = rs * s2 / HD + tied_mean
            mean_gx = rs * (rs * s3 + s4) / HD
            return rs * (z * (rs * (gain2 - mean_gx)) + (tied - mean_g))

        first = base_ref[slot(chunk)] - dot_nn(rated_before, mx_ref[chunk])
        z = first
        g = gradient(z)
        for _ in range(STEPS - 1):
            z = first - dot_nn((g * rate).astype(BF16), matrix)
            g = gradient(z)
        z_ref[chunk] = z
        g_ref[chunk] = g
        return (g * rate).astype(BF16)

    def advance(chunk, weight, bias, rated):
        keys = split_heads(columns(chunk, 1))
        last = places.last(chunk)
        kept = places.row_documents(chunk) == last
        both = jnp.concatenate(
            [masked(keys, kept), masked(head_ref[...].astype(BF16), kept)], axis=1
        )
        step = dot_nn(rated, both)
        keep = places.keeps(chunk)
        start_w, start_c = w_ref[...], c_ref[...]
        return (
            start_w + keep * (weight - start_w) - step[:, :LANES],
            start_c + keep * (bias - start_c) - step[:, LANES:],
        )

    def finish(chunk, weight, bias, rated):
        keys = split_heads(columns(chunk, 1))
        query_rows = columns(chunk, 0)
        queries = split_heads(query_rows)
        same_doc = places.row_documents(chunk) == places.lane_documents(chunk)
        matrix = masked((dot_nt(keys, queries) + 1.0) * output_ref[...], same_doc).astype(BF16)
        mo_ref[chunk] = matrix
        out = read_state(queries, chunk, weight, bias, places.entry(chunk)) - dot_nn(rated, matrix)
        out_ref[chunk] = out
        rs = lax.rsqrt(sum_rows(out * out) / HD + EPS)
        fitted = out * rs * gain_ref[...] + shift_ref[...]
        inner_ref[chunk_rows(chunk), :] = (to_rows(fitted) + query_rows.astype(F32)).astype(BF16)

    prepare(0)
    base(0, w_ref[...], c_ref[...], places.entry(0))

    def body(chunk, carry):
        weight_before, bias_before, rated_before = carry
        for step, when in enumerate(FORWARD_STEPS):
            pl.when(chunk == when)(gather.steps[step])
        before = wrap(chunk - 1, chunks)
        weight, bias = advance(before, weight_before, bias_before, rated_before)
        state_ref[chunk] = weight
        rated = chain(chunk, rated_before)
        base(chunk + 1, weight, bias, places.entry(chunk))
        prepare(chunk + 1)
        finish(before, weight_before, bias_before, rated_before)
        return weight, bias, rated

    carry = (w_ref[...], c_ref[...], jnp.zeros((HD, LANES), BF16))
    weight, bias, rated = lax.fori_loop(0, chunks, body, carry)
    finish(chunks - 1, weight, bias, rated)
    gather.end()


FORWARD_STEPS = (5, 7, 12, 16, 20, 24, 30)
BACKWARD_STEPS = (5, 7, 10, 13, 17, 20, 24)


def backward_kernel(
    starts_ref,
    proj_ref,
    rate_ref,
    dinner_ref,
    dgate_ref,
    mix_ref,
    z_ref,
    g_ref,
    out_ref,
    target_ref,
    state_ref,
    mi_ref,
    mx_ref,
    mo_ref,
    w_ref,
    gain_ref,
    dproj_ref,
    dbias_ref,
    dw_ref,
    dc_ref,
    dgain_ref,
    dshift_ref,
    dout_ref,
    free_ref,
    base_ref,
    diag_ref,
    norm_ref,
    both_ref,
    wide_ref,
    coef_ref,
    y_ref,
    dz_ref,
    lam_ref,
    mix_rows_ref,
    head_ref,
    earlier_ref,
    output_ref,
    *gather_sems,
):
    chunks = rate_ref.shape[0]
    gather = Gather(mix_ref, mix_rows_ref, *gather_sems)
    gather.start()
    places = Places(starts_ref)
    inner_masks(head_ref, earlier_ref, output_ref)
    dbias_ref[...] = jnp.zeros_like(dbias_ref)
    dw_ref[...] = jnp.zeros_like(dw_ref)
    dc_ref[...] = jnp.zeros_like(dc_ref)
    dgain_ref[...] = jnp.zeros_like(dgain_ref)
    dshift_ref[...] = jnp.zeros_like(dshift_ref)

    def columns(chunk, index):
        return proj_ref[chunk_rows(chunk), index * LANES : (index + 1) * LANES]

    def prepare(chunk):
        gain = gain_ref[...]
        gain2 = gain * gain
        given = to_columns(dinner_ref[chunk_rows(chunk), :].astype(F32))
        out = out_ref[chunk]
        rs_out = lax.rsqrt(sum_rows(out * out) / HD + EPS)
        normal = out * rs_out
        scaled = given * gain
        dout = rs_out * (
            scaled - sum_rows(scaled) / HD - normal * (sum_rows(scaled * normal) / HD)
        )
        dgain_ref[...] += given * normal
        dshift_ref[...] += given
        rounded = dout.astype(BF16)
        dout_ref[slot(chunk)] = rounded
        free_ref[slot(chunk)] = dot_nt(rounded, mo_ref[chunk])
        z = z_ref[chunk]
        rs = lax.rsqrt(sum_rows(z * z) / HD + EPS)
        xh = z * rs
        xg = xh * gain2
        g = xg + target_ref[chunk] * gain
        mean_g = sum_rows(g) / HD
        mean_gx = sum_rows(g * xh) / HD
        mean_xg = sum_rows(xg) / HD
        diag_ref[slot(chunk)] = rs * (gain2 - mean_gx)
        norm_ref[slot(chunk)] = xh
        both_ref[slot(chunk)] = xg + g - mean_g - xh * mean_gx
        wide_ref[slot(chunk)] = xg + g
        coef_ref[slot(chunk)] = jnp.concatenate(
            [
                rs * rate_ref[chunk],
                rs,
                sum_rows(gain2) / HD + mean_gx,
                mean_xg + mean_g,
                mean_xg,
                sum_rows(xg * xh) / HD + 2.0 * mean_gx,
                jnp.zeros((2, LANES), F32),
            ],
            axis=0,
        )

    def chain(chunk, dz_after, cross):
        gain = gain_ref[...]
        gain2 = gain * gain
        diag, xh, both, wide = diag_ref[slot(chunk)], norm_ref[slot(chunk)], both_ref[slot(chunk)], wide_ref[slot(chunk)]
        coef = coef_ref[slot(chunk)]
        matrix = mi_ref[chunk]

        def pull(y):
            du = y * coef[0:1]
            a1 = sum_rows(du) / HD
            a2 = sum_rows(du * xh) / HD
            a3 = sum_rows(du * gain2) / HD - a1 * coef[2:3] - a2 * coef[3:4]
            a4 = sum_rows(du * both) / HD - a1 * coef[4:5] - a2 * coef[5:6]
            return diag * du - coef[1:2] * (gain2 * a1 + wide * a2 + a3 + xh * a4)

        first = -(base_ref[slot(chunk)] + dot_nt(dz_after, cross))
        y = first
        dz = pull(y)
        for _ in range(STEPS - 1):
            y = first - dot_nt(dz.astype(BF16), matrix)
            dz = pull(y)
        y_ref[slot(chunk)] = y
        rounded = dz.astype(BF16)
        dz_ref[slot(chunk)] = rounded
        return rounded

    def into_state(chunk, rows, values):
        docs_row, entry = places.row_documents(chunk), places.entry(chunk)
        live, dead = docs_row == entry, docs_row != entry
        heads = head_ref[...].astype(BF16)
        given = dot_nn(
            values,
            jnp.concatenate(
                [
                    masked(rows, live),
                    masked(heads, live),
                    masked(rows, dead),
                    masked(heads, dead),
                ],
                axis=1,
            ),
        )
        dw_ref[...] += given[:, 2 * LANES : 3 * LANES]
        dc_ref[...] += given[:, 3 * LANES :]
        return given[:, :LANES], given[:, LANES : 2 * LANES]

    def reach_back(source, lam_w, lam_c):
        kept_row = places.row_documents(source) == places.last(source)
        kept_lane = places.lane_documents(source) == places.last(source)
        keys = masked(split_heads(columns(source, 1)), kept_row)
        return dot_nt(lam_w.astype(BF16), keys) + jnp.where(kept_lane, lam_c, 0.0)

    def finish(chunk):
        gain = gain_ref[...]
        query_rows = split_heads(columns(chunk, 0))
        key_rows = split_heads(columns(chunk, 1))
        entry = places.entry(chunk)
        docs_row, docs_lane = places.row_documents(chunk), places.lane_documents(chunk)
        live, dead = docs_lane == entry, docs_lane != entry
        kept = docs_lane == places.last(chunk)
        same_doc = docs_row == docs_lane
        y = y_ref[slot(chunk)]
        g = g_ref[chunk]
        coef = coef_ref[slot(chunk)]
        dz = dz_ref[slot(chunk)]
        dout = dout_ref[slot(chunk)]
        xh = norm_ref[slot(chunk)]
        rate = rate_ref[chunk]
        logits = (sum_rows(g * y) * rate * (1.0 - HD * MB * rate)).astype(BF16)
        dbias_ref[...] += logits.astype(F32)
        rated = (g * rate).astype(BF16)
        du = y * coef[0:1]
        dg = du - sum_rows(du) / HD - xh * (sum_rows(du * xh) / HD)
        tied = dg * gain
        dgain_ref[...] += dg * (2.0 * gain * xh + target_ref[chunk])
        dshift_ref[...] += tied
        tied = tied.astype(BF16)
        earlier = earlier_ref[...]
        later = earlier_ref[...].T
        t_out = masked(dot_tn(rated, dout) * output_ref[...], same_doc).astype(BF16)
        t_in = masked(
            dot_tn(rated, dz) * earlier + dot_tn(dz, rated) * later, same_doc
        ).astype(BF16)
        states = jnp.concatenate([state_ref[chunk], w_ref[...]], axis=0).astype(BF16)
        dq = dot_tn(jnp.concatenate([masked(dout, live), masked(dout, dead)], axis=0), states)
        dq = dq - dot_tn(t_out, key_rows)
        sources = jnp.concatenate(
            [masked(dz, live), masked(dz, dead), masked(-rated, kept), tied], axis=0
        )
        pick = selector()
        dk = dot_tn(
            sources, jnp.concatenate([states, lam_ref[slot(chunk)].astype(BF16), pick], axis=0)
        )
        dk = dk - dot_nn(
            jnp.concatenate([t_out, t_in], axis=1),
            jnp.concatenate([query_rows, key_rows], axis=0),
        )
        dv = -dot_tn(tied, pick)
        rows = chunk_rows(chunk)
        dproj_ref[rows, 0:LANES] = (join_heads(dq) + dinner_ref[rows, :].astype(F32)).astype(BF16)
        dproj_ref[rows, LANES : 2 * LANES] = join_heads(dk).astype(BF16)
        dproj_ref[rows, 2 * LANES : 3 * LANES] = join_heads(dv).astype(BF16)
        dproj_ref[rows, 3 * LANES : 4 * LANES] = dgate_ref[rows, :]
        diagonal = masked(
            jnp.broadcast_to(logits.astype(F32), (LANES, LANES)), square_iota(0) == square_iota(1)
        ).astype(BF16)
        head_column = (square_iota(1) == (square_iota(0) >> 6)).astype(F32).astype(BF16)
        spread = dot_nn(diagonal, head_column)
        dproj_ref[rows, 4 * LANES :] = (spread[:CHUNK] + spread[CHUNK:]).astype(BF16)

    last = chunks - 1
    prepare(last)
    base_ref[slot(last)] = free_ref[slot(last)]

    def body(index, carry):
        chunk = last - index
        lam_w, lam_c, dz_after = carry
        for step, when in enumerate(BACKWARD_STEPS):
            pl.when(index == when)(gather.steps[step])
        after = wrap(chunk + 1, chunks)
        cross = mx_ref[chunk + 1]
        dz = chain(chunk, dz_after, cross)
        add_w, add_c = into_state(after, split_heads(columns(after, 1)), dz_after)
        lam_w, lam_c = lam_w + add_w, lam_c + add_c
        lam_ref[slot(chunk)] = lam_w
        keep = places.keeps(chunk)
        dw_ref[...] += (1.0 - keep) * lam_w
        dc_ref[...] += (1.0 - keep) * lam_c
        add_w, add_c = into_state(chunk, split_heads(columns(chunk, 0)), dout_ref[slot(chunk)])
        lam_w, lam_c = keep * lam_w + add_w, keep * lam_c + add_c
        before = wrap(chunk - 1, chunks)

        @pl.when(chunk > 0)
        def _():
            prepare(before)
            base_ref[slot(before)] = free_ref[slot(before)] + reach_back(before, lam_w, lam_c)

        @pl.when(index > 0)
        def _():
            finish(after)

        return lam_w, lam_c, dz

    zero = jnp.zeros((HD, LANES), F32)
    lam_w, lam_c, dz = lax.fori_loop(
        0, chunks, body, (zero, zero, jnp.zeros((HD, LANES), BF16))
    )
    add_w, add_c = into_state(0, split_heads(columns(0, 1)), dz)
    dw_ref[...] += lam_w + add_w
    dc_ref[...] += lam_c + add_c
    finish(0)
    gather.end()


def whole_vmem(count):
    return [pl.BlockSpec(memory_space=pltpu.VMEM) for _ in range(count)]


def inner_forward(starts, proj, rates, ttt_w, ttt_b, gain, shift, own, number):
    tokens = proj.shape[0]
    chunks = tokens // CHUNK
    cell = jax.ShapeDtypeStruct((chunks, HD, LANES), F32)
    square = jax.ShapeDtypeStruct((HD, LANES), F32)
    return pl.pallas_call(
        forward_kernel,
        out_shape=[
            jax.ShapeDtypeStruct((tokens, LANES), BF16),
            cell,
            cell,
            cell,
            jax.ShapeDtypeStruct((chunks + 1, HD, LANES), F32),
            cell,
            jax.ShapeDtypeStruct((chunks + 1, LANES, LANES), BF16),
            jax.ShapeDtypeStruct((chunks + 1, LANES, LANES), BF16),
            jax.ShapeDtypeStruct((chunks, LANES, LANES), BF16),
            square,
            square,
            jax.ShapeDtypeStruct((RING, HD, LANES), F32),
            jax.ShapeDtypeStruct((RING, 8, LANES), F32),
            gathered_shape(own),
        ],
        in_specs=[pl.BlockSpec(memory_space=pltpu.SMEM)] + whole_vmem(6) + [ANYWHERE],
        out_specs=whole_vmem(13) + [ANYWHERE],
        scratch_shapes=[
            pltpu.VMEM((LANES, LANES), F32),
            pltpu.VMEM((LANES, LANES), F32),
            pltpu.VMEM((LANES, LANES), F32),
            pltpu.VMEM((HD, LANES), F32),
            pltpu.VMEM((HD, LANES), F32),
        ]
        + gather_scratch(),
        compiler_params=pltpu.CompilerParams(
            collective_id=number, has_side_effects=True, vmem_limit_bytes=20 * 1024 * 1024
        ),
        name="inner_forward",
    )(starts, proj, rates, ttt_w, ttt_b, gain, shift, own)


def inner_backward(starts, proj, rates, d_inner, d_gate, own, kept, number):
    tokens = proj.shape[0]
    chunks = tokens // CHUNK
    square = jax.ShapeDtypeStruct((HD, LANES), F32)
    cell = jax.ShapeDtypeStruct((RING, HD, LANES), F32)
    cell16 = jax.ShapeDtypeStruct((RING, HD, LANES), BF16)
    return pl.pallas_call(
        backward_kernel,
        out_shape=[
            jax.ShapeDtypeStruct((tokens, 5 * LANES), BF16),
            jax.ShapeDtypeStruct((1, LANES), F32),
            square,
            square,
            square,
            square,
            cell16,
            cell,
            cell,
            cell,
            cell,
            cell,
            cell,
            jax.ShapeDtypeStruct((RING, 8, LANES), F32),
            cell,
            cell16,
            cell,
            gathered_shape(own),
        ],
        in_specs=[pl.BlockSpec(memory_space=pltpu.SMEM)]
        + whole_vmem(4)
        + [ANYWHERE]
        + whole_vmem(len(kept)),
        out_specs=whole_vmem(17) + [ANYWHERE],
        scratch_shapes=[
            pltpu.VMEM((LANES, LANES), F32),
            pltpu.VMEM((LANES, LANES), F32),
            pltpu.VMEM((LANES, LANES), F32),
        ]
        + gather_scratch(),
        compiler_params=pltpu.CompilerParams(
            collective_id=number, has_side_effects=True, vmem_limit_bytes=24 * 1024 * 1024
        ),
        name="inner_backward",
    )(starts, proj, rates, d_inner, d_gate, own, *kept)


def heads_of_lanes(values):
    return jnp.sum(values.reshape(HD, 2, HD), axis=2).T


def project_kernel(x_ref, w_ref, rate_w_ref, bias_ref, proj_ref, rate_ref):
    x = x_ref[...]
    proj_ref[...] = dot_nn(x, w_ref[...]).astype(BF16)
    logits = dot_nt(rate_w_ref[...], x)
    for index in range(rate_ref.shape[0]):
        tokens = slice(index * CHUNK, (index + 1) * CHUNK)
        lanes = jnp.concatenate([logits[0:1, tokens], logits[1:2, tokens]], axis=1)
        rate_ref[index] = jax.nn.sigmoid(lanes + bias_ref[...]) / (HD * MB)


def project(gathered, w_in, w_rate, rate_bias):
    tokens, width = gathered.shape
    columns = w_in.shape[1]
    block = 4 * CHUNK
    rate_w = jnp.pad(w_rate.T, ((0, 14), (0, 0)))
    bias = jnp.repeat(rate_bias, HD)[None]
    return pl.pallas_call(
        project_kernel,
        grid=(tokens // block,),
        out_shape=[
            jax.ShapeDtypeStruct((tokens, columns), BF16),
            jax.ShapeDtypeStruct((tokens // CHUNK, 1, LANES), F32),
        ],
        in_specs=[
            pl.BlockSpec((block, width), lambda i: (i, 0)),
            pl.BlockSpec((width, columns), lambda i: (0, 0)),
            pl.BlockSpec((16, width), lambda i: (0, 0)),
            pl.BlockSpec((1, LANES), lambda i: (0, 0)),
        ],
        out_specs=[
            pl.BlockSpec((block, columns), lambda i: (i, 0)),
            pl.BlockSpec((block // CHUNK, 1, LANES), lambda i: (i, 0, 0)),
        ],
        compiler_params=pltpu.CompilerParams(vmem_limit_bytes=12 * 1024 * 1024),
        name="project",
    )(gathered, w_in, rate_w, bias)


def mean_columns(values):
    return jnp.mean(values, axis=1, keepdims=True)


GELU_RATE = 0.7978845608028654
GELU_CUBE = 0.044715


def gelu_parts(x):
    square = x * x
    tanh = jnp.tanh(GELU_RATE * x * (1.0 + GELU_CUBE * square))
    half = 0.5 * (1.0 + tanh)
    slope = half + 0.5 * x * (1.0 - tanh * tanh) * GELU_RATE * (1.0 + 3.0 * GELU_CUBE * square)
    return x * half, slope


def line_of(gains_ref, index):
    return jnp.concatenate(
        [gains_ref[k, index : index + 1, :] for k in range(gains_ref.shape[0])], axis=1
    )


def post_norm_of(inner_ref):
    inner = inner_ref[...].astype(F32)
    centred = inner - mean_columns(inner)
    rstd = lax.rsqrt(mean_columns(centred * centred) + EPS)
    return centred * rstd, rstd


def middle_forward_kernel(
    inner_ref, gate_ref, gains_ref, tokens_ref, ffn_gain_ref, w_ref, mixed_ref, hidden_ref, norm_ref
):
    xp, _ = post_norm_of(inner_ref)
    post = xp * line_of(gains_ref, 0) + line_of(gains_ref, 1)
    act, _ = gelu_parts(gate_ref[...].astype(F32))
    mixed = (post * act).astype(BF16)
    mixed_ref[...] = mixed
    pieces, _, piece = w_ref.shape
    for k in range(pieces):
        columns = slice(k * piece, (k + 1) * piece)
        hidden_ref[:, columns] = tokens_ref[:, columns].astype(F32) + dot_nn(mixed, w_ref[k])
    hidden = hidden_ref[...]
    scale = lax.rsqrt(mean_columns(hidden * hidden) + EPS)
    norm_ref[...] = (hidden * scale * ffn_gain_ref[...]).astype(BF16)


def middle_forward(inner, gate, gains, tokens, ffn_gain, w_out):
    shape = tokens.shape
    return pl.pallas_call(
        middle_forward_kernel,
        out_shape=[
            jax.ShapeDtypeStruct(shape, BF16),
            jax.ShapeDtypeStruct(shape, F32),
            jax.ShapeDtypeStruct(shape, BF16),
        ],
        in_specs=whole_vmem(6),
        out_specs=whole_vmem(3),
        compiler_params=pltpu.CompilerParams(vmem_limit_bytes=24 * 1024 * 1024),
        name="middle_forward",
    )(inner, gate, gains, tokens, ffn_gain, w_out)


def middle_backward_kernel(
    d_norm_ref,
    hidden_ref,
    cot_ref,
    ffn_gain_ref,
    inner_ref,
    gate_ref,
    gains_ref,
    w_ref,
    d_res_ref,
    d_mix_ref,
    d_inner_ref,
    d_gate_ref,
    sums_ref,
):
    hidden = hidden_ref[...]
    scale = lax.rsqrt(mean_columns(hidden * hidden) + EPS)
    d_norm = d_norm_ref[...]
    weighted = d_norm * ffn_gain_ref[...]
    normed = hidden * scale
    d_res = cot_ref[...].astype(F32) + scale * (
        weighted - normed * mean_columns(weighted * normed)
    )
    d_res_ref[...] = d_res
    d_mix_ref[...] = d_res.astype(BF16)
    pieces, _, piece = w_ref.shape
    d_mixed = dot_nt(d_mix_ref[:, 0:piece], w_ref[0])
    for k in range(1, pieces):
        d_mixed = d_mixed + dot_nt(d_mix_ref[:, k * piece : (k + 1) * piece], w_ref[k])
    xp, rstd = post_norm_of(inner_ref)
    post_gain = line_of(gains_ref, 0)
    post = xp * post_gain + line_of(gains_ref, 1)
    act, slope = gelu_parts(gate_ref[...].astype(F32))
    d_post = d_mixed * act
    d_gate_ref[...] = (d_mixed * post * slope).astype(BF16)
    dx = d_post * post_gain
    d_inner = rstd * (dx - mean_columns(dx) - xp * mean_columns(dx * xp))
    d_inner_ref[...] = d_inner.astype(BF16)
    lines = (sum_rows(d_post * xp), sum_rows(d_post), sum_rows(d_norm * normed))
    for k in range(sums_ref.shape[0]):
        columns = slice(k * LANES, (k + 1) * LANES)
        sums_ref[k] = jnp.concatenate(
            [line[:, columns] for line in lines] + [jnp.zeros((5, LANES), F32)], axis=0
        )


def middle_backward(d_norm, hidden, cotangent, ffn_gain, inner, gate, gains, w_out):
    shape = cotangent.shape
    return pl.pallas_call(
        middle_backward_kernel,
        out_shape=[
            jax.ShapeDtypeStruct(shape, F32),
            jax.ShapeDtypeStruct(shape, BF16),
            jax.ShapeDtypeStruct(shape, BF16),
            jax.ShapeDtypeStruct(shape, BF16),
            jax.ShapeDtypeStruct(gains.shape, F32),
        ],
        in_specs=whole_vmem(8),
        out_specs=whole_vmem(5),
        compiler_params=pltpu.CompilerParams(vmem_limit_bytes=32 * 1024 * 1024),
        name="middle_backward",
    )(d_norm, hidden, cotangent, ffn_gain, inner, gate, gains, w_out)


RING_X = 4
RING_Y = 4
GROUP = RING_X * RING_Y
UNITS = 4
MESH = pl.DeviceIdType.MESH


def place_at(head, dx, dy):
    return lax.rem(head // RING_Y + dx + RING_X, RING_X) * RING_Y + lax.rem(
        lax.rem(head, RING_Y) + dy + RING_Y, RING_Y
    )


def neighbours(head):
    return {
        (axis, way): place_at(head, way if axis == 0 else 0, way if axis == 1 else 0)
        for axis in (0, 1)
        for way in (1, -1)
    }


def greet(peers):
    barrier = pltpu.get_barrier_semaphore()
    for peer in peers:
        pl.semaphore_signal(barrier, inc=1, device_id=peer, device_id_type=MESH)
    pl.semaphore_wait(barrier, len(peers))


def moved(place, axis, way):
    shift = (way, 0) if axis == 0 else (0, way)
    return tuple((p - s) % n for p, s, n in zip(place, shift, (RING_X, RING_Y)))


class Gather:
    def __init__(self, own_ref, full_ref, send_sem, recv_sem, local_sem):
        self.own_ref, self.full_ref = own_ref, full_ref
        self.send_sem, self.recv_sem, self.local_sem = send_sem, recv_sem, local_sem
        self.head = lax.axis_index("head")
        self.near = neighbours(self.head)
        self.rows = own_ref.shape[0]
        self.unit_rows = self.rows // UNITS
        self.count = 0
        self.halves = ((0, (0, 1)), (1, (2, 3)))
        self.steps = [
            partial(self.first_arrivals, 0),
            partial(self.first_arrivals, 1),
            partial(self.second_hops, (0,)),
            self.far_arrivals,
            partial(self.second_hops, (1,)),
            partial(self.second_hops, (3,)),
            partial(self.second_hops, (2,)),
        ]

    def slab(self, place, unit):
        start = place_at(self.head, *place) * self.rows + unit * self.unit_rows
        return self.full_ref.at[pl.ds(pl.multiple_of(start, self.unit_rows), self.unit_rows)]

    def arrival(self, place, unit):
        return self.recv_sem.at[(place[0] * RING_Y + place[1]) * UNITS + unit]

    def send(self, place, unit, axis, way):
        source = (
            self.own_ref.at[pl.ds(unit * self.unit_rows, self.unit_rows)]
            if place == (0, 0)
            else self.slab(place, unit)
        )
        pltpu.make_async_remote_copy(
            src_ref=source,
            dst_ref=self.slab(place, unit),
            send_sem=self.send_sem.at[self.count],
            recv_sem=self.arrival(moved(place, axis, way), unit),
            device_id={"head": self.near[axis, way]},
            device_id_type=MESH,
        ).start()
        self.count += 1

    def waiter(self, place, unit, send_number=0):
        return pltpu.make_async_remote_copy(
            src_ref=self.slab(place, unit),
            dst_ref=self.slab(place, unit),
            send_sem=self.send_sem.at[send_number],
            recv_sem=self.arrival(place, unit),
            device_id={"head": self.near[0, 1]},
            device_id_type=MESH,
        )

    def arrive(self, place, unit):
        self.waiter(place, unit).wait_recv()

    def own_copy(self):
        start = pl.multiple_of(self.head * self.rows, self.rows)
        return pltpu.make_async_copy(
            self.own_ref, self.full_ref.at[pl.ds(start, self.rows)], self.local_sem
        )

    def cross(self, axis, first, second):
        first, second = first % RING_X, second % RING_X
        return (first, second) if axis == 0 else (second, first)

    def start(self):
        greet([{"head": peer} for peer in self.near.values()])
        self.own_copy().start()
        for turned in (False, True):
            for axis, units in self.halves:
                for unit in units:
                    for way in (1, -1):
                        self.send((0, 0), unit, 1 - axis if turned else axis, way)

    def first_arrivals(self, step):
        for axis, units in self.halves:
            for way in (1, -1):
                place = self.cross(axis, -way, 0)
                unit = units[0 if (way == 1) == (step == 0) else 1]
                self.arrive(place, unit)
                if step == 0:
                    self.send(place, unit, axis, way)
                for turn in (1, -1):
                    self.send(place, unit, 1 - axis, turn)

    def second_hops(self, firsts):
        for first in firsts:
            for axis, units in self.halves:
                for way in (1, -1):
                    unit = units[0 if way == 1 else 1]
                    place = self.cross(axis, first, -way)
                    self.arrive(place, unit)
                    self.send(place, unit, 1 - axis, way)

    def far_arrivals(self):
        for way in (1, -1):
            for axis, units in self.halves:
                unit = units[0 if way == 1 else 1]
                place = self.cross(axis, 2, 0)
                self.arrive(place, unit)
                for turn in (1, -1):
                    self.send(place, unit, 1 - axis, turn)

    def end(self):
        for first in range(RING_X):
            for axis, units in self.halves:
                for way in (1, -1):
                    self.arrive(self.cross(axis, first, -way), units[1 if way == 1 else 0])
        for first in range(RING_X):
            for axis, units in self.halves:
                for unit in units:
                    self.arrive(self.cross(axis, first, 2), unit)
        for number in range(TRANSFERS):
            self.waiter((0, 0), 0, number).wait_send()
        self.own_copy().wait()


TRANSFERS = UNITS * (GROUP - 1)
STAGED = 32
ANYWHERE = pl.BlockSpec(memory_space=pl.ANY)


def gather_kernel(*refs):
    gather = Gather(*refs)
    gather.start()
    for step in gather.steps:
        step()
    gather.end()


def gather_scratch():
    return [
        pltpu.SemaphoreType.DMA((TRANSFERS,)),
        pltpu.SemaphoreType.DMA((UNITS * GROUP,)),
        pltpu.SemaphoreType.DMA,
    ]


def gathered_shape(own):
    return jax.ShapeDtypeStruct((own.shape[0] * GROUP, own.shape[1]), own.dtype)


def gather_rows(own, number):
    return pl.pallas_call(
        gather_kernel,
        out_shape=gathered_shape(own),
        in_specs=[ANYWHERE],
        out_specs=ANYWHERE,
        scratch_shapes=gather_scratch(),
        compiler_params=pltpu.CompilerParams(collective_id=number, has_side_effects=True),
        name="gather_rows",
    )(own)


class SmallSums:
    def __init__(self, shard_ref, shard_out, lines_out, held, send_sem, recv_sem, *line_sems):
        self.shard_ref, self.shard_out, self.lines_out = shard_ref, shard_out, lines_out
        self.held, self.send_sem, self.recv_sem = held, send_sem, recv_sem
        self.line_send, self.line_recv = line_sems
        head, seq = lax.axis_index("head"), lax.axis_index("seq")
        self.head = head
        self.seqs = held.shape[0]
        self.seq_peers = [lax.rem(seq + ahead, self.seqs) for ahead in range(1, self.seqs)]
        self.head_peers = [lax.rem(head + ahead, GROUP) for ahead in range(1, GROUP)]

    def peers(self):
        return [{"seq": peer} for peer in self.seq_peers] + [
            {"head": peer} for peer in self.head_peers
        ]

    def start(self):
        self.sends = []
        for ahead, peer in enumerate(self.seq_peers, 1):
            done = pltpu.make_async_remote_copy(
                src_ref=self.shard_ref,
                dst_ref=self.held.at[ahead],
                send_sem=self.send_sem.at[ahead],
                recv_sem=self.recv_sem.at[ahead],
                device_id={"seq": peer},
                device_id_type=MESH,
            )
            done.start()
            self.sends.append(done)

    def turn(self):
        for done in self.sends:
            done.wait_recv()
        shard = self.shard_ref[...]
        for ahead in range(1, self.seqs):
            shard = shard + self.held[ahead]
        self.shard_out[...] = shard
        self.lines_out[self.head] = shard[0:8]
        self.passed = []
        for ahead, peer in enumerate(self.head_peers, 1):
            done = pltpu.make_async_remote_copy(
                src_ref=self.shard_out.at[0:8],
                dst_ref=self.lines_out.at[self.head],
                send_sem=self.line_send.at[ahead],
                recv_sem=self.line_recv.at[ahead],
                device_id={"head": peer},
                device_id_type=MESH,
            )
            done.start()
            self.passed.append(done)

    def end(self):
        for done in self.passed:
            done.wait_recv()
        for done in self.sends + self.passed:
            done.wait_send()


def everywhere_kernel(part_ref, sum_ref, seq_held, line_ref, head_held, *sems):
    head, seq = lax.axis_index("head"), lax.axis_index("seq")
    seqs = seq_held.shape[0]
    seq_peers = [lax.rem(seq + ahead, seqs) for ahead in range(1, seqs)]
    head_peers = [lax.rem(head + ahead, GROUP) for ahead in range(1, GROUP)]
    greet([{"seq": peer} for peer in seq_peers] + [{"head": peer} for peer in head_peers])

    def exchange(source, held, axis, peers, send_sem, recv_sem):
        sends = []
        for ahead, peer in enumerate(peers, 1):
            done = pltpu.make_async_remote_copy(
                src_ref=source,
                dst_ref=held.at[ahead],
                send_sem=send_sem.at[ahead],
                recv_sem=recv_sem.at[ahead],
                device_id={axis: peer},
                device_id_type=MESH,
            )
            done.start()
            sends.append(done)
        total = source[...]
        for ahead, done in enumerate(sends, 1):
            done.wait_recv()
            total = total + held[ahead]
        return total, sends

    line_ref[...], sends = exchange(part_ref, seq_held, "seq", seq_peers, *sems[:2])
    sum_ref[...], passed = exchange(line_ref, head_held, "head", head_peers, *sems[2:])
    for done in sends + passed:
        done.wait_send()


def sum_everywhere(part, seqs, number):
    return pl.pallas_call(
        everywhere_kernel,
        out_shape=jax.ShapeDtypeStruct(part.shape, F32),
        in_specs=whole_vmem(1),
        out_specs=pl.BlockSpec(memory_space=pltpu.VMEM),
        scratch_shapes=[
            pltpu.VMEM((seqs,) + part.shape, F32),
            pltpu.VMEM(part.shape, F32),
            pltpu.VMEM((GROUP,) + part.shape, F32),
            pltpu.SemaphoreType.DMA((seqs,)),
            pltpu.SemaphoreType.DMA((seqs,)),
            pltpu.SemaphoreType.DMA((GROUP,)),
            pltpu.SemaphoreType.DMA((GROUP,)),
        ],
        compiler_params=pltpu.CompilerParams(
            collective_id=number, has_side_effects=True, vmem_limit_bytes=4 * 1024 * 1024
        ),
        name="sum_everywhere",
    )(part)


def scatter_kernel(part_ref, sum_ref, held_ref, stage_ref, send_sem, recv_sem):
    scatter_body(None, part_ref, sum_ref, held_ref, stage_ref, send_sem, recv_sem)


def scatter_small_kernel(
    part_ref,
    shard_ref,
    sum_ref,
    shard_out,
    lines_out,
    held_ref,
    stage_ref,
    send_sem,
    recv_sem,
    *scratch,
):
    small = SmallSums(shard_ref, shard_out, lines_out, *scratch)
    scatter_body(small, part_ref, sum_ref, held_ref, stage_ref, send_sem, recv_sem)


def scatter_body(small, part_ref, sum_ref, held_ref, stage_ref, send_sem, recv_sem):
    head = lax.axis_index("head")
    near = neighbours(head)
    rows = sum_ref.shape[0]
    unit_rows = rows // UNITS
    peers = [{"head": peer} for peer in near.values()]
    greet(peers if small is None else small.peers())
    sends, blocks, staged = [], [], {}

    def slab(place, unit):
        start = place_at(head, *place) * rows + unit * unit_rows
        return part_ref.at[pl.ds(pl.multiple_of(start, unit_rows), unit_rows)]

    def held(index):
        return pl.ds(index * unit_rows, unit_rows)

    def stage(place, unit, total):
        block = stage_ref.at[held(len(blocks))]
        block[...] = total.astype(BF16)
        blocks.append(block)
        staged[place, unit] = block

    def send(place, unit, axis, way):
        index = len(sends)
        done = pltpu.make_async_remote_copy(
            src_ref=staged.get((place, unit), slab(place, unit)),
            dst_ref=held_ref.at[held(index)],
            send_sem=send_sem.at[index],
            recv_sem=recv_sem.at[index],
            device_id={"head": near[axis, way]},
            device_id_type=MESH,
        )
        done.start()
        sends.append(done)
        return index

    def arrived(index):
        sends[index].wait_recv()
        return held_ref[held(index)].astype(F32)

    def add_to(place, unit, *indices):
        total = staged.get((place, unit), slab(place, unit))[...].astype(F32)
        for index in indices:
            total = total + arrived(index)
        return total

    def cross(axis, first, second):
        first, second = first % RING_X, second % RING_X
        return (first, second) if axis == 0 else (second, first)

    halves = ((1, (0, 1)), (0, (2, 3)))

    def far(axis, units, other):
        return {
            way: send(cross(axis, 2, other), units[0 if way == 1 else 1], axis, way)
            for way in (1, -1)
        }

    def plain(axis, units, other):
        return {
            way: send(cross(axis, way, other), units[1 if way == 1 else 0], axis, way)
            for way in (1, -1)
        }

    def onward(axis, units, other, from_far):
        result = {}
        for way in (1, -1):
            place, unit = cross(axis, way, other), units[0 if way == 1 else 1]
            stage(place, unit, add_to(place, unit, from_far[way]))
            result[way] = send(place, unit, axis, way)
        return result

    def collect(axis, units, other, by_plain, by_onward):
        place = cross(axis, 0, other)
        return [
            add_to(place, units[0], by_onward[1], by_plain[-1]),
            add_to(place, units[1], by_onward[-1], by_plain[1]),
        ]

    order = (2, 1, 3, 0)
    fars = {(axis, o): far(axis, units, o) for o in order for axis, units in halves}
    plains = {(axis, o): plain(axis, units, o) for o in order for axis, units in halves}
    if small is not None:
        small.start()
    onwards = {
        (axis, o): onward(axis, units, o, fars[axis, o]) for o in order for axis, units in halves
    }
    last_far, last_plain, last_onward = {}, {}, {}

    def first_sum(axis, units, other):
        totals = collect(axis, units, other, plains[axis, other], onwards[axis, other])
        place = cross(axis, 0, other)
        for unit, total in zip(units, totals):
            stage(place, unit, total)

    for axis, units in halves:
        first_sum(axis, units, 2)
        last_far[axis] = far(1 - axis, units, 0)
    for axis, units in halves:
        first_sum(axis, units, 1)
        first_sum(axis, units, 3)
        last_plain[axis] = plain(1 - axis, units, 0)
    for axis, units in halves:
        last_onward[axis] = onward(1 - axis, units, 0, last_far[axis])
    if small is not None:
        small.turn()
    for axis, units in halves:
        own = collect(axis, units, 0, plains[axis, 0], onwards[axis, 0])
        extra = (
            (last_onward[axis][1], last_plain[axis][-1]),
            (last_onward[axis][-1], last_plain[axis][1]),
        )
        for unit, total, indices in zip(units, own, extra):
            for index in indices:
                total = total + arrived(index)
            sum_ref[pl.ds(unit * unit_rows, unit_rows), :] = total
    for done in sends:
        done.wait_send()
    if small is not None:
        small.end()


def scatter_scratch(rows, width):
    return [
        pltpu.VMEM((TRANSFERS * rows // UNITS, width), BF16),
        pltpu.VMEM((STAGED * rows // UNITS, width), BF16),
        pltpu.SemaphoreType.DMA((TRANSFERS,)),
        pltpu.SemaphoreType.DMA((TRANSFERS,)),
    ]


def scatter_rows(part, number):
    rows, width = part.shape[0] // GROUP, part.shape[1]
    return pl.pallas_call(
        scatter_kernel,
        out_shape=jax.ShapeDtypeStruct((rows, width), F32),
        in_specs=[pl.BlockSpec(memory_space=pltpu.VMEM)],
        out_specs=pl.BlockSpec(memory_space=pltpu.VMEM),
        scratch_shapes=scatter_scratch(rows, width),
        compiler_params=pltpu.CompilerParams(
            collective_id=number, has_side_effects=True, vmem_limit_bytes=28 * 1024 * 1024
        ),
        name="scatter_rows",
    )(part)


def scatter_rows_and_small(part, shard, seqs, number):
    rows, width = part.shape[0] // GROUP, part.shape[1]
    return pl.pallas_call(
        scatter_small_kernel,
        out_shape=[
            jax.ShapeDtypeStruct((rows, width), F32),
            jax.ShapeDtypeStruct(shard.shape, F32),
            jax.ShapeDtypeStruct((GROUP, 8, LANES), F32),
        ],
        in_specs=whole_vmem(2),
        out_specs=whole_vmem(3),
        scratch_shapes=scatter_scratch(rows, width)
        + [
            pltpu.VMEM((seqs,) + shard.shape, F32),
            pltpu.SemaphoreType.DMA((seqs,)),
            pltpu.SemaphoreType.DMA((seqs,)),
            pltpu.SemaphoreType.DMA((GROUP,)),
            pltpu.SemaphoreType.DMA((GROUP,)),
        ],
        compiler_params=pltpu.CompilerParams(
            collective_id=number, has_side_effects=True, vmem_limit_bytes=28 * 1024 * 1024
        ),
        name="scatter_rows_and_small",
    )(part, shard)


def to_tokens_kernel(
    inner_ref,
    gate_ref,
    gains_ref,
    inner_out,
    gate_out,
    gains_out,
    send_sem,
    recv_sem,
    local_sem,
):
    head = lax.axis_index("head")
    rows = inner_out.shape[0]
    first = gate_ref.shape[1] - LANES
    pairs = ((inner_ref, inner_out), (gate_ref.at[:, first:], gate_out))

    def rows_of(index):
        return pl.ds(pl.multiple_of(index * rows, rows), rows)

    def columns_of(index):
        return pl.ds(pl.multiple_of(index * LANES, LANES), LANES)

    mine = [
        pltpu.make_async_copy(
            source.at[rows_of(head)], target.at[:, columns_of(head)], local_sem.at[index]
        )
        for index, (source, target) in enumerate(pairs)
    ] + [pltpu.make_async_copy(gains_ref, gains_out.at[head], local_sem.at[2])]
    for done in mine:
        done.start()
    greet([{"head": lax.rem(head + ahead, GROUP)} for ahead in range(1, GROUP)])
    sends = []
    for ahead in range(1, GROUP):
        peer = lax.rem(head + ahead, GROUP)
        jobs = [
            (source.at[rows_of(peer)], target.at[:, columns_of(head)]) for source, target in pairs
        ] + [(gains_ref, gains_out.at[head])]
        for index, (source, target) in enumerate(jobs):
            done = pltpu.make_async_remote_copy(
                src_ref=source,
                dst_ref=target,
                send_sem=send_sem.at[ahead, index],
                recv_sem=recv_sem.at[ahead, index],
                device_id={"head": peer},
                device_id_type=MESH,
            )
            done.start()
            sends.append(done)
    for done in mine:
        done.wait()
    for done in sends:
        done.wait()


def to_tokens(inner, gate, gains, number):
    rows = inner.shape[0] // GROUP
    wide = jax.ShapeDtypeStruct((rows, GROUP * LANES), BF16)
    return pl.pallas_call(
        to_tokens_kernel,
        out_shape=[wide, wide, jax.ShapeDtypeStruct((GROUP,) + gains.shape, F32)],
        in_specs=whole_vmem(3),
        out_specs=whole_vmem(3),
        scratch_shapes=[
            pltpu.SemaphoreType.DMA((GROUP, 3)),
            pltpu.SemaphoreType.DMA((GROUP, 3)),
            pltpu.SemaphoreType.DMA((3,)),
        ],
        compiler_params=pltpu.CompilerParams(
            collective_id=number, has_side_effects=True, vmem_limit_bytes=8 * 1024 * 1024
        ),
        name="to_tokens",
    )(inner, gate, gains)


def to_heads_kernel(
    inner_ref,
    gate_ref,
    mixed_ref,
    sums_ref,
    inner_out,
    gate_out,
    mixed_out,
    sums_out,
    send_sem,
    recv_sem,
    local_sem,
):
    head = lax.axis_index("head")
    rows = inner_ref.shape[0]
    triples = ((inner_ref, inner_out), (gate_ref, gate_out), (mixed_ref, mixed_out))

    def rows_of(index):
        return pl.ds(pl.multiple_of(index * rows, rows), rows)

    def columns_of(index):
        return pl.ds(pl.multiple_of(index * LANES, LANES), LANES)

    def jobs(peer):
        return [
            (source.at[:, columns_of(peer)], target.at[rows_of(head)]) for source, target in triples
        ] + [(sums_ref.at[peer], sums_out.at[head])]

    mine = [
        pltpu.make_async_copy(source, target, local_sem.at[index])
        for index, (source, target) in enumerate(jobs(head))
    ]
    for done in mine:
        done.start()
    greet([{"head": lax.rem(head + ahead, GROUP)} for ahead in range(1, GROUP)])
    sends = []
    for ahead in range(1, GROUP):
        peer = lax.rem(head + ahead, GROUP)
        for index, (source, target) in enumerate(jobs(peer)):
            done = pltpu.make_async_remote_copy(
                src_ref=source,
                dst_ref=target,
                send_sem=send_sem.at[ahead, index],
                recv_sem=recv_sem.at[ahead, index],
                device_id={"head": peer},
                device_id_type=MESH,
            )
            done.start()
            sends.append(done)
    for done in mine:
        done.wait()
    for done in sends:
        done.wait()


def to_heads(inner, gate, mixed, sums, number):
    rows = inner.shape[0]
    tall = jax.ShapeDtypeStruct((rows * GROUP, LANES), BF16)
    return pl.pallas_call(
        to_heads_kernel,
        out_shape=[tall, tall, tall, jax.ShapeDtypeStruct(sums.shape, F32)],
        in_specs=whole_vmem(4),
        out_specs=whole_vmem(4),
        scratch_shapes=[
            pltpu.SemaphoreType.DMA((GROUP, 4)),
            pltpu.SemaphoreType.DMA((GROUP, 4)),
            pltpu.SemaphoreType.DMA((4,)),
        ],
        compiler_params=pltpu.CompilerParams(
            collective_id=number, has_side_effects=True, vmem_limit_bytes=8 * 1024 * 1024
        ),
        name="to_heads",
    )(inner, gate, mixed, sums)


def after(value, *others):
    return lax.optimization_barrier((value,) + others)[0]


def per_device(
    tokens,
    doc_starts,
    norm_gain,
    w_in,
    w_rate,
    rate_bias,
    ttt_w,
    ttt_b,
    ttt_gain,
    ttt_shift,
    post_gain,
    post_bias,
    w_out,
    ffn_gain,
    w_gate_up,
    w_down,
    cotangent,
):
    seq = lax.axis_index("seq")
    seqs = lax.axis_size("seq")
    tok_rows, width = tokens.shape
    head_count, head_dim = ttt_b.shape
    local_width = head_count * head_dim
    ffn_local = w_down.shape[0]
    w_in_flat = w_in.reshape(width, 4 * local_width)
    w_gu_flat = w_gate_up.reshape(width, 2 * ffn_local)
    ffn_gain_line = ffn_gain[None]

    piece = width // seqs
    w_out_piece = lax.dynamic_slice_in_dim(w_out, seq * piece, piece, axis=1)
    w_out_all = lax.all_gather(w_out_piece, ("seq", "head"), axis=0, tiled=True)
    w_out_all = w_out_all.reshape(seqs, width, piece)

    resid = tokens.astype(F32)
    scale_one = lax.rsqrt(jnp.mean(resid * resid, axis=-1, keepdims=True) + EPS)
    norm_one = (resid * scale_one * norm_gain).astype(BF16)
    gathered = gather_rows(norm_one, 0)
    projected, rate_lanes = project(gathered, w_in_flat, w_rate, rate_bias)
    inner, *kept, _, _, cot_rows = inner_forward(
        doc_starts, projected, rate_lanes, ttt_w, ttt_b, ttt_gain, ttt_shift, cotangent, 7
    )

    gains = jnp.concatenate(
        [post_gain[None], post_bias[None], jnp.zeros((6, local_width), F32)], axis=0
    )
    inner_tok, gate_tok, all_gains = to_tokens(inner, projected, gains, 1)
    mixed_tok, hidden_res, norm_two = middle_forward(
        inner_tok, gate_tok, all_gains, tokens, ffn_gain_line, w_out_all
    )

    ffn_rows = gather_rows(norm_two, 2)
    gate_up = dot_nn(ffn_rows, w_gu_flat).astype(BF16)
    gate_part = gate_up[:, :ffn_local].astype(F32)
    up_part = gate_up[:, ffn_local:].astype(F32)
    silu_val, silu_pull = jax.vjp(jax.nn.silu, gate_part)
    hidden_state = (silu_val * up_part).astype(BF16)
    ffn_part = dot_nn(hidden_state, w_down).astype(BF16)
    d_hidden = dot_nt(cot_rows, w_down)
    d_gate_part = silu_pull(d_hidden * up_part)[0]
    d_gate_up = jnp.concatenate([d_gate_part, d_hidden * silu_val], axis=1).astype(BF16)
    grad_w_down = dot_tn(hidden_state, cot_rows).astype(BF16)
    grad_w_gate_up = dot_tn(ffn_rows, d_gate_up).reshape(width, 2, ffn_local).astype(BF16)
    d_norm_part = dot_nt(d_gate_up, w_gu_flat).astype(BF16)
    d_norm_two = scatter_rows(after(d_norm_part, grad_w_down, grad_w_gate_up, ffn_part), 3)
    ffn_out = lax.psum_scatter(
        after(ffn_part, d_norm_two), "head", scatter_dimension=0, tiled=True
    )

    d_res, d_mix, d_inner_tok, d_gate_tok, token_sums = middle_backward(
        d_norm_two,
        hidden_res,
        cotangent,
        ffn_gain_line,
        inner_tok,
        gate_tok,
        all_gains,
        w_out_all,
    )
    d_inner, d_gate, mixed_in, head_sums = to_heads(
        d_inner_tok, d_gate_tok, mixed_tok, token_sums, 4
    )
    head_sums = jnp.sum(head_sums, axis=0)
    output = (hidden_res + ffn_out.astype(F32)).astype(BF16)

    d_projected, d_bias, d_start_w, d_start_c, d_gain, d_shift, *_, mix_rows = inner_backward(
        doc_starts, projected, rate_lanes, d_inner, d_gate, d_mix, kept, 8
    )
    grad_in = dot_tn(gathered, d_projected)
    w_columns = jnp.pad(w_rate, ((0, 0), (0, local_width - head_count)))
    w_columns = jnp.concatenate([w_in_flat, w_columns], axis=1)
    grad_w_rate = grad_in[:, 4 * local_width : 4 * local_width + head_count]
    grad_w_in = grad_in[:, : 4 * local_width].astype(BF16).reshape(width, 4, local_width)
    grad_w_out = dot_tn(mixed_in, mix_rows).astype(BF16)
    sum_w_in, sum_w_out, sum_w_down, sum_w_gate_up = lax.psum(
        after((grad_w_in, grad_w_out, grad_w_down, grad_w_gate_up), ffn_out), "seq"
    )
    singles = jnp.stack(
        [
            head_sums[2],
            head_sums[0],
            head_sums[1],
            d_start_c[:, ::head_dim].T.reshape(LANES),
            heads_of_lanes(d_gain).reshape(LANES),
            heads_of_lanes(d_shift).reshape(LANES),
            d_bias[0],
            jnp.zeros((LANES,), F32),
        ]
    )
    rate_rows = grad_w_rate.T.reshape(2 * width // LANES, LANES)
    shard = jnp.concatenate([singles, d_start_w, rate_rows], axis=0)
    d_norm_part = dot_nt(d_projected, w_columns).astype(BF16)
    d_norm_one, shard, lines = scatter_rows_and_small(
        after(d_norm_part, grad_w_in, grad_w_out), shard, seqs, 5
    )
    weighted = d_norm_one * norm_gain
    normed = resid * scale_one
    grad_tokens = d_res + scale_one * (
        weighted - normed * jnp.mean(weighted * normed, axis=-1, keepdims=True)
    )

    grad_norm_gain = jnp.sum(d_norm_one * normed, axis=0).reshape(GROUP, LANES)
    sum_norm_gain = sum_everywhere(grad_norm_gain, seqs, 6).reshape(width)
    sum_ffn_gain = lines[:, 0].reshape(width)
    sum_ttt_w = shard[8 : 8 + head_dim].reshape(head_dim, head_count, head_dim)
    per_head = (head_count, head_dim)
    return (
        output,
        grad_tokens,
        sum_norm_gain,
        sum_w_in.astype(F32),
        shard[8 + head_dim :].reshape(head_count, width).T,
        jnp.sum(shard[6].reshape(per_head), axis=1),
        sum_ttt_w.transpose(1, 2, 0),
        shard[3].reshape(per_head),
        shard[4].reshape(per_head),
        shard[5].reshape(per_head),
        shard[1],
        shard[2],
        sum_w_out.astype(F32),
        sum_ffn_gain,
        sum_w_gate_up.astype(F32),
        sum_w_down.astype(F32),
    )


def solution(mesh):
    return jax.shard_map(
        per_device,
        mesh=mesh,
        in_specs=(
            P(("seq", "head"), None),
            P("seq", None),
            P(),
            P(None, None, "head"),
            P(None, "head"),
            P("head"),
            P("head", None, None),
            P("head", None),
            P("head", None),
            P("head", None),
            P("head"),
            P("head"),
            P("head", None),
            P(),
            P(None, None, "head"),
            P("head", None),
            P(("seq", "head"), None),
        ),
        out_specs=(
            P(("seq", "head"), None),
            P(("seq", "head"), None),
            P(),
            P(None, None, "head"),
            P(None, "head"),
            P("head"),
            P("head", None, None),
            P("head", None),
            P("head", None),
            P("head", None),
            P("head"),
            P("head"),
            P("head", None),
            P(),
            P(None, None, "head"),
            P("head", None),
        ),
        check_vma=False,
    )
```

```python
from functools import partial

import jax
import jax.numpy as jnp
from jax import lax
from jax.experimental import pallas as pl
from jax.experimental.pallas import tpu as pltpu
from jax.sharding import PartitionSpec as P

MB = 16
EPS = 1e-06
HD = 64
STEPS = 4
CHUNK = STEPS * MB
LANES = 2 * CHUNK
BF16 = jnp.bfloat16
MOST_VMEM = 56 * 1024 * 1024
F32 = jnp.float32


def dot_nn(a, b):
    return lax.dot_general(a, b, (((1,), (0,)), ((), ())), preferred_element_type=F32)


def dot_nt(a, b):
    return lax.dot_general(a, b, (((1,), (1,)), ((), ())), preferred_element_type=F32)


def dot_tn(a, b):
    return lax.dot_general(a, b, (((0,), (0,)), ((), ())), preferred_element_type=F32)


def sum_rows(x):
    return jnp.sum(x, axis=0, keepdims=True)


def square_iota(dim):
    return lax.broadcasted_iota(jnp.int32, (LANES, LANES), dim)


def step_of(index):
    return (index >> 4) & (STEPS - 1)


class Places:
    def __init__(self, starts_ref):
        self.second = starts_ref[0, 1]
        self.third = starts_ref[0, 2]

    def document(self, step):
        return (step >= self.second).astype(jnp.int32) + (step >= self.third).astype(jnp.int32)

    def lane_documents(self, chunk):
        return self.document(chunk * STEPS + step_of(lax.broadcasted_iota(jnp.int32, (1, LANES), 1)))

    def row_documents(self, chunk):
        return self.document(chunk * STEPS + step_of(lax.broadcasted_iota(jnp.int32, (LANES, 1), 0)))

    def entry(self, chunk):
        return self.document(chunk * STEPS - 1)

    def last(self, chunk):
        return self.document(chunk * STEPS + STEPS - 1)

    def keeps(self, chunk):
        return (self.entry(chunk) == self.last(chunk)).astype(F32)


def split_heads(rows):
    first = lax.broadcasted_iota(jnp.int32, rows.shape, 1) < HD
    zero = jnp.zeros_like(rows)
    return jnp.concatenate([jnp.where(first, rows, zero), jnp.where(first, zero, rows)], axis=0)


def join_heads(square):
    first = lax.broadcasted_iota(jnp.int32, (CHUNK, LANES), 1) < HD
    return jnp.where(first, square[:CHUNK], square[CHUNK:])


def to_columns(rows):
    turned = split_heads(rows).T
    return turned[:HD] + turned[HD:]


def to_rows(columns):
    return join_heads(split_heads(columns).T)


def selector():
    row = lax.broadcasted_iota(jnp.int32, (HD, LANES), 0)
    col = lax.broadcasted_iota(jnp.int32, (HD, LANES), 1)
    return (row == (col & (HD - 1))).astype(F32).astype(BF16)


RING = 4


def slot(chunk):
    return lax.rem(chunk, RING)


def wrap(chunk, chunks):
    return lax.rem(chunk + chunks, chunks)


def chunk_rows(chunk):
    return pl.ds(pl.multiple_of(chunk * CHUNK, CHUNK), CHUNK)


def same_head():
    return (square_iota(0) >> 6) == (square_iota(1) >> 6)


def masked(values, keep):
    return jnp.where(keep, values, jnp.zeros_like(values))


def inner_masks(head_ref, earlier_ref, output_ref):
    row, col = square_iota(0), square_iota(1)
    same = same_head()
    step_row, step_col = step_of(row), step_of(col)
    earlier = jnp.where(same & (step_row < step_col), 1.0, 0.0)
    place = (col & (MB - 1)).astype(F32)
    within = jnp.where(
        same & (step_row == step_col) & ((row & (MB - 1)) <= (col & (MB - 1))),
        MB / (place + 1.0),
        0.0,
    )
    head_ref[...] = jnp.where(same, 1.0, 0.0)
    earlier_ref[...] = earlier
    output_ref[...] = earlier + within


def centred_columns(values):
    return values - sum_rows(values) / HD


def spread(pairs):
    return jnp.concatenate(
        [jnp.broadcast_to(pairs[h : h + 1], (HD, HD)) for h in range(2)], axis=0
    ).T


def forward_kernel(
    starts_ref,
    proj_ref,
    rate_ref,
    ttt_w_ref,
    ttt_b_ref,
    ttt_gain_ref,
    ttt_shift_ref,
    cot_ref,
    inner_ref,
    z_ref,
    g_ref,
    out_ref,
    target_ref,
    state_ref,
    mi_ref,
    mx_ref,
    mo_ref,
    w_ref,
    gain_ref,
    base_ref,
    offset_ref,
    cot_rows_ref,
    head_ref,
    earlier_ref,
    output_ref,
    c_ref,
    shift_ref,
    *gather_sems,
):
    chunks = rate_ref.shape[0]
    gather = Gather(cot_ref, cot_rows_ref, *gather_sems)
    gather.start()
    places = Places(starts_ref)
    inner_masks(head_ref, earlier_ref, output_ref)
    w_ref[...] = centred_columns(jnp.concatenate([ttt_w_ref[0], ttt_w_ref[1]], axis=0).T)
    c_ref[...] = centred_columns(spread(ttt_b_ref[...]))
    gain_ref[...] = spread(ttt_gain_ref[...])
    shift_ref[...] = spread(ttt_shift_ref[...])

    def columns(chunk, index):
        return proj_ref[chunk_rows(chunk), index * LANES : (index + 1) * LANES]

    def prepare(chunk):
        source = wrap(chunk, chunks)
        before = wrap(source - 1, chunks)
        keys = split_heads(columns(source, 1))
        values = split_heads(columns(source, 2))
        docs_row, docs_lane = places.row_documents(source), places.lane_documents(source)
        gram = dot_nt(keys, keys) + 1.0
        mi_ref[chunk] = masked(gram * earlier_ref[...], docs_row == docs_lane).astype(BF16)
        cross = dot_nt(split_heads(columns(before, 1)), keys) + 1.0
        mx_ref[chunk] = masked(
            cross * head_ref[...], places.row_documents(before) == docs_lane
        ).astype(BF16)
        pick = selector()
        target = dot_nt(pick, keys) - dot_nt(pick, values) + shift_ref[...]
        target_ref[chunk] = target
        offset_ref[slot(chunk)] = jnp.broadcast_to(
            sum_rows(target * gain_ref[...]) / HD, offset_ref.shape[1:]
        )

    def read_state(rows, source, weight, bias, entry):
        docs_row = places.row_documents(source)
        live_lane = places.lane_documents(source) == entry
        both = jnp.concatenate(
            [masked(rows, docs_row == entry), masked(rows, docs_row != entry)], axis=1
        )
        weights = jnp.concatenate([weight, w_ref[...]], axis=1).astype(BF16)
        return dot_nt(weights, both) + jnp.where(live_lane, bias, c_ref[...])

    def base(chunk, weight, bias, entry):
        source = wrap(chunk, chunks)
        base_ref[slot(chunk)] = read_state(split_heads(columns(source, 1)), source, weight, bias, entry)

    def chain(chunk, rated_before):
        gain = gain_ref[...]
        gain2 = gain * gain
        tied = target_ref[chunk] * gain
        tied_mean = offset_ref[slot(chunk)][0:1]
        rate = rate_ref[chunk]
        matrix = mi_ref[chunk]

        def gradient(z):
            zg = z * gain2
            s1, s2, s3, s4 = sum_rows(z * z), sum_rows(zg), sum_rows(z * zg), sum_rows(z * tied)
            rs = lax.rsqrt(s1 / HD + EPS)
            mean_g = rs * s2 / HD + tied_mean
            mean_gx = rs * (rs * s3 + s4) / HD
            return rs * (z * (rs * (gain2 - mean_gx)) + (tied - mean_g))

        first = base_ref[slot(chunk)] - dot_nn(rated_before, mx_ref[chunk])
        z = first
        g = gradient(z)
        for _ in range(STEPS - 1):
            z = first - dot_nn((g * rate).astype(BF16), matrix)
            g = gradient(z)
        z_ref[chunk] = z
        g_ref[chunk] = g
        return (g * rate).astype(BF16)

    def advance(chunk, weight, bias, rated):
        keys = split_heads(columns(chunk, 1))
        last = places.last(chunk)
        kept = places.row_documents(chunk) == last
        both = jnp.concatenate(
            [masked(keys, kept), masked(head_ref[...].astype(BF16), kept)], axis=1
        )
        step = dot_nn(rated, both)
        keep = places.keeps(chunk)
        start_w, start_c = w_ref[...], c_ref[...]
        return (
            start_w + keep * (weight - start_w) - step[:, :LANES],
            start_c + keep * (bias - start_c) - step[:, LANES:],
        )

    def finish(chunk, weight, bias, rated):
        keys = split_heads(columns(chunk, 1))
        query_rows = columns(chunk, 0)
        queries = split_heads(query_rows)
        same_doc = places.row_documents(chunk) == places.lane_documents(chunk)
        matrix = masked((dot_nt(keys, queries) + 1.0) * output_ref[...], same_doc).astype(BF16)
        mo_ref[chunk] = matrix
        out = read_state(queries, chunk, weight, bias, places.entry(chunk)) - dot_nn(rated, matrix)
        out_ref[chunk] = out
        rs = lax.rsqrt(sum_rows(out * out) / HD + EPS)
        fitted = out * rs * gain_ref[...] + shift_ref[...]
        inner_ref[chunk_rows(chunk), :] = (to_rows(fitted) + query_rows.astype(F32)).astype(BF16)

    prepare(0)
    base(0, w_ref[...], c_ref[...], places.entry(0))

    def body(chunk, carry):
        weight_before, bias_before, rated_before = carry
        for step, when in enumerate(FORWARD_STEPS):
            pl.when(chunk == when)(gather.steps[step])
        before = wrap(chunk - 1, chunks)
        weight, bias = advance(before, weight_before, bias_before, rated_before)
        state_ref[chunk] = weight
        rated = chain(chunk, rated_before)
        base(chunk + 1, weight, bias, places.entry(chunk))
        prepare(chunk + 1)
        finish(before, weight_before, bias_before, rated_before)
        return weight, bias, rated

    carry = (w_ref[...], c_ref[...], jnp.zeros((HD, LANES), BF16))
    weight, bias, rated = lax.fori_loop(0, chunks, body, carry)
    finish(chunks - 1, weight, bias, rated)
    gather.end()


FORWARD_STEPS = (5, 7, 12, 16, 20, 24, 30)
BACKWARD_STEPS = (5, 7, 10, 13, 17, 20, 24)
SUM_STEPS = (6, 11, 19, 26)


def backward_kernel(
    starts_ref,
    proj_ref,
    rate_ref,
    dinner_ref,
    dgate_ref,
    mixed_ref,
    grad_gu_ref,
    grad_down_ref,
    mix_ref,
    z_ref,
    g_ref,
    out_ref,
    target_ref,
    state_ref,
    mi_ref,
    mx_ref,
    mo_ref,
    w_ref,
    gain_ref,
    dproj_ref,
    dbias_ref,
    dw_ref,
    dc_ref,
    dgain_ref,
    dshift_ref,
    dout_ref,
    free_ref,
    base_ref,
    diag_ref,
    norm_ref,
    both_ref,
    wide_ref,
    coef_ref,
    y_ref,
    dz_ref,
    lam_ref,
    mixed_out,
    sum_gu_ref,
    sum_down_ref,
    mix_rows_ref,
    head_ref,
    earlier_ref,
    output_ref,
    send_sem,
    recv_sem,
    *sems,
):
    chunks = rate_ref.shape[0]
    gather = Gather(mix_ref, mix_rows_ref, *sems[2 * SEQ_SUM_SCRATCH :])
    sums = (
        SeqSum(0, grad_gu_ref, sum_gu_ref, *sems[:SEQ_SUM_SCRATCH]),
        SeqSum(1, grad_down_ref, sum_down_ref, *sems[SEQ_SUM_SCRATCH : 2 * SEQ_SUM_SCRATCH]),
    )
    exchange = ToHeads(
        [(dgate_ref, dproj_ref, 3 * LANES), (mixed_ref, mixed_out, 0)], send_sem, recv_sem
    )
    gather.start([{"head": peer} for peer in exchange.peers] + sums[0].peers())
    exchange.start()
    for total in sums:
        total.start()
    places = Places(starts_ref)
    inner_masks(head_ref, earlier_ref, output_ref)
    dbias_ref[...] = jnp.zeros_like(dbias_ref)
    dw_ref[...] = jnp.zeros_like(dw_ref)
    dc_ref[...] = jnp.zeros_like(dc_ref)
    dgain_ref[...] = jnp.zeros_like(dgain_ref)
    dshift_ref[...] = jnp.zeros_like(dshift_ref)

    def columns(chunk, index):
        return proj_ref[chunk_rows(chunk), index * LANES : (index + 1) * LANES]

    def prepare(chunk):
        gain = gain_ref[...]
        gain2 = gain * gain
        given = to_columns(dinner_ref[chunk_rows(chunk), :].astype(F32))
        out = out_ref[chunk]
        rs_out = lax.rsqrt(sum_rows(out * out) / HD + EPS)
        normal = out * rs_out
        scaled = given * gain
        dout = rs_out * (
            scaled - sum_rows(scaled) / HD - normal * (sum_rows(scaled * normal) / HD)
        )
        dgain_ref[...] += given * normal
        dshift_ref[...] += given
        rounded = dout.astype(BF16)
        dout_ref[slot(chunk)] = rounded
        free_ref[slot(chunk)] = dot_nt(rounded, mo_ref[chunk])
        z = z_ref[chunk]
        rs = lax.rsqrt(sum_rows(z * z) / HD + EPS)
        xh = z * rs
        xg = xh * gain2
        g = xg + target_ref[chunk] * gain
        mean_g = sum_rows(g) / HD
        mean_gx = sum_rows(g * xh) / HD
        mean_xg = sum_rows(xg) / HD
        diag_ref[slot(chunk)] = rs * (gain2 - mean_gx)
        norm_ref[slot(chunk)] = xh
        both_ref[slot(chunk)] = xg + g - mean_g - xh * mean_gx
        wide_ref[slot(chunk)] = xg + g
        coef_ref[slot(chunk)] = jnp.concatenate(
            [
                rs * rate_ref[chunk],
                rs,
                sum_rows(gain2) / HD + mean_gx,
                mean_xg + mean_g,
                mean_xg,
                sum_rows(xg * xh) / HD + 2.0 * mean_gx,
                jnp.zeros((2, LANES), F32),
            ],
            axis=0,
        )

    def chain(chunk, dz_after, cross):
        gain = gain_ref[...]
        gain2 = gain * gain
        diag, xh, both, wide = diag_ref[slot(chunk)], norm_ref[slot(chunk)], both_ref[slot(chunk)], wide_ref[slot(chunk)]
        coef = coef_ref[slot(chunk)]
        matrix = mi_ref[chunk]

        def pull(y):
            du = y * coef[0:1]
            a1 = sum_rows(du) / HD
            a2 = sum_rows(du * xh) / HD
            a3 = sum_rows(du * gain2) / HD - a1 * coef[2:3] - a2 * coef[3:4]
            a4 = sum_rows(du * both) / HD - a1 * coef[4:5] - a2 * coef[5:6]
            return diag * du - coef[1:2] * (gain2 * a1 + wide * a2 + a3 + xh * a4)

        first = -(base_ref[slot(chunk)] + dot_nt(dz_after, cross))
        y = first
        dz = pull(y)
        for _ in range(STEPS - 1):
            y = first - dot_nt(dz.astype(BF16), matrix)
            dz = pull(y)
        y_ref[slot(chunk)] = y
        rounded = dz.astype(BF16)
        dz_ref[slot(chunk)] = rounded
        return rounded

    def into_state(chunk, rows, values):
        docs_row, entry = places.row_documents(chunk), places.entry(chunk)
        live, dead = docs_row == entry, docs_row != entry
        heads = head_ref[...].astype(BF16)
        given = dot_nn(
            values,
            jnp.concatenate(
                [
                    masked(rows, live),
                    masked(heads, live),
                    masked(rows, dead),
                    masked(heads, dead),
                ],
                axis=1,
            ),
        )
        dw_ref[...] += given[:, 2 * LANES : 3 * LANES]
        dc_ref[...] += given[:, 3 * LANES :]
        return given[:, :LANES], given[:, LANES : 2 * LANES]

    def reach_back(source, lam_w, lam_c):
        kept_row = places.row_documents(source) == places.last(source)
        kept_lane = places.lane_documents(source) == places.last(source)
        keys = masked(split_heads(columns(source, 1)), kept_row)
        return dot_nt(lam_w.astype(BF16), keys) + jnp.where(kept_lane, lam_c, 0.0)

    def finish(chunk):
        gain = gain_ref[...]
        query_rows = split_heads(columns(chunk, 0))
        key_rows = split_heads(columns(chunk, 1))
        entry = places.entry(chunk)
        docs_row, docs_lane = places.row_documents(chunk), places.lane_documents(chunk)
        live, dead = docs_lane == entry, docs_lane != entry
        kept = docs_lane == places.last(chunk)
        same_doc = docs_row == docs_lane
        y = y_ref[slot(chunk)]
        g = g_ref[chunk]
        coef = coef_ref[slot(chunk)]
        dz = dz_ref[slot(chunk)]
        dout = dout_ref[slot(chunk)]
        xh = norm_ref[slot(chunk)]
        rate = rate_ref[chunk]
        logits = (sum_rows(g * y) * rate * (1.0 - HD * MB * rate)).astype(BF16)
        dbias_ref[...] += logits.astype(F32)
        rated = (g * rate).astype(BF16)
        du = y * coef[0:1]
        dg = du - sum_rows(du) / HD - xh * (sum_rows(du * xh) / HD)
        tied = dg * gain
        dgain_ref[...] += dg * (2.0 * gain * xh + target_ref[chunk])
        dshift_ref[...] += tied
        tied = tied.astype(BF16)
        earlier = earlier_ref[...]
        later = earlier_ref[...].T
        t_out = masked(dot_tn(rated, dout) * output_ref[...], same_doc).astype(BF16)
        t_in = masked(
            dot_tn(rated, dz) * earlier + dot_tn(dz, rated) * later, same_doc
        ).astype(BF16)
        states = jnp.concatenate([state_ref[chunk], w_ref[...]], axis=0).astype(BF16)
        dq = dot_tn(jnp.concatenate([masked(dout, live), masked(dout, dead)], axis=0), states)
        dq = dq - dot_tn(t_out, key_rows)
        sources = jnp.concatenate(
            [masked(dz, live), masked(dz, dead), masked(-rated, kept), tied], axis=0
        )
        pick = selector()
        dk = dot_tn(
            sources, jnp.concatenate([states, lam_ref[slot(chunk)].astype(BF16), pick], axis=0)
        )
        dk = dk - dot_nn(
            jnp.concatenate([t_out, t_in], axis=1),
            jnp.concatenate([query_rows, key_rows], axis=0),
        )
        dv = -dot_tn(tied, pick)
        rows = chunk_rows(chunk)
        dproj_ref[rows, 0:LANES] = (join_heads(dq) + dinner_ref[rows, :].astype(F32)).astype(BF16)
        dproj_ref[rows, LANES : 2 * LANES] = join_heads(dk).astype(BF16)
        dproj_ref[rows, 2 * LANES : 3 * LANES] = join_heads(dv).astype(BF16)
        diagonal = masked(
            jnp.broadcast_to(logits.astype(F32), (LANES, LANES)), square_iota(0) == square_iota(1)
        ).astype(BF16)
        head_column = (square_iota(1) == (square_iota(0) >> 6)).astype(F32).astype(BF16)
        spread = dot_nn(diagonal, head_column)
        dproj_ref[rows, 4 * LANES :] = (spread[:CHUNK] + spread[CHUNK:]).astype(BF16)

    last = chunks - 1
    prepare(last)
    base_ref[slot(last)] = free_ref[slot(last)]

    def body(index, carry):
        chunk = last - index
        lam_w, lam_c, dz_after = carry
        for step, when in enumerate(BACKWARD_STEPS):
            pl.when(index == when)(gather.steps[step])
        for step, when in enumerate(SUM_STEPS):
            for total in sums:
                pl.when(index == when)(total.steps[step])
        after = wrap(chunk + 1, chunks)
        cross = mx_ref[chunk + 1]
        dz = chain(chunk, dz_after, cross)
        add_w, add_c = into_state(after, split_heads(columns(after, 1)), dz_after)
        lam_w, lam_c = lam_w + add_w, lam_c + add_c
        lam_ref[slot(chunk)] = lam_w
        keep = places.keeps(chunk)
        dw_ref[...] += (1.0 - keep) * lam_w
        dc_ref[...] += (1.0 - keep) * lam_c
        add_w, add_c = into_state(chunk, split_heads(columns(chunk, 0)), dout_ref[slot(chunk)])
        lam_w, lam_c = keep * lam_w + add_w, keep * lam_c + add_c
        before = wrap(chunk - 1, chunks)

        @pl.when(chunk > 0)
        def _():
            prepare(before)
            base_ref[slot(before)] = free_ref[slot(before)] + reach_back(before, lam_w, lam_c)

        @pl.when(index > 0)
        def _():
            finish(after)

        return lam_w, lam_c, dz

    zero = jnp.zeros((HD, LANES), F32)
    lam_w, lam_c, dz = lax.fori_loop(
        0, chunks, body, (zero, zero, jnp.zeros((HD, LANES), BF16))
    )
    add_w, add_c = into_state(0, split_heads(columns(0, 1)), dz)
    dw_ref[...] += lam_w + add_w
    dc_ref[...] += lam_c + add_c
    finish(0)
    exchange.end()
    for total in sums:
        total.end()
    gather.end()


def whole_vmem(count):
    return [pl.BlockSpec(memory_space=pltpu.VMEM) for _ in range(count)]


def inner_forward(starts, proj, rates, ttt_w, ttt_b, gain, shift, own, number):
    tokens = proj.shape[0]
    chunks = tokens // CHUNK
    cell = jax.ShapeDtypeStruct((chunks, HD, LANES), F32)
    square = jax.ShapeDtypeStruct((HD, LANES), F32)
    return pl.pallas_call(
        forward_kernel,
        out_shape=[
            jax.ShapeDtypeStruct((tokens, LANES), BF16),
            cell,
            cell,
            cell,
            jax.ShapeDtypeStruct((chunks + 1, HD, LANES), F32),
            cell,
            jax.ShapeDtypeStruct((chunks + 1, LANES, LANES), BF16),
            jax.ShapeDtypeStruct((chunks + 1, LANES, LANES), BF16),
            jax.ShapeDtypeStruct((chunks, LANES, LANES), BF16),
            square,
            square,
            jax.ShapeDtypeStruct((RING, HD, LANES), F32),
            jax.ShapeDtypeStruct((RING, 8, LANES), F32),
            gathered_shape(own),
        ],
        in_specs=[pl.BlockSpec(memory_space=pltpu.SMEM)] + whole_vmem(6) + [ANYWHERE],
        out_specs=whole_vmem(13) + [ANYWHERE],
        scratch_shapes=[
            pltpu.VMEM((LANES, LANES), F32),
            pltpu.VMEM((LANES, LANES), F32),
            pltpu.VMEM((LANES, LANES), F32),
            pltpu.VMEM((HD, LANES), F32),
            pltpu.VMEM((HD, LANES), F32),
        ]
        + gather_scratch(),
        compiler_params=pltpu.CompilerParams(
            collective_id=number, has_side_effects=True, vmem_limit_bytes=MOST_VMEM
        ),
        name="inner_forward",
    )(starts, proj, rates, ttt_w, ttt_b, gain, shift, own)


def inner_backward(starts, proj, rates, d_inner, d_gate, mixed, grads, own, kept, number):
    tokens = proj.shape[0]
    chunks = tokens // CHUNK
    square = jax.ShapeDtypeStruct((HD, LANES), F32)
    cell = jax.ShapeDtypeStruct((RING, HD, LANES), F32)
    cell16 = jax.ShapeDtypeStruct((RING, HD, LANES), BF16)
    return pl.pallas_call(
        backward_kernel,
        out_shape=[
            jax.ShapeDtypeStruct((tokens, 5 * LANES), BF16),
            jax.ShapeDtypeStruct((1, LANES), F32),
            square,
            square,
            square,
            square,
            cell16,
            cell,
            cell,
            cell,
            cell,
            cell,
            cell,
            jax.ShapeDtypeStruct((RING, 8, LANES), F32),
            cell,
            cell16,
            cell,
            jax.ShapeDtypeStruct((tokens, LANES), BF16),
            *(jax.ShapeDtypeStruct(grad.shape, BF16) for grad in grads),
            gathered_shape(own),
        ],
        in_specs=[pl.BlockSpec(memory_space=pltpu.SMEM)]
        + whole_vmem(7)
        + [ANYWHERE]
        + whole_vmem(len(kept)),
        out_specs=whole_vmem(20) + [ANYWHERE],
        scratch_shapes=[
            pltpu.VMEM((LANES, LANES), F32),
            pltpu.VMEM((LANES, LANES), F32),
            pltpu.VMEM((LANES, LANES), F32),
        ]
        + to_heads_scratch(2)
        + seq_sum_scratch(grads[0].shape, 0)
        + seq_sum_scratch(grads[1].shape, 1)
        + gather_scratch(),
        compiler_params=pltpu.CompilerParams(
            collective_id=number, has_side_effects=True, vmem_limit_bytes=MOST_VMEM
        ),
        name="inner_backward",
    )(starts, proj, rates, d_inner, d_gate, mixed, *grads, own, *kept)


def heads_of_lanes(values):
    return jnp.sum(values.reshape(HD, 2, HD), axis=2).T


def project_kernel(x_ref, w_ref, rate_w_ref, bias_ref, proj_ref, rate_ref):
    x = x_ref[...]
    proj_ref[...] = dot_nn(x, w_ref[...]).astype(BF16)
    logits = dot_nt(rate_w_ref[...], x)
    for index in range(rate_ref.shape[0]):
        tokens = slice(index * CHUNK, (index + 1) * CHUNK)
        lanes = jnp.concatenate([logits[0:1, tokens], logits[1:2, tokens]], axis=1)
        rate_ref[index] = jax.nn.sigmoid(lanes + bias_ref[...]) / (HD * MB)


def project(gathered, w_in, w_rate, rate_bias):
    tokens, width = gathered.shape
    columns = w_in.shape[1]
    block = 4 * CHUNK
    rate_w = jnp.pad(w_rate.T, ((0, 14), (0, 0)))
    bias = jnp.repeat(rate_bias, HD)[None]
    return pl.pallas_call(
        project_kernel,
        grid=(tokens // block,),
        out_shape=[
            jax.ShapeDtypeStruct((tokens, columns), BF16),
            jax.ShapeDtypeStruct((tokens // CHUNK, 1, LANES), F32),
        ],
        in_specs=[
            pl.BlockSpec((block, width), lambda i: (i, 0)),
            pl.BlockSpec((width, columns), lambda i: (0, 0)),
            pl.BlockSpec((16, width), lambda i: (0, 0)),
            pl.BlockSpec((1, LANES), lambda i: (0, 0)),
        ],
        out_specs=[
            pl.BlockSpec((block, columns), lambda i: (i, 0)),
            pl.BlockSpec((block // CHUNK, 1, LANES), lambda i: (i, 0, 0)),
        ],
        compiler_params=pltpu.CompilerParams(vmem_limit_bytes=MOST_VMEM),
        name="project",
    )(gathered, w_in, rate_w, bias)


def mean_columns(values):
    return jnp.mean(values, axis=1, keepdims=True)


GELU_RATE = 0.7978845608028654
GELU_CUBE = 0.044715


def gelu_parts(x):
    square = x * x
    tanh = jnp.tanh(GELU_RATE * x * (1.0 + GELU_CUBE * square))
    half = 0.5 * (1.0 + tanh)
    slope = half + 0.5 * x * (1.0 - tanh * tanh) * GELU_RATE * (1.0 + 3.0 * GELU_CUBE * square)
    return x * half, slope


def line_of(gains_ref, index):
    return jnp.concatenate(
        [gains_ref[k, index : index + 1, :] for k in range(gains_ref.shape[0])], axis=1
    )


def post_norm_of(inner_ref):
    inner = inner_ref[...].astype(F32)
    centred = inner - mean_columns(inner)
    rstd = lax.rsqrt(mean_columns(centred * centred) + EPS)
    return centred * rstd, rstd


def middle_forward_kernel(
    inner_ref, gate_ref, gains_ref, tokens_ref, ffn_gain_ref, w_ref, mixed_ref, hidden_ref, norm_ref
):
    xp, _ = post_norm_of(inner_ref)
    post = xp * line_of(gains_ref, 0) + line_of(gains_ref, 1)
    act, _ = gelu_parts(gate_ref[...].astype(F32))
    mixed = (post * act).astype(BF16)
    mixed_ref[...] = mixed
    pieces, _, piece = w_ref.shape
    for k in range(pieces):
        columns = slice(k * piece, (k + 1) * piece)
        hidden_ref[:, columns] = tokens_ref[:, columns].astype(F32) + dot_nn(mixed, w_ref[k])
    hidden = hidden_ref[...]
    scale = lax.rsqrt(mean_columns(hidden * hidden) + EPS)
    norm_ref[...] = (hidden * scale * ffn_gain_ref[...]).astype(BF16)


def middle_forward(inner, gate, gains, tokens, ffn_gain, w_out):
    shape = tokens.shape
    return pl.pallas_call(
        middle_forward_kernel,
        out_shape=[
            jax.ShapeDtypeStruct(shape, BF16),
            jax.ShapeDtypeStruct(shape, F32),
            jax.ShapeDtypeStruct(shape, BF16),
        ],
        in_specs=whole_vmem(6),
        out_specs=whole_vmem(3),
        compiler_params=pltpu.CompilerParams(vmem_limit_bytes=24 * 1024 * 1024),
        name="middle_forward",
    )(inner, gate, gains, tokens, ffn_gain, w_out)


def middle_backward_kernel(
    d_norm_ref,
    hidden_ref,
    cot_ref,
    ffn_gain_ref,
    inner_ref,
    gate_ref,
    gains_ref,
    w_ref,
    d_res_ref,
    d_mix_ref,
    d_inner_ref,
    d_gate_ref,
    sums_ref,
):
    hidden = hidden_ref[...]
    scale = lax.rsqrt(mean_columns(hidden * hidden) + EPS)
    d_norm = d_norm_ref[...]
    weighted = d_norm * ffn_gain_ref[...]
    normed = hidden * scale
    d_res = cot_ref[...].astype(F32) + scale * (
        weighted - normed * mean_columns(weighted * normed)
    )
    d_res_ref[...] = d_res
    d_mix_ref[...] = d_res.astype(BF16)
    pieces, _, piece = w_ref.shape
    d_mixed = dot_nt(d_mix_ref[:, 0:piece], w_ref[0])
    for k in range(1, pieces):
        d_mixed = d_mixed + dot_nt(d_mix_ref[:, k * piece : (k + 1) * piece], w_ref[k])
    xp, rstd = post_norm_of(inner_ref)
    post_gain = line_of(gains_ref, 0)
    post = xp * post_gain + line_of(gains_ref, 1)
    act, slope = gelu_parts(gate_ref[...].astype(F32))
    d_post = d_mixed * act
    d_gate_ref[...] = (d_mixed * post * slope).astype(BF16)
    dx = d_post * post_gain
    d_inner = rstd * (dx - mean_columns(dx) - xp * mean_columns(dx * xp))
    d_inner_ref[...] = d_inner.astype(BF16)
    lines = (sum_rows(d_post * xp), sum_rows(d_post), sum_rows(d_norm * normed))
    for k in range(sums_ref.shape[0]):
        columns = slice(k * LANES, (k + 1) * LANES)
        sums_ref[k] = jnp.concatenate(
            [line[:, columns] for line in lines] + [jnp.zeros((5, LANES), F32)], axis=0
        )


def middle_backward(d_norm, hidden, cotangent, ffn_gain, inner, gate, gains, w_out):
    shape = cotangent.shape
    return pl.pallas_call(
        middle_backward_kernel,
        out_shape=[
            jax.ShapeDtypeStruct(shape, F32),
            jax.ShapeDtypeStruct(shape, BF16),
            jax.ShapeDtypeStruct(shape, BF16),
            jax.ShapeDtypeStruct(shape, BF16),
            jax.ShapeDtypeStruct(gains.shape, F32),
        ],
        in_specs=whole_vmem(8),
        out_specs=whole_vmem(5),
        compiler_params=pltpu.CompilerParams(vmem_limit_bytes=32 * 1024 * 1024),
        name="middle_backward",
    )(d_norm, hidden, cotangent, ffn_gain, inner, gate, gains, w_out)


RING_X = 4
RING_Y = 4
GROUP = RING_X * RING_Y
UNITS = 4
MESH = pl.DeviceIdType.MESH


def place_at(head, dx, dy):
    return lax.rem(head // RING_Y + dx + RING_X, RING_X) * RING_Y + lax.rem(
        lax.rem(head, RING_Y) + dy + RING_Y, RING_Y
    )


def neighbours(head):
    return {
        (axis, way): place_at(head, way if axis == 0 else 0, way if axis == 1 else 0)
        for axis in (0, 1)
        for way in (1, -1)
    }


def greet(peers):
    barrier = pltpu.get_barrier_semaphore()
    for peer in peers:
        pl.semaphore_signal(barrier, inc=1, device_id=peer, device_id_type=MESH)
    pl.semaphore_wait(barrier, len(peers))


def moved(place, axis, way):
    shift = (way, 0) if axis == 0 else (0, way)
    return tuple((p - s) % n for p, s, n in zip(place, shift, (RING_X, RING_Y)))


class Gather:
    def __init__(self, own_ref, full_ref, send_sem, recv_sem, local_sem):
        self.own_ref, self.full_ref = own_ref, full_ref
        self.send_sem, self.recv_sem, self.local_sem = send_sem, recv_sem, local_sem
        self.head = lax.axis_index("head")
        self.near = neighbours(self.head)
        self.rows = own_ref.shape[0]
        self.unit_rows = self.rows // UNITS
        self.count = 0
        self.halves = ((0, (0, 1)), (1, (2, 3)))
        self.steps = [
            partial(self.first_arrivals, 0),
            partial(self.first_arrivals, 1),
            partial(self.second_hops, (0,)),
            self.far_arrivals,
            partial(self.second_hops, (1,)),
            partial(self.second_hops, (3,)),
            partial(self.second_hops, (2,)),
        ]

    def slab(self, place, unit):
        start = place_at(self.head, *place) * self.rows + unit * self.unit_rows
        return self.full_ref.at[pl.ds(pl.multiple_of(start, self.unit_rows), self.unit_rows)]

    def arrival(self, place, unit):
        return self.recv_sem.at[(place[0] * RING_Y + place[1]) * UNITS + unit]

    def send(self, place, unit, axis, way):
        source = (
            self.own_ref.at[pl.ds(unit * self.unit_rows, self.unit_rows)]
            if place == (0, 0)
            else self.slab(place, unit)
        )
        pltpu.make_async_remote_copy(
            src_ref=source,
            dst_ref=self.slab(place, unit),
            send_sem=self.send_sem.at[self.count],
            recv_sem=self.arrival(moved(place, axis, way), unit),
            device_id={"head": self.near[axis, way]},
            device_id_type=MESH,
        ).start()
        self.count += 1

    def waiter(self, place, unit, send_number=0):
        return pltpu.make_async_remote_copy(
            src_ref=self.slab(place, unit),
            dst_ref=self.slab(place, unit),
            send_sem=self.send_sem.at[send_number],
            recv_sem=self.arrival(place, unit),
            device_id={"head": self.near[0, 1]},
            device_id_type=MESH,
        )

    def arrive(self, place, unit):
        self.waiter(place, unit).wait_recv()

    def own_copy(self):
        start = pl.multiple_of(self.head * self.rows, self.rows)
        return pltpu.make_async_copy(
            self.own_ref, self.full_ref.at[pl.ds(start, self.rows)], self.local_sem
        )

    def cross(self, axis, first, second):
        first, second = first % RING_X, second % RING_X
        return (first, second) if axis == 0 else (second, first)

    def start(self, greeted=None):
        greet(greeted or [{"head": peer} for peer in self.near.values()])
        self.own_copy().start()
        for turned in (False, True):
            for axis, units in self.halves:
                for unit in units:
                    for way in (1, -1):
                        self.send((0, 0), unit, 1 - axis if turned else axis, way)

    def first_arrivals(self, step):
        for axis, units in self.halves:
            for way in (1, -1):
                place = self.cross(axis, -way, 0)
                unit = units[0 if (way == 1) == (step == 0) else 1]
                self.arrive(place, unit)
                if step == 0:
                    self.send(place, unit, axis, way)
                for turn in (1, -1):
                    self.send(place, unit, 1 - axis, turn)

    def second_hops(self, firsts):
        for first in firsts:
            for axis, units in self.halves:
                for way in (1, -1):
                    unit = units[0 if way == 1 else 1]
                    place = self.cross(axis, first, -way)
                    self.arrive(place, unit)
                    self.send(place, unit, 1 - axis, way)

    def far_arrivals(self):
        for way in (1, -1):
            for axis, units in self.halves:
                unit = units[0 if way == 1 else 1]
                place = self.cross(axis, 2, 0)
                self.arrive(place, unit)
                for turn in (1, -1):
                    self.send(place, unit, 1 - axis, turn)

    def end(self):
        for first in range(RING_X):
            for axis, units in self.halves:
                for way in (1, -1):
                    self.arrive(self.cross(axis, first, -way), units[1 if way == 1 else 0])
        for first in range(RING_X):
            for axis, units in self.halves:
                for unit in units:
                    self.arrive(self.cross(axis, first, 2), unit)
        for number in range(TRANSFERS):
            self.waiter((0, 0), 0, number).wait_send()
        self.own_copy().wait()


TRANSFERS = UNITS * (GROUP - 1)
STAGED = 32
ANYWHERE = pl.BlockSpec(memory_space=pl.ANY)


def gather_kernel(*refs):
    gather = Gather(*refs)
    gather.start()
    for step in gather.steps:
        step()
    gather.end()


def gather_scratch():
    return [
        pltpu.SemaphoreType.DMA((TRANSFERS,)),
        pltpu.SemaphoreType.DMA((UNITS * GROUP,)),
        pltpu.SemaphoreType.DMA,
    ]


def gathered_shape(own):
    return jax.ShapeDtypeStruct((own.shape[0] * GROUP, own.shape[1]), own.dtype)


def gather_rows(own, number):
    return pl.pallas_call(
        gather_kernel,
        out_shape=gathered_shape(own),
        in_specs=[ANYWHERE],
        out_specs=ANYWHERE,
        scratch_shapes=gather_scratch(),
        compiler_params=pltpu.CompilerParams(collective_id=number, has_side_effects=True),
        name="gather_rows",
    )(own)


class SeqSum:
    SENDS = 24

    def __init__(
        self, axis, part_ref, sum_ref, pair_held, ring_held, stage_ref, send_sem, recv_sem
    ):
        self.axis = axis
        self.part_ref, self.sum_ref = part_ref, sum_ref
        self.pair_held, self.ring_held, self.stage_ref = pair_held, ring_held, stage_ref
        self.send_sem, self.recv_sem = send_sem, recv_sem
        seq = lax.axis_index("seq")
        self.chips = lax.axis_size("seq") // 2
        self.z, self.core = seq // 2, lax.rem(seq, 2)
        self.quarter = part_ref.shape[axis] // (2 * self.chips)
        self.unit = self.quarter // 2
        self.sibling = self.z * 2 + 1 - self.core
        self.near = {
            way: lax.rem(self.z + way + self.chips, self.chips) * 2 + self.core for way in (1, -1)
        }
        self.sends = []
        self.steps = [self.pair_arrivals, self.far_arrivals, self.own_sum, self.ring_arrivals]

    def peers(self):
        return [{"seq": peer} for peer in (self.sibling, self.near[1], self.near[-1])]

    def cut(self, ref, start, size):
        if not isinstance(start, int):
            start = pl.multiple_of(start, size)
        return ref.at[pl.ds(start, size)] if self.axis == 0 else ref.at[:, pl.ds(start, size)]

    def part(self, ref, core, dz, unit=None):
        owner = lax.rem(self.z + dz + self.chips, self.chips)
        start = (core * self.chips + owner) * self.quarter
        if unit is None:
            return self.cut(ref, start, self.quarter)
        return self.cut(ref, start + unit * self.unit, self.unit)

    def paired(self, dz):
        return self.cut(self.pair_held, dz * self.quarter, self.quarter)

    def staged(self, dz, unit=None):
        if unit is None:
            return self.cut(self.stage_ref, dz * self.quarter, self.quarter)
        return self.cut(self.stage_ref, dz * self.quarter + unit * self.unit, self.unit)

    def held(self, number):
        return self.cut(self.ring_held, number * self.unit, self.unit)

    def send(self, source, target, peer):
        number = len(self.sends)

        def copy():
            return pltpu.make_async_remote_copy(
                src_ref=source(),
                dst_ref=target(),
                send_sem=self.send_sem.at[number],
                recv_sem=self.recv_sem.at[number],
                device_id={"seq": peer},
                device_id_type=MESH,
            )

        copy().start()
        self.sends.append(copy)
        return number

    def arrive(self, number):
        self.sends[number]().wait_recv()

    def start(self):
        self.pair = {}
        for dz in (2, 1, 3, 0):
            self.pair[dz] = self.send(
                partial(self.part, self.part_ref, 1 - self.core, dz),
                partial(self.paired, dz),
                self.sibling,
            )

    def pair_arrivals(self):
        for dz in (2, 1, 3, 0):
            self.arrive(self.pair[dz])
            total = self.part(self.part_ref, self.core, dz)[...].astype(F32)
            total = total + self.paired(dz)[...].astype(F32)
            self.staged(dz)[...] = total.astype(BF16)
            if dz == 2:
                self.far = {
                    way: self.send(
                        partial(self.staged, 2, unit), partial(self.held, unit), self.near[way]
                    )
                    for way, unit in ((1, 0), (-1, 1))
                }
        self.plain = {
            way: self.send(
                partial(self.staged, way % 4, unit), partial(self.held, 2 + unit), self.near[way]
            )
            for way, unit in ((1, 1), (-1, 0))
        }

    def far_arrivals(self):
        self.onward = {}
        for way, unit in ((1, 0), (-1, 1)):
            self.arrive(self.far[way])
            place = self.staged(way % 4, unit)
            total = place[...].astype(F32) + self.held(unit)[...].astype(F32)
            place[...] = total.astype(BF16)
            self.onward[way] = self.send(
                partial(self.staged, way % 4, unit), partial(self.held, 4 + unit), self.near[way]
            )

    def own_sum(self):
        for way in (1, -1):
            self.arrive(self.plain[way])
            self.arrive(self.onward[way])
        self.direct = {}
        for unit in (0, 1):
            total = self.staged(0, unit)[...].astype(F32)
            total = total + self.held(2 + unit)[...].astype(F32)
            total = total + self.held(4 + unit)[...].astype(F32)
            place = self.part(self.sum_ref, self.core, 0, unit)
            place[...] = total.astype(BF16)
        for unit in (0, 1):
            place = partial(self.part, self.sum_ref, self.core, 0, unit)
            for way in (1, -1):
                self.direct[way, unit] = self.send(place, place, self.near[way])
        self.relayed = [self.relay(0, unit) for unit in (0, 1)]

    def relay(self, dz, unit):
        place = partial(self.part, self.sum_ref, self.core, dz, unit)
        return self.send(place, place, self.sibling)

    def ring_arrivals(self):
        self.passed = {}
        for unit in (0, 1):
            for way in (1, -1):
                self.arrive(self.direct[way, unit])
                if unit == (0 if way == 1 else 1):
                    place = partial(self.part, self.sum_ref, self.core, -way, unit)
                    self.passed[way] = self.send(place, place, self.near[way])
        for unit in (0, 1):
            for way in (1, -1):
                self.relayed.append(self.relay(-way, unit))

    def end(self):
        for way, unit in ((1, 0), (-1, 1)):
            self.arrive(self.passed[way])
            self.relayed.append(self.relay(2, unit))
        for number in self.relayed:
            self.arrive(number)
        for copy in self.sends:
            copy().wait_send()


def seq_sum_scratch(shape, axis):
    def pieces(numerator, denominator):
        size = numerator * shape[axis] // denominator
        return pltpu.VMEM((size, shape[1]) if axis == 0 else (shape[0], size), BF16)

    return [
        pieces(1, 2),
        pieces(6, 16),
        pieces(1, 2),
        pltpu.SemaphoreType.DMA((SeqSum.SENDS,)),
        pltpu.SemaphoreType.DMA((SeqSum.SENDS,)),
    ]


SEQ_SUM_SCRATCH = 5


class SmallSums:
    def __init__(
        self, sums, shard_ref, shard_out, lines_out, held, send_sem, recv_sem, *line_sems
    ):
        self.sums = sums
        self.shard_ref, self.shard_out, self.lines_out = shard_ref, shard_out, lines_out
        self.held, self.send_sem, self.recv_sem = held, send_sem, recv_sem
        self.line_send, self.line_recv = line_sems
        head, seq = lax.axis_index("head"), lax.axis_index("seq")
        self.head = head
        self.seqs = held.shape[0]
        self.seq_peers = [lax.rem(seq + ahead, self.seqs) for ahead in range(1, self.seqs)]
        self.head_peers = [lax.rem(head + ahead, GROUP) for ahead in range(1, GROUP)]

    def peers(self):
        return [{"seq": peer} for peer in self.seq_peers] + [
            {"head": peer} for peer in self.head_peers
        ]

    def step(self, index):
        for total in self.sums:
            total.steps[index]()

    def start(self):
        for total in self.sums:
            total.start()
        self.sends = []
        for ahead, peer in enumerate(self.seq_peers, 1):
            done = pltpu.make_async_remote_copy(
                src_ref=self.shard_ref,
                dst_ref=self.held.at[ahead],
                send_sem=self.send_sem.at[ahead],
                recv_sem=self.recv_sem.at[ahead],
                device_id={"seq": peer},
                device_id_type=MESH,
            )
            done.start()
            self.sends.append(done)

    def turn(self):
        for done in self.sends:
            done.wait_recv()
        shard = self.shard_ref[...]
        for ahead in range(1, self.seqs):
            shard = shard + self.held[ahead]
        self.shard_out[...] = shard
        self.lines_out[self.head] = shard[0:8]
        self.passed = []
        for ahead, peer in enumerate(self.head_peers, 1):
            done = pltpu.make_async_remote_copy(
                src_ref=self.shard_out.at[0:8],
                dst_ref=self.lines_out.at[self.head],
                send_sem=self.line_send.at[ahead],
                recv_sem=self.line_recv.at[ahead],
                device_id={"head": peer},
                device_id_type=MESH,
            )
            done.start()
            self.passed.append(done)

    def end(self):
        for total in self.sums:
            total.end()
        for done in self.passed:
            done.wait_recv()
        for done in self.sends + self.passed:
            done.wait_send()


class Everywhere:
    def __init__(self, part_ref, sum_ref, seq_held, line_ref, head_held, *sems):
        self.part_ref, self.sum_ref = part_ref, sum_ref
        self.seq_held, self.line_ref, self.head_held = seq_held, line_ref, head_held
        self.sems = sems

    def push(self, source, held, axis, send_sem, recv_sem):
        count, me = held.shape[0], lax.axis_index(axis)
        sends = []
        for ahead in range(1, count):
            done = pltpu.make_async_remote_copy(
                src_ref=source,
                dst_ref=held.at[ahead],
                send_sem=send_sem.at[ahead],
                recv_sem=recv_sem.at[ahead],
                device_id={axis: lax.rem(me + ahead, count)},
                device_id_type=MESH,
            )
            done.start()
            sends.append(done)
        return sends

    def total(self, source, held, sends):
        total = source[...]
        for ahead, done in enumerate(sends, 1):
            done.wait_recv()
            total = total + held[ahead]
        return total

    def start(self):
        self.over_seq = self.push(self.part_ref, self.seq_held, "seq", *self.sems[:2])

    def turn(self):
        self.line_ref[...] = self.total(self.part_ref, self.seq_held, self.over_seq)
        self.over_head = self.push(self.line_ref, self.head_held, "head", *self.sems[2:])

    def end(self):
        self.sum_ref[...] = self.total(self.line_ref, self.head_held, self.over_head)
        for done in self.over_seq + self.over_head:
            done.wait_send()


def everywhere_scratch(shape, seqs):
    return [
        pltpu.VMEM((seqs,) + shape, F32),
        pltpu.VMEM(shape, F32),
        pltpu.VMEM((GROUP,) + shape, F32),
        pltpu.SemaphoreType.DMA((seqs,)),
        pltpu.SemaphoreType.DMA((seqs,)),
        pltpu.SemaphoreType.DMA((GROUP,)),
        pltpu.SemaphoreType.DMA((GROUP,)),
    ]


EVERYWHERE_SCRATCH = 7


def scatter_kernel(part_ref, sum_ref, held_ref, stage_ref, send_sem, recv_sem):
    scatter_body(None, part_ref, sum_ref, held_ref, stage_ref, send_sem, recv_sem)


def scatter_small_kernel(
    part_ref,
    shard_ref,
    grad_in_ref,
    grad_out_ref,
    tokens_ref,
    d_res_ref,
    gain_ref,
    grad_tokens_ref,
    gain_sum_ref,
    shard_out,
    lines_out,
    sum_in_ref,
    sum_out_ref,
    held_ref,
    stage_ref,
    send_sem,
    recv_sem,
    sum_ref,
    gain_part_ref,
    *scratch,
):
    count = 2 * SEQ_SUM_SCRATCH
    sums = (
        SeqSum(0, grad_in_ref, sum_in_ref, *scratch[:SEQ_SUM_SCRATCH]),
        SeqSum(1, grad_out_ref, sum_out_ref, *scratch[SEQ_SUM_SCRATCH:count]),
    )
    more = count + EVERYWHERE_SCRATCH
    gain_sum = Everywhere(gain_part_ref, gain_sum_ref, *scratch[count:more])
    small = SmallSums(sums, shard_ref, shard_out, lines_out, *scratch[more:])
    scatter_body(small, part_ref, sum_ref, held_ref, stage_ref, send_sem, recv_sem)
    resid = tokens_ref[...].astype(F32)
    scale = lax.rsqrt(mean_columns(resid * resid) + EPS)
    normed = resid * scale
    d_norm = sum_ref[...]
    line = sum_rows(d_norm * normed)
    for k in range(GROUP):
        gain_part_ref[k : k + 1, :] = line[:, k * LANES : (k + 1) * LANES]
    gain_sum.start()
    weighted = d_norm * gain_ref[...]
    grad_tokens_ref[...] = d_res_ref[...] + scale * (
        weighted - normed * mean_columns(weighted * normed)
    )
    gain_sum.turn()
    small.end()
    gain_sum.end()


def scatter_body(small, part_ref, sum_ref, held_ref, stage_ref, send_sem, recv_sem):
    head = lax.axis_index("head")
    near = neighbours(head)
    rows = sum_ref.shape[0]
    unit_rows = rows // UNITS
    peers = [{"head": peer} for peer in near.values()]
    greet(peers if small is None else small.peers())
    sends, blocks, staged = [], [], {}

    def slab(place, unit):
        start = place_at(head, *place) * rows + unit * unit_rows
        return part_ref.at[pl.ds(pl.multiple_of(start, unit_rows), unit_rows)]

    def held(index):
        return pl.ds(index * unit_rows, unit_rows)

    def stage(place, unit, total):
        block = stage_ref.at[held(len(blocks))]
        block[...] = total.astype(BF16)
        blocks.append(block)
        staged[place, unit] = block

    def send(place, unit, axis, way):
        index = len(sends)
        done = pltpu.make_async_remote_copy(
            src_ref=staged.get((place, unit), slab(place, unit)),
            dst_ref=held_ref.at[held(index)],
            send_sem=send_sem.at[index],
            recv_sem=recv_sem.at[index],
            device_id={"head": near[axis, way]},
            device_id_type=MESH,
        )
        done.start()
        sends.append(done)
        return index

    def arrived(index):
        sends[index].wait_recv()
        return held_ref[held(index)].astype(F32)

    def add_to(place, unit, *indices):
        total = staged.get((place, unit), slab(place, unit))[...].astype(F32)
        for index in indices:
            total = total + arrived(index)
        return total

    def cross(axis, first, second):
        first, second = first % RING_X, second % RING_X
        return (first, second) if axis == 0 else (second, first)

    halves = ((1, (0, 1)), (0, (2, 3)))

    def far(axis, units, other):
        return {
            way: send(cross(axis, 2, other), units[0 if way == 1 else 1], axis, way)
            for way in (1, -1)
        }

    def plain(axis, units, other):
        return {
            way: send(cross(axis, way, other), units[1 if way == 1 else 0], axis, way)
            for way in (1, -1)
        }

    def onward(axis, units, other, from_far):
        result = {}
        for way in (1, -1):
            place, unit = cross(axis, way, other), units[0 if way == 1 else 1]
            stage(place, unit, add_to(place, unit, from_far[way]))
            result[way] = send(place, unit, axis, way)
        return result

    def collect(axis, units, other, by_plain, by_onward):
        place = cross(axis, 0, other)
        return [
            add_to(place, units[0], by_onward[1], by_plain[-1]),
            add_to(place, units[1], by_onward[-1], by_plain[1]),
        ]

    order = (2, 1, 3, 0)
    fars = {(axis, o): far(axis, units, o) for o in order for axis, units in halves}
    plains = {(axis, o): plain(axis, units, o) for o in order for axis, units in halves}
    if small is not None:
        small.start()
        small.step(0)
    onwards = {
        (axis, o): onward(axis, units, o, fars[axis, o]) for o in order for axis, units in halves
    }
    if small is not None:
        small.step(1)
    last_far, last_plain, last_onward = {}, {}, {}

    def first_sum(axis, units, other):
        totals = collect(axis, units, other, plains[axis, other], onwards[axis, other])
        place = cross(axis, 0, other)
        for unit, total in zip(units, totals):
            stage(place, unit, total)

    for axis, units in halves:
        first_sum(axis, units, 2)
        last_far[axis] = far(1 - axis, units, 0)
    for axis, units in halves:
        first_sum(axis, units, 1)
        first_sum(axis, units, 3)
        last_plain[axis] = plain(1 - axis, units, 0)
    if small is not None:
        small.step(2)
    for axis, units in halves:
        last_onward[axis] = onward(1 - axis, units, 0, last_far[axis])
    if small is not None:
        small.step(3)
        small.turn()
    for axis, units in halves:
        own = collect(axis, units, 0, plains[axis, 0], onwards[axis, 0])
        extra = (
            (last_onward[axis][1], last_plain[axis][-1]),
            (last_onward[axis][-1], last_plain[axis][1]),
        )
        for unit, total, indices in zip(units, own, extra):
            for index in indices:
                total = total + arrived(index)
            sum_ref[pl.ds(unit * unit_rows, unit_rows), :] = total
    for done in sends:
        done.wait_send()


def scatter_scratch(rows, width):
    return [
        pltpu.VMEM((TRANSFERS * rows // UNITS, width), BF16),
        pltpu.VMEM((STAGED * rows // UNITS, width), BF16),
        pltpu.SemaphoreType.DMA((TRANSFERS,)),
        pltpu.SemaphoreType.DMA((TRANSFERS,)),
    ]


def scatter_rows(part, number):
    rows, width = part.shape[0] // GROUP, part.shape[1]
    return pl.pallas_call(
        scatter_kernel,
        out_shape=jax.ShapeDtypeStruct((rows, width), F32),
        in_specs=[pl.BlockSpec(memory_space=pltpu.VMEM)],
        out_specs=pl.BlockSpec(memory_space=pltpu.VMEM),
        scratch_shapes=scatter_scratch(rows, width),
        compiler_params=pltpu.CompilerParams(
            collective_id=number, has_side_effects=True, vmem_limit_bytes=28 * 1024 * 1024
        ),
        name="scatter_rows",
    )(part)


def scatter_rows_and_small(part, shard, grads, tokens, d_res, gain, seqs, number):
    rows, width = tokens.shape
    lines = (GROUP, width // GROUP)
    return pl.pallas_call(
        scatter_small_kernel,
        out_shape=[
            jax.ShapeDtypeStruct((rows, width), F32),
            jax.ShapeDtypeStruct(lines, F32),
            jax.ShapeDtypeStruct(shard.shape, F32),
            jax.ShapeDtypeStruct((GROUP, 8, LANES), F32),
            *(jax.ShapeDtypeStruct(grad.shape, BF16) for grad in grads),
        ],
        in_specs=whole_vmem(7),
        out_specs=whole_vmem(6),
        scratch_shapes=scatter_scratch(rows, width)
        + [pltpu.VMEM((rows, width), F32), pltpu.VMEM(lines, F32)]
        + seq_sum_scratch(grads[0].shape, 0)
        + seq_sum_scratch(grads[1].shape, 1)
        + everywhere_scratch(lines, seqs)
        + [
            pltpu.VMEM((seqs,) + shard.shape, F32),
            pltpu.SemaphoreType.DMA((seqs,)),
            pltpu.SemaphoreType.DMA((seqs,)),
            pltpu.SemaphoreType.DMA((GROUP,)),
            pltpu.SemaphoreType.DMA((GROUP,)),
        ],
        compiler_params=pltpu.CompilerParams(
            collective_id=number, has_side_effects=True, vmem_limit_bytes=48 * 1024 * 1024
        ),
        name="scatter_rows_and_small",
    )(part, shard, *grads, tokens, d_res, gain)


def to_tokens_kernel(
    inner_ref,
    gate_ref,
    gains_ref,
    inner_out,
    gate_out,
    gains_out,
    send_sem,
    recv_sem,
    local_sem,
):
    head = lax.axis_index("head")
    rows = inner_out.shape[0]
    first = gate_ref.shape[1] - LANES
    pairs = ((inner_ref, inner_out), (gate_ref.at[:, first:], gate_out))

    def rows_of(index):
        return pl.ds(pl.multiple_of(index * rows, rows), rows)

    def columns_of(index):
        return pl.ds(pl.multiple_of(index * LANES, LANES), LANES)

    mine = [
        pltpu.make_async_copy(
            source.at[rows_of(head)], target.at[:, columns_of(head)], local_sem.at[index]
        )
        for index, (source, target) in enumerate(pairs)
    ] + [pltpu.make_async_copy(gains_ref, gains_out.at[head], local_sem.at[2])]
    for done in mine:
        done.start()
    greet([{"head": lax.rem(head + ahead, GROUP)} for ahead in range(1, GROUP)])
    sends = []
    for ahead in range(1, GROUP):
        peer = lax.rem(head + ahead, GROUP)
        jobs = [
            (source.at[rows_of(peer)], target.at[:, columns_of(head)]) for source, target in pairs
        ] + [(gains_ref, gains_out.at[head])]
        for index, (source, target) in enumerate(jobs):
            done = pltpu.make_async_remote_copy(
                src_ref=source,
                dst_ref=target,
                send_sem=send_sem.at[ahead, index],
                recv_sem=recv_sem.at[ahead, index],
                device_id={"head": peer},
                device_id_type=MESH,
            )
            done.start()
            sends.append(done)
    for done in mine:
        done.wait()
    for done in sends:
        done.wait()


def to_tokens(inner, gate, gains, number):
    rows = inner.shape[0] // GROUP
    wide = jax.ShapeDtypeStruct((rows, GROUP * LANES), BF16)
    return pl.pallas_call(
        to_tokens_kernel,
        out_shape=[wide, wide, jax.ShapeDtypeStruct((GROUP,) + gains.shape, F32)],
        in_specs=whole_vmem(3),
        out_specs=whole_vmem(3),
        scratch_shapes=[
            pltpu.SemaphoreType.DMA((GROUP, 3)),
            pltpu.SemaphoreType.DMA((GROUP, 3)),
            pltpu.SemaphoreType.DMA((3,)),
        ],
        compiler_params=pltpu.CompilerParams(
            collective_id=number, has_side_effects=True, vmem_limit_bytes=8 * 1024 * 1024
        ),
        name="to_tokens",
    )(inner, gate, gains)


class ToHeads:
    def __init__(self, pairs, send_sem, recv_sem):
        self.pairs, self.send_sem, self.recv_sem = pairs, send_sem, recv_sem
        self.head = lax.axis_index("head")
        self.rows = pairs[0][0].shape[0]
        self.peers = [lax.rem(self.head + ahead, GROUP) for ahead in range(1, GROUP)]

    def rows_of(self, index):
        return pl.ds(pl.multiple_of(index * self.rows, self.rows), self.rows)

    def columns_of(self, index):
        return pl.ds(pl.multiple_of(index * LANES, LANES), LANES)

    def start(self):
        self.sends = []
        for ahead, peer in enumerate(self.peers, 1):
            for index, (source, target, first) in enumerate(self.pairs):
                done = pltpu.make_async_remote_copy(
                    src_ref=source.at[:, self.columns_of(peer)],
                    dst_ref=target.at[self.rows_of(self.head), first : first + LANES],
                    send_sem=self.send_sem.at[ahead, index],
                    recv_sem=self.recv_sem.at[ahead, index],
                    device_id={"head": peer},
                    device_id_type=MESH,
                )
                done.start()
                self.sends.append(done)
        for source, target, first in self.pairs:
            target[self.rows_of(self.head), first : first + LANES] = source[
                :, self.columns_of(self.head)
            ]

    def end(self):
        for done in self.sends:
            done.wait()


def to_heads_scratch(arrays):
    return [
        pltpu.SemaphoreType.DMA((GROUP, arrays)),
        pltpu.SemaphoreType.DMA((GROUP, arrays)),
    ]


def to_heads_kernel(inner_ref, sums_ref, inner_out, sums_out, send_sem, recv_sem, *sums_sems):
    exchange = ToHeads([(inner_ref, inner_out, 0)], send_sem, recv_sem)
    head = exchange.head
    greet([{"head": peer} for peer in exchange.peers])
    exchange.start()
    sends = []
    for ahead, peer in enumerate(exchange.peers, 1):
        done = pltpu.make_async_remote_copy(
            src_ref=sums_ref.at[peer],
            dst_ref=sums_out.at[head],
            send_sem=sums_sems[0].at[ahead],
            recv_sem=sums_sems[1].at[ahead],
            device_id={"head": peer},
            device_id_type=MESH,
        )
        done.start()
        sends.append(done)
    sums_out[head] = sums_ref[head]
    exchange.end()
    for done in sends:
        done.wait()


def to_heads(inner, sums, number):
    rows = inner.shape[0]
    return pl.pallas_call(
        to_heads_kernel,
        out_shape=[
            jax.ShapeDtypeStruct((rows * GROUP, LANES), BF16),
            jax.ShapeDtypeStruct(sums.shape, F32),
        ],
        in_specs=whole_vmem(2),
        out_specs=whole_vmem(2),
        scratch_shapes=to_heads_scratch(1)
        + [pltpu.SemaphoreType.DMA((GROUP,)), pltpu.SemaphoreType.DMA((GROUP,))],
        compiler_params=pltpu.CompilerParams(
            collective_id=number, has_side_effects=True, vmem_limit_bytes=8 * 1024 * 1024
        ),
        name="to_heads",
    )(inner, sums)


def after(value, *others):
    return lax.optimization_barrier((value,) + others)[0]


def per_device(
    tokens,
    doc_starts,
    norm_gain,
    w_in,
    w_rate,
    rate_bias,
    ttt_w,
    ttt_b,
    ttt_gain,
    ttt_shift,
    post_gain,
    post_bias,
    w_out,
    ffn_gain,
    w_gate_up,
    w_down,
    cotangent,
):
    seq = lax.axis_index("seq")
    seqs = lax.axis_size("seq")
    tok_rows, width = tokens.shape
    head_count, head_dim = ttt_b.shape
    local_width = head_count * head_dim
    ffn_local = w_down.shape[0]
    w_in_flat = w_in.reshape(width, 4 * local_width)
    w_gu_flat = w_gate_up.reshape(width, 2 * ffn_local)
    ffn_gain_line = ffn_gain[None]

    piece = width // seqs
    w_out_piece = lax.dynamic_slice_in_dim(w_out, seq * piece, piece, axis=1)
    w_out_all = lax.all_gather(w_out_piece, ("seq", "head"), axis=0, tiled=True)
    w_out_all = w_out_all.reshape(seqs, width, piece)

    resid = tokens.astype(F32)
    scale_one = lax.rsqrt(jnp.mean(resid * resid, axis=-1, keepdims=True) + EPS)
    norm_one = (resid * scale_one * norm_gain).astype(BF16)
    gathered = gather_rows(norm_one, 0)
    projected, rate_lanes = project(gathered, w_in_flat, w_rate, rate_bias)
    inner, *kept, _, _, cot_rows = inner_forward(
        doc_starts, projected, rate_lanes, ttt_w, ttt_b, ttt_gain, ttt_shift, cotangent, 7
    )

    gains = jnp.concatenate(
        [post_gain[None], post_bias[None], jnp.zeros((6, local_width), F32)], axis=0
    )
    inner_tok, gate_tok, all_gains = to_tokens(inner, projected, gains, 1)
    mixed_tok, hidden_res, norm_two = middle_forward(
        inner_tok, gate_tok, all_gains, tokens, ffn_gain_line, w_out_all
    )

    ffn_rows = gather_rows(norm_two, 2)
    gate_up = dot_nn(ffn_rows, w_gu_flat).astype(BF16)
    gate_part = gate_up[:, :ffn_local].astype(F32)
    up_part = gate_up[:, ffn_local:].astype(F32)
    silu_val, silu_pull = jax.vjp(jax.nn.silu, gate_part)
    hidden_state = (silu_val * up_part).astype(BF16)
    half = width // 2
    ffn_first = dot_nn(hidden_state, w_down[:, :half]).astype(BF16)
    out_first = lax.psum_scatter(ffn_first, "head", scatter_dimension=0, tiled=True)
    cot_rows = after(cot_rows, ffn_first)
    d_hidden = dot_nt(cot_rows, w_down)
    d_gate_part = silu_pull(d_hidden * up_part)[0]
    d_gate_up = jnp.concatenate([d_gate_part, d_hidden * silu_val], axis=1).astype(BF16)
    grad_w_down = dot_tn(hidden_state, cot_rows).astype(BF16)
    grad_w_down = jnp.pad(grad_w_down, ((0, -ffn_local % 16), (0, 0)))
    grad_w_gate_up = dot_tn(ffn_rows, d_gate_up).astype(BF16)
    d_norm_part = dot_nt(d_gate_up, w_gu_flat).astype(BF16)
    d_norm_two = scatter_rows(after(d_norm_part, grad_w_down, grad_w_gate_up), 3)

    d_res, d_mix, d_inner_tok, d_gate_tok, token_sums = middle_backward(
        d_norm_two,
        hidden_res,
        cotangent,
        ffn_gain_line,
        inner_tok,
        gate_tok,
        all_gains,
        w_out_all,
    )
    d_inner, head_sums = to_heads(d_inner_tok, token_sums, 4)
    head_sums = jnp.sum(head_sums, axis=0)

    (
        d_projected,
        d_bias,
        d_start_w,
        d_start_c,
        d_gain,
        d_shift,
        *_,
        mixed_in,
        sum_w_gate_up,
        sum_w_down,
        mix_rows,
    ) = inner_backward(
        doc_starts,
        projected,
        rate_lanes,
        after(d_inner, out_first),
        d_gate_tok,
        mixed_tok,
        (grad_w_gate_up, grad_w_down),
        d_mix,
        kept,
        8,
    )
    ffn_second = dot_nn(after(hidden_state, d_projected), w_down[:, half:]).astype(BF16)
    out_second = lax.psum_scatter(ffn_second, "head", scatter_dimension=0, tiled=True)
    ffn_out = jnp.concatenate([out_first, out_second], axis=1).astype(F32)
    output = (hidden_res + ffn_out).astype(BF16)
    grad_in = dot_tn(after(gathered, ffn_second), d_projected)
    w_columns = jnp.pad(w_rate, ((0, 0), (0, local_width - head_count)))
    w_columns = jnp.concatenate([w_in_flat, w_columns], axis=1)
    grad_w_rate = grad_in[:, 4 * local_width : 4 * local_width + head_count]
    grad_w_in = grad_in[:, : 4 * local_width].astype(BF16)
    grad_w_out = dot_tn(mixed_in, mix_rows).astype(BF16)
    singles = jnp.stack(
        [
            head_sums[2],
            head_sums[0],
            head_sums[1],
            d_start_c[:, ::head_dim].T.reshape(LANES),
            heads_of_lanes(d_gain).reshape(LANES),
            heads_of_lanes(d_shift).reshape(LANES),
            d_bias[0],
            jnp.zeros((LANES,), F32),
        ]
    )
    rate_rows = grad_w_rate.T.reshape(2 * width // LANES, LANES)
    shard = jnp.concatenate([singles, d_start_w, rate_rows], axis=0)
    d_norm_part = dot_nt(d_projected, w_columns).astype(BF16)
    grad_tokens, sum_norm_gain, shard, lines, sum_w_in, sum_w_out = scatter_rows_and_small(
        d_norm_part,
        shard,
        (grad_w_in, grad_w_out),
        tokens,
        d_res,
        norm_gain[None],
        seqs,
        5,
    )
    sum_ffn_gain = lines[:, 0].reshape(width)
    sum_ttt_w = shard[8 : 8 + head_dim].reshape(head_dim, head_count, head_dim)
    per_head = (head_count, head_dim)
    return (
        output,
        grad_tokens,
        sum_norm_gain.reshape(width),
        sum_w_in.astype(F32).reshape(width, 4, local_width),
        shard[8 + head_dim :].reshape(head_count, width).T,
        jnp.sum(shard[6].reshape(per_head), axis=1),
        sum_ttt_w.transpose(1, 2, 0),
        shard[3].reshape(per_head),
        shard[4].reshape(per_head),
        shard[5].reshape(per_head),
        shard[1],
        shard[2],
        sum_w_out.astype(F32),
        sum_ffn_gain,
        sum_w_gate_up.astype(F32).reshape(width, 2, ffn_local),
        sum_w_down[:ffn_local].astype(F32),
    )


def solution(mesh):
    return jax.shard_map(
        per_device,
        mesh=mesh,
        in_specs=(
            P(("seq", "head"), None),
            P("seq", None),
            P(),
            P(None, None, "head"),
            P(None, "head"),
            P("head"),
            P("head", None, None),
            P("head", None),
            P("head", None),
            P("head", None),
            P("head"),
            P("head"),
            P("head", None),
            P(),
            P(None, None, "head"),
            P("head", None),
            P(("seq", "head"), None),
        ),
        out_specs=(
            P(("seq", "head"), None),
            P(("seq", "head"), None),
            P(),
            P(None, None, "head"),
            P(None, "head"),
            P("head"),
            P("head", None, None),
            P("head", None),
            P("head", None),
            P("head", None),
            P("head"),
            P("head"),
            P("head", None),
            P(),
            P(None, None, "head"),
            P("head", None),
        ),
        check_vma=False,
    )
```

```python
from functools import partial

import jax
import jax.numpy as jnp
from jax import lax
from jax.experimental import pallas as pl
from jax.experimental.pallas import tpu as pltpu
from jax.sharding import PartitionSpec as P

MB = 16
EPS = 1e-06
HD = 64
STEPS = 4
CHUNK = STEPS * MB
LANES = 2 * CHUNK
BF16 = jnp.bfloat16
MOST_VMEM = 56 * 1024 * 1024
F32 = jnp.float32


def dot_nn(a, b):
    return lax.dot_general(a, b, (((1,), (0,)), ((), ())), preferred_element_type=F32)


def dot_nt(a, b):
    return lax.dot_general(a, b, (((1,), (1,)), ((), ())), preferred_element_type=F32)


def dot_tn(a, b):
    return lax.dot_general(a, b, (((0,), (0,)), ((), ())), preferred_element_type=F32)


def sum_rows(x):
    return jnp.sum(x, axis=0, keepdims=True)


def square_iota(dim):
    return lax.broadcasted_iota(jnp.int32, (LANES, LANES), dim)


def step_of(index):
    return (index >> 4) & (STEPS - 1)


class Places:
    def __init__(self, starts_ref):
        self.second = starts_ref[0, 1]
        self.third = starts_ref[0, 2]

    def document(self, step):
        return (step >= self.second).astype(jnp.int32) + (step >= self.third).astype(jnp.int32)

    def lane_documents(self, chunk):
        return self.document(chunk * STEPS + step_of(lax.broadcasted_iota(jnp.int32, (1, LANES), 1)))

    def row_documents(self, chunk):
        return self.document(chunk * STEPS + step_of(lax.broadcasted_iota(jnp.int32, (LANES, 1), 0)))

    def entry(self, chunk):
        return self.document(chunk * STEPS - 1)

    def last(self, chunk):
        return self.document(chunk * STEPS + STEPS - 1)

    def keeps(self, chunk):
        return (self.entry(chunk) == self.last(chunk)).astype(F32)


def split_heads(rows):
    first = lax.broadcasted_iota(jnp.int32, rows.shape, 1) < HD
    zero = jnp.zeros_like(rows)
    return jnp.concatenate([jnp.where(first, rows, zero), jnp.where(first, zero, rows)], axis=0)


def join_heads(square):
    first = lax.broadcasted_iota(jnp.int32, (CHUNK, LANES), 1) < HD
    return jnp.where(first, square[:CHUNK], square[CHUNK:])


def to_columns(rows):
    turned = split_heads(rows).T
    return turned[:HD] + turned[HD:]


def to_rows(columns):
    return join_heads(split_heads(columns).T)


def selector():
    row = lax.broadcasted_iota(jnp.int32, (HD, LANES), 0)
    col = lax.broadcasted_iota(jnp.int32, (HD, LANES), 1)
    return (row == (col & (HD - 1))).astype(F32).astype(BF16)


RING = 4


def slot(chunk):
    return lax.rem(chunk, RING)


def wrap(chunk, chunks):
    return lax.rem(chunk + chunks, chunks)


def chunk_rows(chunk):
    return pl.ds(pl.multiple_of(chunk * CHUNK, CHUNK), CHUNK)


def same_head():
    return (square_iota(0) >> 6) == (square_iota(1) >> 6)


def masked(values, keep):
    return jnp.where(keep, values, jnp.zeros_like(values))


def inner_masks(head_ref, earlier_ref, output_ref):
    row, col = square_iota(0), square_iota(1)
    same = same_head()
    step_row, step_col = step_of(row), step_of(col)
    earlier = jnp.where(same & (step_row < step_col), 1.0, 0.0)
    place = (col & (MB - 1)).astype(F32)
    within = jnp.where(
        same & (step_row == step_col) & ((row & (MB - 1)) <= (col & (MB - 1))),
        MB / (place + 1.0),
        0.0,
    )
    head_ref[...] = jnp.where(same, 1.0, 0.0)
    earlier_ref[...] = earlier
    output_ref[...] = earlier + within


def centred_columns(values):
    return values - sum_rows(values) / HD


def spread(pairs):
    return jnp.concatenate(
        [jnp.broadcast_to(pairs[h : h + 1], (HD, HD)) for h in range(2)], axis=0
    ).T


def forward_kernel(
    starts_ref,
    proj_ref,
    rate_ref,
    ttt_w_ref,
    ttt_b_ref,
    ttt_gain_ref,
    ttt_shift_ref,
    cot_ref,
    inner_ref,
    z_ref,
    g_ref,
    out_ref,
    target_ref,
    state_ref,
    mi_ref,
    mx_ref,
    mo_ref,
    w_ref,
    gain_ref,
    base_ref,
    offset_ref,
    cot_rows_ref,
    head_ref,
    earlier_ref,
    output_ref,
    c_ref,
    shift_ref,
    *gather_sems,
):
    chunks = rate_ref.shape[0]
    gather = Gather(cot_ref, cot_rows_ref, *gather_sems)
    gather.start()
    places = Places(starts_ref)
    inner_masks(head_ref, earlier_ref, output_ref)
    w_ref[...] = centred_columns(jnp.concatenate([ttt_w_ref[0], ttt_w_ref[1]], axis=0).T)
    c_ref[...] = centred_columns(spread(ttt_b_ref[...]))
    gain_ref[...] = spread(ttt_gain_ref[...])
    shift_ref[...] = spread(ttt_shift_ref[...])

    def columns(chunk, index):
        return proj_ref[chunk_rows(chunk), index * LANES : (index + 1) * LANES]

    def prepare(chunk):
        source = wrap(chunk, chunks)
        before = wrap(source - 1, chunks)
        keys = split_heads(columns(source, 1))
        values = split_heads(columns(source, 2))
        docs_row, docs_lane = places.row_documents(source), places.lane_documents(source)
        gram = dot_nt(keys, keys) + 1.0
        mi_ref[chunk] = masked(gram * earlier_ref[...], docs_row == docs_lane).astype(BF16)
        cross = dot_nt(split_heads(columns(before, 1)), keys) + 1.0
        mx_ref[chunk] = masked(
            cross * head_ref[...], places.row_documents(before) == docs_lane
        ).astype(BF16)
        pick = selector()
        target = dot_nt(pick, keys) - dot_nt(pick, values) + shift_ref[...]
        target_ref[chunk] = target
        offset_ref[slot(chunk)] = jnp.broadcast_to(
            sum_rows(target * gain_ref[...]) / HD, offset_ref.shape[1:]
        )

    def read_state(rows, source, weight, bias, entry):
        docs_row = places.row_documents(source)
        live_lane = places.lane_documents(source) == entry
        both = jnp.concatenate(
            [masked(rows, docs_row == entry), masked(rows, docs_row != entry)], axis=1
        )
        weights = jnp.concatenate([weight, w_ref[...]], axis=1).astype(BF16)
        return dot_nt(weights, both) + jnp.where(live_lane, bias, c_ref[...])

    def base(chunk, weight, bias, entry):
        source = wrap(chunk, chunks)
        base_ref[slot(chunk)] = read_state(split_heads(columns(source, 1)), source, weight, bias, entry)

    def chain(chunk, rated_before):
        gain = gain_ref[...]
        gain2 = gain * gain
        tied = target_ref[chunk] * gain
        tied_mean = offset_ref[slot(chunk)][0:1]
        rate = rate_ref[chunk]
        matrix = mi_ref[chunk]

        def gradient(z):
            zg = z * gain2
            s1, s2, s3, s4 = sum_rows(z * z), sum_rows(zg), sum_rows(z * zg), sum_rows(z * tied)
            rs = lax.rsqrt(s1 / HD + EPS)
            mean_g = rs * s2 / HD + tied_mean
            mean_gx = rs * (rs * s3 + s4) / HD
            return rs * (z * (rs * (gain2 - mean_gx)) + (tied - mean_g))

        first = base_ref[slot(chunk)] - dot_nn(rated_before, mx_ref[chunk])
        z = first
        g = gradient(z)
        for _ in range(STEPS - 1):
            z = first - dot_nn((g * rate).astype(BF16), matrix)
            g = gradient(z)
        z_ref[chunk] = z
        g_ref[chunk] = g
        return (g * rate).astype(BF16)

    def advance(chunk, weight, bias, rated):
        keys = split_heads(columns(chunk, 1))
        last = places.last(chunk)
        kept = places.row_documents(chunk) == last
        both = jnp.concatenate(
            [masked(keys, kept), masked(head_ref[...].astype(BF16), kept)], axis=1
        )
        step = dot_nn(rated, both)
        keep = places.keeps(chunk)
        start_w, start_c = w_ref[...], c_ref[...]
        return (
            start_w + keep * (weight - start_w) - step[:, :LANES],
            start_c + keep * (bias - start_c) - step[:, LANES:],
        )

    def finish(chunk, weight, bias, rated):
        keys = split_heads(columns(chunk, 1))
        query_rows = columns(chunk, 0)
        queries = split_heads(query_rows)
        same_doc = places.row_documents(chunk) == places.lane_documents(chunk)
        matrix = masked((dot_nt(keys, queries) + 1.0) * output_ref[...], same_doc).astype(BF16)
        mo_ref[chunk] = matrix
        out = read_state(queries, chunk, weight, bias, places.entry(chunk)) - dot_nn(rated, matrix)
        out_ref[chunk] = out
        rs = lax.rsqrt(sum_rows(out * out) / HD + EPS)
        fitted = out * rs * gain_ref[...] + shift_ref[...]
        inner_ref[chunk_rows(chunk), :] = (to_rows(fitted) + query_rows.astype(F32)).astype(BF16)

    prepare(0)
    base(0, w_ref[...], c_ref[...], places.entry(0))

    def body(chunk, carry):
        weight_before, bias_before, rated_before = carry
        for step, when in enumerate(FORWARD_STEPS):
            pl.when(chunk == when)(gather.steps[step])
        before = wrap(chunk - 1, chunks)
        weight, bias = advance(before, weight_before, bias_before, rated_before)
        state_ref[chunk] = weight
        rated = chain(chunk, rated_before)
        base(chunk + 1, weight, bias, places.entry(chunk))
        prepare(chunk + 1)
        finish(before, weight_before, bias_before, rated_before)
        return weight, bias, rated

    carry = (w_ref[...], c_ref[...], jnp.zeros((HD, LANES), BF16))
    weight, bias, rated = lax.fori_loop(0, chunks, body, carry)
    finish(chunks - 1, weight, bias, rated)
    gather.end()


FORWARD_STEPS = (5, 7, 12, 16, 20, 24, 30)
BACKWARD_STEPS = (5, 7, 10, 13, 17, 20, 24)
SUM_STEPS = (6, 11, 19, 26)


def backward_kernel(
    starts_ref,
    proj_ref,
    rate_ref,
    dinner_ref,
    dgate_ref,
    mixed_ref,
    grads_ref,
    mix_ref,
    z_ref,
    g_ref,
    out_ref,
    target_ref,
    state_ref,
    mi_ref,
    mx_ref,
    mo_ref,
    w_ref,
    gain_ref,
    dproj_ref,
    dbias_ref,
    dw_ref,
    dc_ref,
    dgain_ref,
    dshift_ref,
    dout_ref,
    free_ref,
    base_ref,
    diag_ref,
    norm_ref,
    both_ref,
    wide_ref,
    coef_ref,
    y_ref,
    dz_ref,
    lam_ref,
    mixed_out,
    sums_ref,
    mix_rows_ref,
    head_ref,
    earlier_ref,
    output_ref,
    send_sem,
    recv_sem,
    *sems,
):
    chunks = rate_ref.shape[0]
    gather = Gather(mix_ref, mix_rows_ref, *sems[SEQ_SUM_SCRATCH:])
    total = SeqSum(1, grads_ref, sums_ref, *sems[:SEQ_SUM_SCRATCH])
    exchange = ToHeads(
        [(dgate_ref, dproj_ref, 3 * LANES), (mixed_ref, mixed_out, 0)], send_sem, recv_sem
    )
    gather.start([{"head": peer} for peer in exchange.peers] + total.peers())
    exchange.start()
    total.start()
    places = Places(starts_ref)
    inner_masks(head_ref, earlier_ref, output_ref)
    dbias_ref[...] = jnp.zeros_like(dbias_ref)
    dw_ref[...] = jnp.zeros_like(dw_ref)
    dc_ref[...] = jnp.zeros_like(dc_ref)
    dgain_ref[...] = jnp.zeros_like(dgain_ref)
    dshift_ref[...] = jnp.zeros_like(dshift_ref)

    def columns(chunk, index):
        return proj_ref[chunk_rows(chunk), index * LANES : (index + 1) * LANES]

    def prepare(chunk):
        gain = gain_ref[...]
        gain2 = gain * gain
        given = to_columns(dinner_ref[chunk_rows(chunk), :].astype(F32))
        out = out_ref[chunk]
        rs_out = lax.rsqrt(sum_rows(out * out) / HD + EPS)
        normal = out * rs_out
        scaled = given * gain
        dout = rs_out * (
            scaled - sum_rows(scaled) / HD - normal * (sum_rows(scaled * normal) / HD)
        )
        dgain_ref[...] += given * normal
        dshift_ref[...] += given
        rounded = dout.astype(BF16)
        dout_ref[slot(chunk)] = rounded
        free_ref[slot(chunk)] = dot_nt(rounded, mo_ref[chunk])
        z = z_ref[chunk]
        rs = lax.rsqrt(sum_rows(z * z) / HD + EPS)
        xh = z * rs
        xg = xh * gain2
        g = xg + target_ref[chunk] * gain
        mean_g = sum_rows(g) / HD
        mean_gx = sum_rows(g * xh) / HD
        mean_xg = sum_rows(xg) / HD
        diag_ref[slot(chunk)] = rs * (gain2 - mean_gx)
        norm_ref[slot(chunk)] = xh
        both_ref[slot(chunk)] = xg + g - mean_g - xh * mean_gx
        wide_ref[slot(chunk)] = xg + g
        coef_ref[slot(chunk)] = jnp.concatenate(
            [
                rs * rate_ref[chunk],
                rs,
                sum_rows(gain2) / HD + mean_gx,
                mean_xg + mean_g,
                mean_xg,
                sum_rows(xg * xh) / HD + 2.0 * mean_gx,
                jnp.zeros((2, LANES), F32),
            ],
            axis=0,
        )

    def chain(chunk, dz_after, cross):
        gain = gain_ref[...]
        gain2 = gain * gain
        diag, xh, both, wide = diag_ref[slot(chunk)], norm_ref[slot(chunk)], both_ref[slot(chunk)], wide_ref[slot(chunk)]
        coef = coef_ref[slot(chunk)]
        matrix = mi_ref[chunk]

        def pull(y):
            du = y * coef[0:1]
            a1 = sum_rows(du) / HD
            a2 = sum_rows(du * xh) / HD
            a3 = sum_rows(du * gain2) / HD - a1 * coef[2:3] - a2 * coef[3:4]
            a4 = sum_rows(du * both) / HD - a1 * coef[4:5] - a2 * coef[5:6]
            return diag * du - coef[1:2] * (gain2 * a1 + wide * a2 + a3 + xh * a4)

        first = -(base_ref[slot(chunk)] + dot_nt(dz_after, cross))
        y = first
        dz = pull(y)
        for _ in range(STEPS - 1):
            y = first - dot_nt(dz.astype(BF16), matrix)
            dz = pull(y)
        y_ref[slot(chunk)] = y
        rounded = dz.astype(BF16)
        dz_ref[slot(chunk)] = rounded
        return rounded

    def into_state(chunk, rows, values):
        docs_row, entry = places.row_documents(chunk), places.entry(chunk)
        live, dead = docs_row == entry, docs_row != entry
        heads = head_ref[...].astype(BF16)
        given = dot_nn(
            values,
            jnp.concatenate(
                [
                    masked(rows, live),
                    masked(heads, live),
                    masked(rows, dead),
                    masked(heads, dead),
                ],
                axis=1,
            ),
        )
        dw_ref[...] += given[:, 2 * LANES : 3 * LANES]
        dc_ref[...] += given[:, 3 * LANES :]
        return given[:, :LANES], given[:, LANES : 2 * LANES]

    def reach_back(source, lam_w, lam_c):
        kept_row = places.row_documents(source) == places.last(source)
        kept_lane = places.lane_documents(source) == places.last(source)
        keys = masked(split_heads(columns(source, 1)), kept_row)
        return dot_nt(lam_w.astype(BF16), keys) + jnp.where(kept_lane, lam_c, 0.0)

    def finish(chunk):
        gain = gain_ref[...]
        query_rows = split_heads(columns(chunk, 0))
        key_rows = split_heads(columns(chunk, 1))
        entry = places.entry(chunk)
        docs_row, docs_lane = places.row_documents(chunk), places.lane_documents(chunk)
        live, dead = docs_lane == entry, docs_lane != entry
        kept = docs_lane == places.last(chunk)
        same_doc = docs_row == docs_lane
        y = y_ref[slot(chunk)]
        g = g_ref[chunk]
        coef = coef_ref[slot(chunk)]
        dz = dz_ref[slot(chunk)]
        dout = dout_ref[slot(chunk)]
        xh = norm_ref[slot(chunk)]
        rate = rate_ref[chunk]
        logits = (sum_rows(g * y) * rate * (1.0 - HD * MB * rate)).astype(BF16)
        dbias_ref[...] += logits.astype(F32)
        rated = (g * rate).astype(BF16)
        du = y * coef[0:1]
        dg = du - sum_rows(du) / HD - xh * (sum_rows(du * xh) / HD)
        tied = dg * gain
        dgain_ref[...] += dg * (2.0 * gain * xh + target_ref[chunk])
        dshift_ref[...] += tied
        tied = tied.astype(BF16)
        earlier = earlier_ref[...]
        later = earlier_ref[...].T
        t_out = masked(dot_tn(rated, dout) * output_ref[...], same_doc).astype(BF16)
        t_in = masked(
            dot_tn(rated, dz) * earlier + dot_tn(dz, rated) * later, same_doc
        ).astype(BF16)
        states = jnp.concatenate([state_ref[chunk], w_ref[...]], axis=0).astype(BF16)
        dq = dot_tn(jnp.concatenate([masked(dout, live), masked(dout, dead)], axis=0), states)
        dq = dq - dot_tn(t_out, key_rows)
        sources = jnp.concatenate(
            [masked(dz, live), masked(dz, dead), masked(-rated, kept), tied], axis=0
        )
        pick = selector()
        dk = dot_tn(
            sources, jnp.concatenate([states, lam_ref[slot(chunk)].astype(BF16), pick], axis=0)
        )
        dk = dk - dot_nn(
            jnp.concatenate([t_out, t_in], axis=1),
            jnp.concatenate([query_rows, key_rows], axis=0),
        )
        dv = -dot_tn(tied, pick)
        rows = chunk_rows(chunk)
        dproj_ref[rows, 0:LANES] = (join_heads(dq) + dinner_ref[rows, :].astype(F32)).astype(BF16)
        dproj_ref[rows, LANES : 2 * LANES] = join_heads(dk).astype(BF16)
        dproj_ref[rows, 2 * LANES : 3 * LANES] = join_heads(dv).astype(BF16)
        diagonal = masked(
            jnp.broadcast_to(logits.astype(F32), (LANES, LANES)), square_iota(0) == square_iota(1)
        ).astype(BF16)
        head_column = (square_iota(1) == (square_iota(0) >> 6)).astype(F32).astype(BF16)
        spread = dot_nn(diagonal, head_column)
        dproj_ref[rows, 4 * LANES :] = (spread[:CHUNK] + spread[CHUNK:]).astype(BF16)

    last = chunks - 1
    prepare(last)
    base_ref[slot(last)] = free_ref[slot(last)]

    def body(index, carry):
        chunk = last - index
        lam_w, lam_c, dz_after = carry
        for step, when in enumerate(BACKWARD_STEPS):
            pl.when(index == when)(gather.steps[step])
        for step, when in enumerate(SUM_STEPS):
            pl.when(index == when)(total.steps[step])
        after = wrap(chunk + 1, chunks)
        cross = mx_ref[chunk + 1]
        dz = chain(chunk, dz_after, cross)
        add_w, add_c = into_state(after, split_heads(columns(after, 1)), dz_after)
        lam_w, lam_c = lam_w + add_w, lam_c + add_c
        lam_ref[slot(chunk)] = lam_w
        keep = places.keeps(chunk)
        dw_ref[...] += (1.0 - keep) * lam_w
        dc_ref[...] += (1.0 - keep) * lam_c
        add_w, add_c = into_state(chunk, split_heads(columns(chunk, 0)), dout_ref[slot(chunk)])
        lam_w, lam_c = keep * lam_w + add_w, keep * lam_c + add_c
        before = wrap(chunk - 1, chunks)

        @pl.when(chunk > 0)
        def _():
            prepare(before)
            base_ref[slot(before)] = free_ref[slot(before)] + reach_back(before, lam_w, lam_c)

        @pl.when(index > 0)
        def _():
            finish(after)

        return lam_w, lam_c, dz

    zero = jnp.zeros((HD, LANES), F32)
    lam_w, lam_c, dz = lax.fori_loop(
        0, chunks, body, (zero, zero, jnp.zeros((HD, LANES), BF16))
    )
    add_w, add_c = into_state(0, split_heads(columns(0, 1)), dz)
    dw_ref[...] += lam_w + add_w
    dc_ref[...] += lam_c + add_c
    finish(0)
    exchange.end()
    total.end()
    gather.end()


def whole_vmem(count):
    return [pl.BlockSpec(memory_space=pltpu.VMEM) for _ in range(count)]


def inner_forward(starts, proj, rates, ttt_w, ttt_b, gain, shift, own, number):
    tokens = proj.shape[0]
    chunks = tokens // CHUNK
    cell = jax.ShapeDtypeStruct((chunks, HD, LANES), F32)
    square = jax.ShapeDtypeStruct((HD, LANES), F32)
    return pl.pallas_call(
        forward_kernel,
        out_shape=[
            jax.ShapeDtypeStruct((tokens, LANES), BF16),
            cell,
            cell,
            cell,
            jax.ShapeDtypeStruct((chunks + 1, HD, LANES), F32),
            cell,
            jax.ShapeDtypeStruct((chunks + 1, LANES, LANES), BF16),
            jax.ShapeDtypeStruct((chunks + 1, LANES, LANES), BF16),
            jax.ShapeDtypeStruct((chunks, LANES, LANES), BF16),
            square,
            square,
            jax.ShapeDtypeStruct((RING, HD, LANES), F32),
            jax.ShapeDtypeStruct((RING, 8, LANES), F32),
            gathered_shape(own),
        ],
        in_specs=[pl.BlockSpec(memory_space=pltpu.SMEM)] + whole_vmem(6) + [ANYWHERE],
        out_specs=whole_vmem(13) + [ANYWHERE],
        scratch_shapes=[
            pltpu.VMEM((LANES, LANES), F32),
            pltpu.VMEM((LANES, LANES), F32),
            pltpu.VMEM((LANES, LANES), F32),
            pltpu.VMEM((HD, LANES), F32),
            pltpu.VMEM((HD, LANES), F32),
        ]
        + gather_scratch(),
        compiler_params=pltpu.CompilerParams(
            collective_id=number, has_side_effects=True, vmem_limit_bytes=MOST_VMEM
        ),
        name="inner_forward",
    )(starts, proj, rates, ttt_w, ttt_b, gain, shift, own)


def inner_backward(starts, proj, rates, d_inner, d_gate, mixed, grads, own, kept, number):
    tokens = proj.shape[0]
    chunks = tokens // CHUNK
    square = jax.ShapeDtypeStruct((HD, LANES), F32)
    cell = jax.ShapeDtypeStruct((RING, HD, LANES), F32)
    cell16 = jax.ShapeDtypeStruct((RING, HD, LANES), BF16)
    return pl.pallas_call(
        backward_kernel,
        out_shape=[
            jax.ShapeDtypeStruct((tokens, 5 * LANES), BF16),
            jax.ShapeDtypeStruct((1, LANES), F32),
            square,
            square,
            square,
            square,
            cell16,
            cell,
            cell,
            cell,
            cell,
            cell,
            cell,
            jax.ShapeDtypeStruct((RING, 8, LANES), F32),
            cell,
            cell16,
            cell,
            jax.ShapeDtypeStruct((tokens, LANES), BF16),
            jax.ShapeDtypeStruct(grads.shape, BF16),
            gathered_shape(own),
        ],
        in_specs=[pl.BlockSpec(memory_space=pltpu.SMEM)]
        + whole_vmem(6)
        + [ANYWHERE]
        + whole_vmem(len(kept)),
        out_specs=whole_vmem(19) + [ANYWHERE],
        scratch_shapes=[
            pltpu.VMEM((LANES, LANES), F32),
            pltpu.VMEM((LANES, LANES), F32),
            pltpu.VMEM((LANES, LANES), F32),
        ]
        + to_heads_scratch(2)
        + seq_sum_scratch(grads.shape, 1)
        + gather_scratch(),
        compiler_params=pltpu.CompilerParams(
            collective_id=number, has_side_effects=True, vmem_limit_bytes=MOST_VMEM
        ),
        name="inner_backward",
    )(starts, proj, rates, d_inner, d_gate, mixed, grads, own, *kept)


def heads_of_lanes(values):
    return jnp.sum(values.reshape(HD, 2, HD), axis=2).T


def project_kernel(x_ref, w_ref, rate_w_ref, bias_ref, proj_ref, rate_ref):
    x = x_ref[...]
    proj_ref[...] = dot_nn(x, w_ref[...]).astype(BF16)
    logits = dot_nt(rate_w_ref[...], x)
    for index in range(rate_ref.shape[0]):
        tokens = slice(index * CHUNK, (index + 1) * CHUNK)
        lanes = jnp.concatenate([logits[0:1, tokens], logits[1:2, tokens]], axis=1)
        rate_ref[index] = jax.nn.sigmoid(lanes + bias_ref[...]) / (HD * MB)


def project(gathered, w_in, w_rate, rate_bias):
    tokens, width = gathered.shape
    columns = w_in.shape[1]
    block = 4 * CHUNK
    rate_w = jnp.pad(w_rate.T, ((0, 14), (0, 0)))
    bias = jnp.repeat(rate_bias, HD)[None]
    return pl.pallas_call(
        project_kernel,
        grid=(tokens // block,),
        out_shape=[
            jax.ShapeDtypeStruct((tokens, columns), BF16),
            jax.ShapeDtypeStruct((tokens // CHUNK, 1, LANES), F32),
        ],
        in_specs=[
            pl.BlockSpec((block, width), lambda i: (i, 0)),
            pl.BlockSpec((width, columns), lambda i: (0, 0)),
            pl.BlockSpec((16, width), lambda i: (0, 0)),
            pl.BlockSpec((1, LANES), lambda i: (0, 0)),
        ],
        out_specs=[
            pl.BlockSpec((block, columns), lambda i: (i, 0)),
            pl.BlockSpec((block // CHUNK, 1, LANES), lambda i: (i, 0, 0)),
        ],
        compiler_params=pltpu.CompilerParams(vmem_limit_bytes=MOST_VMEM),
        name="project",
    )(gathered, w_in, rate_w, bias)


def mean_columns(values):
    return jnp.mean(values, axis=1, keepdims=True)


GELU_RATE = 0.7978845608028654
GELU_CUBE = 0.044715


def gelu_parts(x):
    square = x * x
    tanh = jnp.tanh(GELU_RATE * x * (1.0 + GELU_CUBE * square))
    half = 0.5 * (1.0 + tanh)
    slope = half + 0.5 * x * (1.0 - tanh * tanh) * GELU_RATE * (1.0 + 3.0 * GELU_CUBE * square)
    return x * half, slope


def line_of(gains_ref, index):
    return jnp.concatenate(
        [gains_ref[k, index : index + 1, :] for k in range(gains_ref.shape[0])], axis=1
    )


def post_norm_of(inner_ref):
    inner = inner_ref[...].astype(F32)
    centred = inner - mean_columns(inner)
    rstd = lax.rsqrt(mean_columns(centred * centred) + EPS)
    return centred * rstd, rstd


def middle_forward_kernel(
    inner_ref, gate_ref, gains_ref, tokens_ref, ffn_gain_ref, w_ref, mixed_ref, hidden_ref, norm_ref
):
    xp, _ = post_norm_of(inner_ref)
    post = xp * line_of(gains_ref, 0) + line_of(gains_ref, 1)
    act, _ = gelu_parts(gate_ref[...].astype(F32))
    mixed = (post * act).astype(BF16)
    mixed_ref[...] = mixed
    pieces, _, piece = w_ref.shape
    for k in range(pieces):
        columns = slice(k * piece, (k + 1) * piece)
        hidden_ref[:, columns] = tokens_ref[:, columns].astype(F32) + dot_nn(mixed, w_ref[k])
    hidden = hidden_ref[...]
    scale = lax.rsqrt(mean_columns(hidden * hidden) + EPS)
    norm_ref[...] = (hidden * scale * ffn_gain_ref[...]).astype(BF16)


def middle_forward(inner, gate, gains, tokens, ffn_gain, w_out):
    shape = tokens.shape
    return pl.pallas_call(
        middle_forward_kernel,
        out_shape=[
            jax.ShapeDtypeStruct(shape, BF16),
            jax.ShapeDtypeStruct(shape, F32),
            jax.ShapeDtypeStruct(shape, BF16),
        ],
        in_specs=whole_vmem(6),
        out_specs=whole_vmem(3),
        compiler_params=pltpu.CompilerParams(vmem_limit_bytes=24 * 1024 * 1024),
        name="middle_forward",
    )(inner, gate, gains, tokens, ffn_gain, w_out)


def middle_backward_kernel(
    d_norm_ref,
    hidden_ref,
    cot_ref,
    ffn_gain_ref,
    inner_ref,
    gate_ref,
    gains_ref,
    w_ref,
    d_res_ref,
    d_mix_ref,
    d_inner_ref,
    d_gate_ref,
    sums_ref,
):
    hidden = hidden_ref[...]
    scale = lax.rsqrt(mean_columns(hidden * hidden) + EPS)
    d_norm = d_norm_ref[...]
    weighted = d_norm * ffn_gain_ref[...]
    normed = hidden * scale
    d_res = cot_ref[...].astype(F32) + scale * (
        weighted - normed * mean_columns(weighted * normed)
    )
    d_res_ref[...] = d_res
    d_mix_ref[...] = d_res.astype(BF16)
    pieces, _, piece = w_ref.shape
    d_mixed = dot_nt(d_mix_ref[:, 0:piece], w_ref[0])
    for k in range(1, pieces):
        d_mixed = d_mixed + dot_nt(d_mix_ref[:, k * piece : (k + 1) * piece], w_ref[k])
    xp, rstd = post_norm_of(inner_ref)
    post_gain = line_of(gains_ref, 0)
    post = xp * post_gain + line_of(gains_ref, 1)
    act, slope = gelu_parts(gate_ref[...].astype(F32))
    d_post = d_mixed * act
    d_gate_ref[...] = (d_mixed * post * slope).astype(BF16)
    dx = d_post * post_gain
    d_inner = rstd * (dx - mean_columns(dx) - xp * mean_columns(dx * xp))
    d_inner_ref[...] = d_inner.astype(BF16)
    lines = (sum_rows(d_post * xp), sum_rows(d_post), sum_rows(d_norm * normed))
    for k in range(sums_ref.shape[0]):
        columns = slice(k * LANES, (k + 1) * LANES)
        sums_ref[k] = jnp.concatenate(
            [line[:, columns] for line in lines] + [jnp.zeros((5, LANES), F32)], axis=0
        )


def middle_backward(d_norm, hidden, cotangent, ffn_gain, inner, gate, gains, w_out):
    shape = cotangent.shape
    return pl.pallas_call(
        middle_backward_kernel,
        out_shape=[
            jax.ShapeDtypeStruct(shape, F32),
            jax.ShapeDtypeStruct(shape, BF16),
            jax.ShapeDtypeStruct(shape, BF16),
            jax.ShapeDtypeStruct(shape, BF16),
            jax.ShapeDtypeStruct(gains.shape, F32),
        ],
        in_specs=whole_vmem(8),
        out_specs=whole_vmem(5),
        compiler_params=pltpu.CompilerParams(vmem_limit_bytes=32 * 1024 * 1024),
        name="middle_backward",
    )(d_norm, hidden, cotangent, ffn_gain, inner, gate, gains, w_out)


RING_X = 4
RING_Y = 4
GROUP = RING_X * RING_Y
UNITS = 4
MESH = pl.DeviceIdType.MESH


def place_at(head, dx, dy):
    return lax.rem(head // RING_Y + dx + RING_X, RING_X) * RING_Y + lax.rem(
        lax.rem(head, RING_Y) + dy + RING_Y, RING_Y
    )


def neighbours(head):
    return {
        (axis, way): place_at(head, way if axis == 0 else 0, way if axis == 1 else 0)
        for axis in (0, 1)
        for way in (1, -1)
    }


def greet(peers):
    barrier = pltpu.get_barrier_semaphore()
    for peer in peers:
        pl.semaphore_signal(barrier, inc=1, device_id=peer, device_id_type=MESH)
    pl.semaphore_wait(barrier, len(peers))


def moved(place, axis, way):
    shift = (way, 0) if axis == 0 else (0, way)
    return tuple((p - s) % n for p, s, n in zip(place, shift, (RING_X, RING_Y)))


class Gather:
    def __init__(self, own_ref, full_ref, send_sem, recv_sem, local_sem):
        self.own_ref, self.full_ref = own_ref, full_ref
        self.send_sem, self.recv_sem, self.local_sem = send_sem, recv_sem, local_sem
        self.head = lax.axis_index("head")
        self.near = neighbours(self.head)
        self.rows = own_ref.shape[0]
        self.unit_rows = self.rows // UNITS
        self.count = 0
        self.halves = ((0, (0, 1)), (1, (2, 3)))
        self.steps = [
            partial(self.first_arrivals, 0),
            partial(self.first_arrivals, 1),
            partial(self.second_hops, (0,)),
            self.far_arrivals,
            partial(self.second_hops, (1,)),
            partial(self.second_hops, (3,)),
            partial(self.second_hops, (2,)),
        ]

    def slab(self, place, unit):
        start = place_at(self.head, *place) * self.rows + unit * self.unit_rows
        return self.full_ref.at[pl.ds(pl.multiple_of(start, self.unit_rows), self.unit_rows)]

    def arrival(self, place, unit):
        return self.recv_sem.at[(place[0] * RING_Y + place[1]) * UNITS + unit]

    def send(self, place, unit, axis, way):
        source = (
            self.own_ref.at[pl.ds(unit * self.unit_rows, self.unit_rows)]
            if place == (0, 0)
            else self.slab(place, unit)
        )
        pltpu.make_async_remote_copy(
            src_ref=source,
            dst_ref=self.slab(place, unit),
            send_sem=self.send_sem.at[self.count],
            recv_sem=self.arrival(moved(place, axis, way), unit),
            device_id={"head": self.near[axis, way]},
            device_id_type=MESH,
        ).start()
        self.count += 1

    def waiter(self, place, unit, send_number=0):
        return pltpu.make_async_remote_copy(
            src_ref=self.slab(place, unit),
            dst_ref=self.slab(place, unit),
            send_sem=self.send_sem.at[send_number],
            recv_sem=self.arrival(place, unit),
            device_id={"head": self.near[0, 1]},
            device_id_type=MESH,
        )

    def arrive(self, place, unit):
        self.waiter(place, unit).wait_recv()

    def own_copy(self):
        start = pl.multiple_of(self.head * self.rows, self.rows)
        return pltpu.make_async_copy(
            self.own_ref, self.full_ref.at[pl.ds(start, self.rows)], self.local_sem
        )

    def cross(self, axis, first, second):
        first, second = first % RING_X, second % RING_X
        return (first, second) if axis == 0 else (second, first)

    def start(self, greeted=None):
        greet(greeted or [{"head": peer} for peer in self.near.values()])
        self.own_copy().start()
        for turned in (False, True):
            for axis, units in self.halves:
                for unit in units:
                    for way in (1, -1):
                        self.send((0, 0), unit, 1 - axis if turned else axis, way)

    def first_arrivals(self, step):
        for axis, units in self.halves:
            for way in (1, -1):
                place = self.cross(axis, -way, 0)
                unit = units[0 if (way == 1) == (step == 0) else 1]
                self.arrive(place, unit)
                if step == 0:
                    self.send(place, unit, axis, way)
                for turn in (1, -1):
                    self.send(place, unit, 1 - axis, turn)

    def second_hops(self, firsts):
        for first in firsts:
            for axis, units in self.halves:
                for way in (1, -1):
                    unit = units[0 if way == 1 else 1]
                    place = self.cross(axis, first, -way)
                    self.arrive(place, unit)
                    self.send(place, unit, 1 - axis, way)

    def far_arrivals(self):
        for way in (1, -1):
            for axis, units in self.halves:
                unit = units[0 if way == 1 else 1]
                place = self.cross(axis, 2, 0)
                self.arrive(place, unit)
                for turn in (1, -1):
                    self.send(place, unit, 1 - axis, turn)

    def end(self):
        for first in range(RING_X):
            for axis, units in self.halves:
                for way in (1, -1):
                    self.arrive(self.cross(axis, first, -way), units[1 if way == 1 else 0])
        for first in range(RING_X):
            for axis, units in self.halves:
                for unit in units:
                    self.arrive(self.cross(axis, first, 2), unit)
        for number in range(TRANSFERS):
            self.waiter((0, 0), 0, number).wait_send()
        self.own_copy().wait()


TRANSFERS = UNITS * (GROUP - 1)
STAGED = 32
ANYWHERE = pl.BlockSpec(memory_space=pl.ANY)


def gather_kernel(*refs):
    gather = Gather(*refs)
    gather.start()
    for step in gather.steps:
        step()
    gather.end()


def gather_scratch():
    return [
        pltpu.SemaphoreType.DMA((TRANSFERS,)),
        pltpu.SemaphoreType.DMA((UNITS * GROUP,)),
        pltpu.SemaphoreType.DMA,
    ]


def gathered_shape(own):
    return jax.ShapeDtypeStruct((own.shape[0] * GROUP, own.shape[1]), own.dtype)


def gather_rows(own, number):
    return pl.pallas_call(
        gather_kernel,
        out_shape=gathered_shape(own),
        in_specs=[ANYWHERE],
        out_specs=ANYWHERE,
        scratch_shapes=gather_scratch(),
        compiler_params=pltpu.CompilerParams(collective_id=number, has_side_effects=True),
        name="gather_rows",
    )(own)


class SeqSum:
    SENDS = 24

    def __init__(
        self, axis, part_ref, sum_ref, pair_held, ring_held, stage_ref, send_sem, recv_sem
    ):
        self.axis = axis
        self.part_ref, self.sum_ref = part_ref, sum_ref
        self.pair_held, self.ring_held, self.stage_ref = pair_held, ring_held, stage_ref
        self.send_sem, self.recv_sem = send_sem, recv_sem
        seq = lax.axis_index("seq")
        self.chips = lax.axis_size("seq") // 2
        self.z, self.core = seq // 2, lax.rem(seq, 2)
        self.quarter = part_ref.shape[axis] // (2 * self.chips)
        self.unit = self.quarter // 2
        self.sibling = self.z * 2 + 1 - self.core
        self.near = {
            way: lax.rem(self.z + way + self.chips, self.chips) * 2 + self.core for way in (1, -1)
        }
        self.sends = []
        self.steps = [self.pair_arrivals, self.far_arrivals, self.own_sum, self.ring_arrivals]

    def peers(self):
        return [{"seq": peer} for peer in (self.sibling, self.near[1], self.near[-1])]

    def cut(self, ref, start, size):
        if not isinstance(start, int):
            start = pl.multiple_of(start, size)
        return ref.at[pl.ds(start, size)] if self.axis == 0 else ref.at[:, pl.ds(start, size)]

    def part(self, ref, core, dz, unit=None):
        owner = lax.rem(self.z + dz + self.chips, self.chips)
        start = (core * self.chips + owner) * self.quarter
        if unit is None:
            return self.cut(ref, start, self.quarter)
        return self.cut(ref, start + unit * self.unit, self.unit)

    def paired(self, dz):
        return self.cut(self.pair_held, dz * self.quarter, self.quarter)

    def staged(self, dz, unit=None):
        if unit is None:
            return self.cut(self.stage_ref, dz * self.quarter, self.quarter)
        return self.cut(self.stage_ref, dz * self.quarter + unit * self.unit, self.unit)

    def held(self, number):
        return self.cut(self.ring_held, number * self.unit, self.unit)

    def send(self, source, target, peer):
        number = len(self.sends)

        def copy():
            return pltpu.make_async_remote_copy(
                src_ref=source(),
                dst_ref=target(),
                send_sem=self.send_sem.at[number],
                recv_sem=self.recv_sem.at[number],
                device_id={"seq": peer},
                device_id_type=MESH,
            )

        copy().start()
        self.sends.append(copy)
        return number

    def arrive(self, number):
        self.sends[number]().wait_recv()

    def start(self):
        self.pair = {}
        for dz in (2, 1, 3, 0):
            self.pair[dz] = self.send(
                partial(self.part, self.part_ref, 1 - self.core, dz),
                partial(self.paired, dz),
                self.sibling,
            )

    def pair_arrivals(self):
        for dz in (2, 1, 3, 0):
            self.arrive(self.pair[dz])
            total = self.part(self.part_ref, self.core, dz)[...].astype(F32)
            total = total + self.paired(dz)[...].astype(F32)
            self.staged(dz)[...] = total.astype(BF16)
            if dz == 2:
                self.far = {
                    way: self.send(
                        partial(self.staged, 2, unit), partial(self.held, unit), self.near[way]
                    )
                    for way, unit in ((1, 0), (-1, 1))
                }
        self.plain = {
            way: self.send(
                partial(self.staged, way % 4, unit), partial(self.held, 2 + unit), self.near[way]
            )
            for way, unit in ((1, 1), (-1, 0))
        }

    def far_arrivals(self):
        self.onward = {}
        for way, unit in ((1, 0), (-1, 1)):
            self.arrive(self.far[way])
            place = self.staged(way % 4, unit)
            total = place[...].astype(F32) + self.held(unit)[...].astype(F32)
            place[...] = total.astype(BF16)
            self.onward[way] = self.send(
                partial(self.staged, way % 4, unit), partial(self.held, 4 + unit), self.near[way]
            )

    def own_sum(self):
        for way in (1, -1):
            self.arrive(self.plain[way])
            self.arrive(self.onward[way])
        self.direct = {}
        for unit in (0, 1):
            total = self.staged(0, unit)[...].astype(F32)
            total = total + self.held(2 + unit)[...].astype(F32)
            total = total + self.held(4 + unit)[...].astype(F32)
            place = self.part(self.sum_ref, self.core, 0, unit)
            place[...] = total.astype(BF16)
        for unit in (0, 1):
            place = partial(self.part, self.sum_ref, self.core, 0, unit)
            for way in (1, -1):
                self.direct[way, unit] = self.send(place, place, self.near[way])
        self.relayed = [self.relay(0, unit) for unit in (0, 1)]

    def relay(self, dz, unit):
        place = partial(self.part, self.sum_ref, self.core, dz, unit)
        return self.send(place, place, self.sibling)

    def ring_arrivals(self):
        self.passed = {}
        for unit in (0, 1):
            for way in (1, -1):
                self.arrive(self.direct[way, unit])
                if unit == (0 if way == 1 else 1):
                    place = partial(self.part, self.sum_ref, self.core, -way, unit)
                    self.passed[way] = self.send(place, place, self.near[way])
        for unit in (0, 1):
            for way in (1, -1):
                self.relayed.append(self.relay(-way, unit))

    def end(self):
        for way, unit in ((1, 0), (-1, 1)):
            self.arrive(self.passed[way])
            self.relayed.append(self.relay(2, unit))
        for number in self.relayed:
            self.arrive(number)
        for copy in self.sends:
            copy().wait_send()


def seq_sum_scratch(shape, axis):
    def pieces(numerator, denominator):
        size = numerator * shape[axis] // denominator
        return pltpu.VMEM((size, shape[1]) if axis == 0 else (shape[0], size), BF16)

    return [
        pieces(1, 2),
        pieces(6, 16),
        pieces(1, 2),
        pltpu.SemaphoreType.DMA((SeqSum.SENDS,)),
        pltpu.SemaphoreType.DMA((SeqSum.SENDS,)),
    ]


SEQ_SUM_SCRATCH = 5


class SmallSums:
    def __init__(
        self, sums, shard_ref, shard_out, lines_out, held, send_sem, recv_sem, *line_sems
    ):
        self.sums = sums
        self.shard_ref, self.shard_out, self.lines_out = shard_ref, shard_out, lines_out
        self.held, self.send_sem, self.recv_sem = held, send_sem, recv_sem
        self.line_send, self.line_recv = line_sems
        head, seq = lax.axis_index("head"), lax.axis_index("seq")
        self.head = head
        self.seqs = held.shape[0]
        self.seq_peers = [lax.rem(seq + ahead, self.seqs) for ahead in range(1, self.seqs)]
        self.head_peers = [lax.rem(head + ahead, GROUP) for ahead in range(1, GROUP)]

    def peers(self):
        return [{"seq": peer} for peer in self.seq_peers] + [
            {"head": peer} for peer in self.head_peers
        ]

    def step(self, index):
        for total in self.sums:
            total.steps[index]()

    def start(self):
        for total in self.sums:
            total.start()
        self.sends = []
        for ahead, peer in enumerate(self.seq_peers, 1):
            done = pltpu.make_async_remote_copy(
                src_ref=self.shard_ref,
                dst_ref=self.held.at[ahead],
                send_sem=self.send_sem.at[ahead],
                recv_sem=self.recv_sem.at[ahead],
                device_id={"seq": peer},
                device_id_type=MESH,
            )
            done.start()
            self.sends.append(done)

    def turn(self):
        for done in self.sends:
            done.wait_recv()
        shard = self.shard_ref[...]
        for ahead in range(1, self.seqs):
            shard = shard + self.held[ahead]
        self.shard_out[...] = shard
        self.lines_out[self.head] = shard[0:8]
        self.passed = []
        for ahead, peer in enumerate(self.head_peers, 1):
            done = pltpu.make_async_remote_copy(
                src_ref=self.shard_out.at[0:8],
                dst_ref=self.lines_out.at[self.head],
                send_sem=self.line_send.at[ahead],
                recv_sem=self.line_recv.at[ahead],
                device_id={"head": peer},
                device_id_type=MESH,
            )
            done.start()
            self.passed.append(done)

    def end(self):
        for total in self.sums:
            total.end()
        for done in self.passed:
            done.wait_recv()
        for done in self.sends + self.passed:
            done.wait_send()


class Everywhere:
    def __init__(self, part_ref, sum_ref, seq_held, line_ref, head_held, *sems):
        self.part_ref, self.sum_ref = part_ref, sum_ref
        self.seq_held, self.line_ref, self.head_held = seq_held, line_ref, head_held
        self.sems = sems

    def push(self, source, held, axis, send_sem, recv_sem):
        count, me = held.shape[0], lax.axis_index(axis)
        sends = []
        for ahead in range(1, count):
            done = pltpu.make_async_remote_copy(
                src_ref=source,
                dst_ref=held.at[ahead],
                send_sem=send_sem.at[ahead],
                recv_sem=recv_sem.at[ahead],
                device_id={axis: lax.rem(me + ahead, count)},
                device_id_type=MESH,
            )
            done.start()
            sends.append(done)
        return sends

    def total(self, source, held, sends):
        total = source[...]
        for ahead, done in enumerate(sends, 1):
            done.wait_recv()
            total = total + held[ahead]
        return total

    def start(self):
        self.over_seq = self.push(self.part_ref, self.seq_held, "seq", *self.sems[:2])

    def turn(self):
        self.line_ref[...] = self.total(self.part_ref, self.seq_held, self.over_seq)
        self.over_head = self.push(self.line_ref, self.head_held, "head", *self.sems[2:])

    def end(self):
        self.sum_ref[...] = self.total(self.line_ref, self.head_held, self.over_head)
        for done in self.over_seq + self.over_head:
            done.wait_send()


def everywhere_scratch(shape, seqs):
    return [
        pltpu.VMEM((seqs,) + shape, F32),
        pltpu.VMEM(shape, F32),
        pltpu.VMEM((GROUP,) + shape, F32),
        pltpu.SemaphoreType.DMA((seqs,)),
        pltpu.SemaphoreType.DMA((seqs,)),
        pltpu.SemaphoreType.DMA((GROUP,)),
        pltpu.SemaphoreType.DMA((GROUP,)),
    ]


EVERYWHERE_SCRATCH = 7


class FeedForwardGradients:
    def __init__(self, turned, rows_ref, cot_ref, grads_ref, wide_ref, sem):
        self.turned, self.grads_ref, self.wide_ref = turned, grads_ref, wide_ref
        self.fetch = pltpu.make_async_copy(rows_ref, wide_ref, sem.at[0])
        self.fetch_cot = pltpu.make_async_copy(cot_ref, wide_ref, sem.at[1])
        self.padded = grads_ref.shape[0] // len(turned)
        self.tile = 256
        self.tiles = wide_ref.shape[1] // self.tile

    def start(self):
        self.fetch.start()

    def product(self, indices, first, last):
        def step(number, carry):
            cut = pl.ds(pl.multiple_of(number * self.tile, self.tile), self.tile)
            wide = self.wide_ref[:, cut]
            for index in indices:
                turned = self.turned[index]
                spare = jnp.zeros((self.padded - turned.shape[0], self.tile), F32)
                product = jnp.concatenate([dot_nn(turned[...], wide), spare], axis=0)
                place = slice(index * self.padded, (index + 1) * self.padded)
                self.grads_ref[place, cut] = product.astype(BF16)
            return carry

        lax.fori_loop(first, last, step, 0)

    def piece(self, index):
        half = self.tiles // 2
        if index == 0:
            self.fetch.wait()
            self.product((0, 1), 0, half)
        elif index == 1:
            self.product((0, 1), half, self.tiles)
            self.fetch_cot.start()
        elif index == 2:
            self.fetch_cot.wait()
            self.product((2,), 0, self.tiles)


def scatter_kernel(
    part_ref,
    d_gate_ref,
    d_up_ref,
    hidden_ref,
    rows_ref,
    cot_ref,
    sum_ref,
    grads_ref,
    held_ref,
    stage_ref,
    send_sem,
    recv_sem,
    wide_ref,
    sem,
):
    work = FeedForwardGradients(
        (d_gate_ref, d_up_ref, hidden_ref), rows_ref, cot_ref, grads_ref, wide_ref, sem
    )
    work.start()
    scatter_body(None, part_ref, sum_ref, held_ref, stage_ref, send_sem, recv_sem, work)


def scatter_small_kernel(
    part_ref,
    shard_ref,
    grad_in_ref,
    grad_out_ref,
    tokens_ref,
    d_res_ref,
    gain_ref,
    grad_tokens_ref,
    gain_sum_ref,
    shard_out,
    lines_out,
    sum_in_ref,
    sum_out_ref,
    held_ref,
    stage_ref,
    send_sem,
    recv_sem,
    sum_ref,
    gain_part_ref,
    *scratch,
):
    count = 2 * SEQ_SUM_SCRATCH
    sums = (
        SeqSum(0, grad_in_ref, sum_in_ref, *scratch[:SEQ_SUM_SCRATCH]),
        SeqSum(1, grad_out_ref, sum_out_ref, *scratch[SEQ_SUM_SCRATCH:count]),
    )
    more = count + EVERYWHERE_SCRATCH
    gain_sum = Everywhere(gain_part_ref, gain_sum_ref, *scratch[count:more])
    small = SmallSums(sums, shard_ref, shard_out, lines_out, *scratch[more:])
    scatter_body(small, part_ref, sum_ref, held_ref, stage_ref, send_sem, recv_sem)
    resid = tokens_ref[...].astype(F32)
    scale = lax.rsqrt(mean_columns(resid * resid) + EPS)
    normed = resid * scale
    d_norm = sum_ref[...]
    line = sum_rows(d_norm * normed)
    for k in range(GROUP):
        gain_part_ref[k : k + 1, :] = line[:, k * LANES : (k + 1) * LANES]
    gain_sum.start()
    weighted = d_norm * gain_ref[...]
    grad_tokens_ref[...] = d_res_ref[...] + scale * (
        weighted - normed * mean_columns(weighted * normed)
    )
    gain_sum.turn()
    small.end()
    gain_sum.end()


def scatter_body(
    small, part_ref, sum_ref, held_ref, stage_ref, send_sem, recv_sem, work=None
):
    head = lax.axis_index("head")
    near = neighbours(head)
    rows = sum_ref.shape[0]
    unit_rows = rows // UNITS
    peers = [{"head": peer} for peer in near.values()]
    greet(peers if small is None else small.peers())
    sends, blocks, staged = [], [], {}

    def slab(place, unit):
        start = place_at(head, *place) * rows + unit * unit_rows
        return part_ref.at[pl.ds(pl.multiple_of(start, unit_rows), unit_rows)]

    def held(index):
        return pl.ds(index * unit_rows, unit_rows)

    def stage(place, unit, total):
        block = stage_ref.at[held(len(blocks))]
        block[...] = total.astype(BF16)
        blocks.append(block)
        staged[place, unit] = block

    def send(place, unit, axis, way):
        index = len(sends)
        done = pltpu.make_async_remote_copy(
            src_ref=staged.get((place, unit), slab(place, unit)),
            dst_ref=held_ref.at[held(index)],
            send_sem=send_sem.at[index],
            recv_sem=recv_sem.at[index],
            device_id={"head": near[axis, way]},
            device_id_type=MESH,
        )
        done.start()
        sends.append(done)
        return index

    def arrived(index):
        sends[index].wait_recv()
        return held_ref[held(index)].astype(F32)

    def add_to(place, unit, *indices):
        total = staged.get((place, unit), slab(place, unit))[...].astype(F32)
        for index in indices:
            total = total + arrived(index)
        return total

    def cross(axis, first, second):
        first, second = first % RING_X, second % RING_X
        return (first, second) if axis == 0 else (second, first)

    halves = ((1, (0, 1)), (0, (2, 3)))

    def far(axis, units, other):
        return {
            way: send(cross(axis, 2, other), units[0 if way == 1 else 1], axis, way)
            for way in (1, -1)
        }

    def plain(axis, units, other):
        return {
            way: send(cross(axis, way, other), units[1 if way == 1 else 0], axis, way)
            for way in (1, -1)
        }

    def onward(axis, units, other, from_far):
        result = {}
        for way in (1, -1):
            place, unit = cross(axis, way, other), units[0 if way == 1 else 1]
            stage(place, unit, add_to(place, unit, from_far[way]))
            result[way] = send(place, unit, axis, way)
        return result

    def collect(axis, units, other, by_plain, by_onward):
        place = cross(axis, 0, other)
        return [
            add_to(place, units[0], by_onward[1], by_plain[-1]),
            add_to(place, units[1], by_onward[-1], by_plain[1]),
        ]

    order = (2, 1, 3, 0)
    fars = {(axis, o): far(axis, units, o) for o in order for axis, units in halves}
    plains = {(axis, o): plain(axis, units, o) for o in order for axis, units in halves}
    if small is not None:
        small.start()
        small.step(0)
    if work is not None:
        work.piece(0)
    onwards = {
        (axis, o): onward(axis, units, o, fars[axis, o]) for o in order for axis, units in halves
    }
    if small is not None:
        small.step(1)
    if work is not None:
        work.piece(1)
    last_far, last_plain, last_onward = {}, {}, {}

    def first_sum(axis, units, other):
        totals = collect(axis, units, other, plains[axis, other], onwards[axis, other])
        place = cross(axis, 0, other)
        for unit, total in zip(units, totals):
            stage(place, unit, total)

    for axis, units in halves:
        first_sum(axis, units, 2)
        last_far[axis] = far(1 - axis, units, 0)
    for axis, units in halves:
        first_sum(axis, units, 1)
        first_sum(axis, units, 3)
        last_plain[axis] = plain(1 - axis, units, 0)
    if small is not None:
        small.step(2)
    if work is not None:
        work.piece(2)
    for axis, units in halves:
        last_onward[axis] = onward(1 - axis, units, 0, last_far[axis])
    if small is not None:
        small.step(3)
        small.turn()
    for axis, units in halves:
        own = collect(axis, units, 0, plains[axis, 0], onwards[axis, 0])
        extra = (
            (last_onward[axis][1], last_plain[axis][-1]),
            (last_onward[axis][-1], last_plain[axis][1]),
        )
        for unit, total, indices in zip(units, own, extra):
            for index in indices:
                total = total + arrived(index)
            sum_ref[pl.ds(unit * unit_rows, unit_rows), :] = total
    for done in sends:
        done.wait_send()


def scatter_scratch(rows, width):
    return [
        pltpu.VMEM((TRANSFERS * rows // UNITS, width), BF16),
        pltpu.VMEM((STAGED * rows // UNITS, width), BF16),
        pltpu.SemaphoreType.DMA((TRANSFERS,)),
        pltpu.SemaphoreType.DMA((TRANSFERS,)),
    ]


def scatter_rows(part, turned, rows_all, cot_rows, number):
    rows, width = part.shape[0] // GROUP, part.shape[1]
    columns, tokens = turned[0].shape
    padded = columns + -columns % 16
    return pl.pallas_call(
        scatter_kernel,
        out_shape=[
            jax.ShapeDtypeStruct((rows, width), F32),
            jax.ShapeDtypeStruct((len(turned) * padded, width), BF16),
        ],
        in_specs=whole_vmem(1 + len(turned)) + [ANYWHERE, ANYWHERE],
        out_specs=whole_vmem(2),
        scratch_shapes=scatter_scratch(rows, width)
        + [pltpu.VMEM((tokens, width), BF16), pltpu.SemaphoreType.DMA((2,))],
        compiler_params=pltpu.CompilerParams(
            collective_id=number, has_side_effects=True, vmem_limit_bytes=44 * 1024 * 1024
        ),
        name="scatter_rows",
    )(part, *turned, rows_all, cot_rows)


def scatter_rows_and_small(part, shard, grads, tokens, d_res, gain, seqs, number):
    rows, width = tokens.shape
    lines = (GROUP, width // GROUP)
    return pl.pallas_call(
        scatter_small_kernel,
        out_shape=[
            jax.ShapeDtypeStruct((rows, width), F32),
            jax.ShapeDtypeStruct(lines, F32),
            jax.ShapeDtypeStruct(shard.shape, F32),
            jax.ShapeDtypeStruct((GROUP, 8, LANES), F32),
            *(jax.ShapeDtypeStruct(grad.shape, BF16) for grad in grads),
        ],
        in_specs=whole_vmem(7),
        out_specs=whole_vmem(6),
        scratch_shapes=scatter_scratch(rows, width)
        + [pltpu.VMEM((rows, width), F32), pltpu.VMEM(lines, F32)]
        + seq_sum_scratch(grads[0].shape, 0)
        + seq_sum_scratch(grads[1].shape, 1)
        + everywhere_scratch(lines, seqs)
        + [
            pltpu.VMEM((seqs,) + shard.shape, F32),
            pltpu.SemaphoreType.DMA((seqs,)),
            pltpu.SemaphoreType.DMA((seqs,)),
            pltpu.SemaphoreType.DMA((GROUP,)),
            pltpu.SemaphoreType.DMA((GROUP,)),
        ],
        compiler_params=pltpu.CompilerParams(
            collective_id=number, has_side_effects=True, vmem_limit_bytes=48 * 1024 * 1024
        ),
        name="scatter_rows_and_small",
    )(part, shard, *grads, tokens, d_res, gain)


def to_tokens_kernel(
    inner_ref,
    gate_ref,
    gains_ref,
    inner_out,
    gate_out,
    gains_out,
    send_sem,
    recv_sem,
    local_sem,
):
    head = lax.axis_index("head")
    rows = inner_out.shape[0]
    first = gate_ref.shape[1] - LANES
    pairs = ((inner_ref, inner_out), (gate_ref.at[:, first:], gate_out))

    def rows_of(index):
        return pl.ds(pl.multiple_of(index * rows, rows), rows)

    def columns_of(index):
        return pl.ds(pl.multiple_of(index * LANES, LANES), LANES)

    mine = [
        pltpu.make_async_copy(
            source.at[rows_of(head)], target.at[:, columns_of(head)], local_sem.at[index]
        )
        for index, (source, target) in enumerate(pairs)
    ] + [pltpu.make_async_copy(gains_ref, gains_out.at[head], local_sem.at[2])]
    for done in mine:
        done.start()
    greet([{"head": lax.rem(head + ahead, GROUP)} for ahead in range(1, GROUP)])
    sends = []
    for ahead in range(1, GROUP):
        peer = lax.rem(head + ahead, GROUP)
        jobs = [
            (source.at[rows_of(peer)], target.at[:, columns_of(head)]) for source, target in pairs
        ] + [(gains_ref, gains_out.at[head])]
        for index, (source, target) in enumerate(jobs):
            done = pltpu.make_async_remote_copy(
                src_ref=source,
                dst_ref=target,
                send_sem=send_sem.at[ahead, index],
                recv_sem=recv_sem.at[ahead, index],
                device_id={"head": peer},
                device_id_type=MESH,
            )
            done.start()
            sends.append(done)
    for done in mine:
        done.wait()
    for done in sends:
        done.wait()


def to_tokens(inner, gate, gains, number):
    rows = inner.shape[0] // GROUP
    wide = jax.ShapeDtypeStruct((rows, GROUP * LANES), BF16)
    return pl.pallas_call(
        to_tokens_kernel,
        out_shape=[wide, wide, jax.ShapeDtypeStruct((GROUP,) + gains.shape, F32)],
        in_specs=whole_vmem(3),
        out_specs=whole_vmem(3),
        scratch_shapes=[
            pltpu.SemaphoreType.DMA((GROUP, 3)),
            pltpu.SemaphoreType.DMA((GROUP, 3)),
            pltpu.SemaphoreType.DMA((3,)),
        ],
        compiler_params=pltpu.CompilerParams(
            collective_id=number, has_side_effects=True, vmem_limit_bytes=8 * 1024 * 1024
        ),
        name="to_tokens",
    )(inner, gate, gains)


class ToHeads:
    def __init__(self, pairs, send_sem, recv_sem):
        self.pairs, self.send_sem, self.recv_sem = pairs, send_sem, recv_sem
        self.head = lax.axis_index("head")
        self.rows = pairs[0][0].shape[0]
        self.peers = [lax.rem(self.head + ahead, GROUP) for ahead in range(1, GROUP)]

    def rows_of(self, index):
        return pl.ds(pl.multiple_of(index * self.rows, self.rows), self.rows)

    def columns_of(self, index):
        return pl.ds(pl.multiple_of(index * LANES, LANES), LANES)

    def start(self):
        self.sends = []
        for ahead, peer in enumerate(self.peers, 1):
            for index, (source, target, first) in enumerate(self.pairs):
                done = pltpu.make_async_remote_copy(
                    src_ref=source.at[:, self.columns_of(peer)],
                    dst_ref=target.at[self.rows_of(self.head), first : first + LANES],
                    send_sem=self.send_sem.at[ahead, index],
                    recv_sem=self.recv_sem.at[ahead, index],
                    device_id={"head": peer},
                    device_id_type=MESH,
                )
                done.start()
                self.sends.append(done)
        for source, target, first in self.pairs:
            target[self.rows_of(self.head), first : first + LANES] = source[
                :, self.columns_of(self.head)
            ]

    def end(self):
        for done in self.sends:
            done.wait()


def to_heads_scratch(arrays):
    return [
        pltpu.SemaphoreType.DMA((GROUP, arrays)),
        pltpu.SemaphoreType.DMA((GROUP, arrays)),
    ]


def to_heads_kernel(inner_ref, sums_ref, inner_out, sums_out, send_sem, recv_sem, *sums_sems):
    exchange = ToHeads([(inner_ref, inner_out, 0)], send_sem, recv_sem)
    head = exchange.head
    greet([{"head": peer} for peer in exchange.peers])
    exchange.start()
    sends = []
    for ahead, peer in enumerate(exchange.peers, 1):
        done = pltpu.make_async_remote_copy(
            src_ref=sums_ref.at[peer],
            dst_ref=sums_out.at[head],
            send_sem=sums_sems[0].at[ahead],
            recv_sem=sums_sems[1].at[ahead],
            device_id={"head": peer},
            device_id_type=MESH,
        )
        done.start()
        sends.append(done)
    sums_out[head] = sums_ref[head]
    exchange.end()
    for done in sends:
        done.wait()


def to_heads(inner, sums, number):
    rows = inner.shape[0]
    return pl.pallas_call(
        to_heads_kernel,
        out_shape=[
            jax.ShapeDtypeStruct((rows * GROUP, LANES), BF16),
            jax.ShapeDtypeStruct(sums.shape, F32),
        ],
        in_specs=whole_vmem(2),
        out_specs=whole_vmem(2),
        scratch_shapes=to_heads_scratch(1)
        + [pltpu.SemaphoreType.DMA((GROUP,)), pltpu.SemaphoreType.DMA((GROUP,))],
        compiler_params=pltpu.CompilerParams(
            collective_id=number, has_side_effects=True, vmem_limit_bytes=8 * 1024 * 1024
        ),
        name="to_heads",
    )(inner, sums)


def after(value, *others):
    return lax.optimization_barrier((value,) + others)[0]


def per_device(
    tokens,
    doc_starts,
    norm_gain,
    w_in,
    w_rate,
    rate_bias,
    ttt_w,
    ttt_b,
    ttt_gain,
    ttt_shift,
    post_gain,
    post_bias,
    w_out,
    ffn_gain,
    w_gate_up,
    w_down,
    cotangent,
):
    seq = lax.axis_index("seq")
    seqs = lax.axis_size("seq")
    tok_rows, width = tokens.shape
    head_count, head_dim = ttt_b.shape
    local_width = head_count * head_dim
    ffn_local = w_down.shape[0]
    w_in_flat = w_in.reshape(width, 4 * local_width)
    w_gu_flat = w_gate_up.reshape(width, 2 * ffn_local)
    ffn_gain_line = ffn_gain[None]

    piece = width // seqs
    w_out_piece = lax.dynamic_slice_in_dim(w_out, seq * piece, piece, axis=1)
    w_out_all = lax.all_gather(w_out_piece, ("seq", "head"), axis=0, tiled=True)
    w_out_all = w_out_all.reshape(seqs, width, piece)

    resid = tokens.astype(F32)
    scale_one = lax.rsqrt(jnp.mean(resid * resid, axis=-1, keepdims=True) + EPS)
    norm_one = (resid * scale_one * norm_gain).astype(BF16)
    gathered = gather_rows(norm_one, 0)
    projected, rate_lanes = project(gathered, w_in_flat, w_rate, rate_bias)
    inner, *kept, _, _, cot_rows = inner_forward(
        doc_starts, projected, rate_lanes, ttt_w, ttt_b, ttt_gain, ttt_shift, cotangent, 7
    )

    gains = jnp.concatenate(
        [post_gain[None], post_bias[None], jnp.zeros((6, local_width), F32)], axis=0
    )
    inner_tok, gate_tok, all_gains = to_tokens(inner, projected, gains, 1)
    mixed_tok, hidden_res, norm_two = middle_forward(
        inner_tok, gate_tok, all_gains, tokens, ffn_gain_line, w_out_all
    )

    ffn_rows = gather_rows(norm_two, 2)
    gate_up = dot_nn(ffn_rows, w_gu_flat).astype(BF16)
    gate_part = gate_up[:, :ffn_local].astype(F32)
    up_part = gate_up[:, ffn_local:].astype(F32)
    silu_val, silu_pull = jax.vjp(jax.nn.silu, gate_part)
    hidden_state = (silu_val * up_part).astype(BF16)
    half = width // 2
    ffn_first = dot_nn(hidden_state, w_down[:, :half]).astype(BF16)
    out_first = lax.psum_scatter(ffn_first, "head", scatter_dimension=0, tiled=True)
    cot_rows = after(cot_rows, ffn_first)
    d_hidden = dot_nt(cot_rows, w_down)
    d_gate_part = silu_pull(d_hidden * up_part)[0].astype(BF16)
    d_up_part = (d_hidden * silu_val).astype(BF16)
    d_gate_up = jnp.concatenate([d_gate_part, d_up_part], axis=1)
    d_norm_part = dot_nt(d_gate_up, w_gu_flat).astype(BF16)
    d_norm_two, ffn_grads = scatter_rows(
        d_norm_part, (d_gate_part.T, d_up_part.T, hidden_state.T), ffn_rows, cot_rows, 3
    )

    d_res, d_mix, d_inner_tok, d_gate_tok, token_sums = middle_backward(
        d_norm_two,
        hidden_res,
        cotangent,
        ffn_gain_line,
        inner_tok,
        gate_tok,
        all_gains,
        w_out_all,
    )
    d_inner, head_sums = to_heads(d_inner_tok, token_sums, 4)
    head_sums = jnp.sum(head_sums, axis=0)

    (
        d_projected,
        d_bias,
        d_start_w,
        d_start_c,
        d_gain,
        d_shift,
        *_,
        mixed_in,
        ffn_sums,
        mix_rows,
    ) = inner_backward(
        doc_starts,
        projected,
        rate_lanes,
        after(d_inner, out_first),
        d_gate_tok,
        mixed_tok,
        ffn_grads,
        d_mix,
        kept,
        8,
    )
    ffn_sums = ffn_sums.reshape(3, -1, width)[:, :ffn_local].astype(F32)
    ffn_second = dot_nn(after(hidden_state, d_projected), w_down[:, half:]).astype(BF16)
    out_second = lax.psum_scatter(ffn_second, "head", scatter_dimension=0, tiled=True)
    ffn_out = jnp.concatenate([out_first, out_second], axis=1).astype(F32)
    output = (hidden_res + ffn_out).astype(BF16)
    grad_in = dot_tn(after(gathered, ffn_second), d_projected)
    w_columns = jnp.pad(w_rate, ((0, 0), (0, local_width - head_count)))
    w_columns = jnp.concatenate([w_in_flat, w_columns], axis=1)
    grad_w_rate = grad_in[:, 4 * local_width : 4 * local_width + head_count]
    grad_w_in = grad_in[:, : 4 * local_width].astype(BF16)
    grad_w_out = dot_tn(mixed_in, mix_rows).astype(BF16)
    singles = jnp.stack(
        [
            head_sums[2],
            head_sums[0],
            head_sums[1],
            d_start_c[:, ::head_dim].T.reshape(LANES),
            heads_of_lanes(d_gain).reshape(LANES),
            heads_of_lanes(d_shift).reshape(LANES),
            d_bias[0],
            jnp.zeros((LANES,), F32),
        ]
    )
    rate_rows = grad_w_rate.T.reshape(2 * width // LANES, LANES)
    shard = jnp.concatenate([singles, d_start_w, rate_rows], axis=0)
    d_norm_part = dot_nt(d_projected, w_columns).astype(BF16)
    grad_tokens, sum_norm_gain, shard, lines, sum_w_in, sum_w_out = scatter_rows_and_small(
        d_norm_part,
        shard,
        (grad_w_in, grad_w_out),
        tokens,
        d_res,
        norm_gain[None],
        seqs,
        5,
    )
    sum_ffn_gain = lines[:, 0].reshape(width)
    sum_ttt_w = shard[8 : 8 + head_dim].reshape(head_dim, head_count, head_dim)
    per_head = (head_count, head_dim)
    return (
        output,
        grad_tokens,
        sum_norm_gain.reshape(width),
        sum_w_in.astype(F32).reshape(width, 4, local_width),
        shard[8 + head_dim :].reshape(head_count, width).T,
        jnp.sum(shard[6].reshape(per_head), axis=1),
        sum_ttt_w.transpose(1, 2, 0),
        shard[3].reshape(per_head),
        shard[4].reshape(per_head),
        shard[5].reshape(per_head),
        shard[1],
        shard[2],
        sum_w_out.astype(F32),
        sum_ffn_gain,
        ffn_sums[:2].transpose(2, 0, 1),
        ffn_sums[2],
    )


def solution(mesh):
    return jax.shard_map(
        per_device,
        mesh=mesh,
        in_specs=(
            P(("seq", "head"), None),
            P("seq", None),
            P(),
            P(None, None, "head"),
            P(None, "head"),
            P("head"),
            P("head", None, None),
            P("head", None),
            P("head", None),
            P("head", None),
            P("head"),
            P("head"),
            P("head", None),
            P(),
            P(None, None, "head"),
            P("head", None),
            P(("seq", "head"), None),
        ),
        out_specs=(
            P(("seq", "head"), None),
            P(("seq", "head"), None),
            P(),
            P(None, None, "head"),
            P(None, "head"),
            P("head"),
            P("head", None, None),
            P("head", None),
            P("head", None),
            P("head", None),
            P("head"),
            P("head"),
            P("head", None),
            P(),
            P(None, None, "head"),
            P("head", None),
        ),
        check_vma=False,
    )
```
